256 devices in a mesh: dom: 64 (over z, x, core), col: 4 (over y).
Axes of the slice: x: 4, y: 4, z: 8, core: 2. Of those that a mesh axis runs over, the one named last changes fastest.
Arguments:
- start_block: float32 [256, 64, 16, 128], P('col', 'dom'), may hold values from -6 to 6
- node_mass: float32 [64, 16, 128], P('dom'), as said below
- material_ids: int32 [64, 16, 128], P('dom'), may hold values from 0 to 15
- moduli_table: float32 [16], replicated, may hold values from 1 to 30
- influence: bfloat16 [3072, 64, 16, 128], P('col', 'dom'), may hold values from -6 to 6
Outputs:
- modes: float32 [256, 64, 16, 128], P('col', 'dom')
- ritz_matrix: float32 [256, 256], replicated
- participation: float32 [256, 3072], P('dom', 'col')
The draws below stay inside these ranges and needn't reach their ends.
Inputs may be any that keep to these rules, and one draw needn't show every extreme that they name: `node_mass`: positive.
All inputs are finite; a program needn't handle non-finite values.
Results may differ from the reference program's by a relative error of at most 0.0029.
Values may be sent and summed in bfloat16 or wider, within the bound.
No kernel may reach another device: no remote copies, remote signals or barrier semaphores. Data moves between devices by JAX's collectives and lax.ppermute only.
A program may use at most 64 MiB of HBM per device.

```python
import math
import jax
import jax.numpy as jnp
from jax import lax

COLS = 256
NR = 3072
NMAT = 16
DEGREE = 4
NY = 16
NZ = 128
NX = 64


def draw_node_mass(key, part):
    key = jax.random.fold_in(key, 11)
    base_key = jax.random.fold_in(key, 1)
    spot_key = jax.random.fold_in(key, 2)
    light_key = jax.random.fold_in(key, 3)
    position = jnp.arange(NX, dtype=jnp.float32) / max(NX - 1, 1)
    profile = jnp.exp(-math.log(3.0) * position)
    base_mass = jnp.exp(jax.random.uniform(base_key, (NX, NY, NZ), jnp.float32, math.log(0.5), math.log(2.0)))
    flat_mass = (base_mass * profile[:, None, None]).reshape(-1)
    spot_index = jax.random.randint(spot_key, (), 0, NX * NY * NZ, dtype=jnp.int32)
    light_mass = jnp.exp(jax.random.uniform(light_key, (), jnp.float32, math.log(0.05), math.log(0.15)))
    cell_index = jnp.arange(NX * NY * NZ, dtype=jnp.int32)
    flat_mass = jnp.where(cell_index == spot_index, light_mass, flat_mass)
    return flat_mass.reshape(NX, NY, NZ)


def set_ends(values, rng, smallest, top_value):
    place = [jax.random.randint(jax.random.fold_in(rng, axis), (), 0, length) for axis, length in enumerate(values.shape)]
    longest = values.shape.index(max(values.shape))
    neighbour = place[:longest] + [(place[longest] + 1) % values.shape[longest]] + place[longest + 1:]
    return values.at[tuple(place)].set(smallest).at[tuple(neighbour)].set(top_value)


def shard_levels(key, dims, split, least, high):
    def one(dim, shards_of):
        heights = jax.random.uniform(jax.random.fold_in(jax.random.fold_in(key, 6), dim), (shards_of,), jnp.float32, least / len(split), high / len(split))
        return jnp.repeat(jnp.exp(heights), dims[dim] // shards_of).reshape((-1,) + (1,) * (len(dims) - dim - 1))

    level = one(*split[0])
    for cut in split[1:]:
        level = level * one(*cut)
    return level


def bell_draw(stream_key, extent, deviation, bound, split=(), kind=jnp.bfloat16):
    drawn = deviation * jax.random.normal(stream_key, extent, jnp.float32)
    if split:
        drawn = drawn * shard_levels(stream_key, extent, split, -0.22, 0.18)
    return jnp.clip(drawn, -bound, bound).astype(kind)


def setup_inputs(seed: int = 0) -> dict:
    key_list = jax.random.split(jax.random.key(seed), 6)
    return {
        "start_block": bell_draw(key_list[0], (COLS, NX, NY, NZ), 1.0, 6.0, ((0, 4), (1, 64)), jnp.float32),
        "node_mass": draw_node_mass(jax.random.fold_in(key_list[5], 71), 0),
        "material_ids": set_ends(jax.random.randint(key_list[2], (NX, NY, NZ), 0, NMAT), jax.random.fold_in(key_list[2], 1), 0, NMAT - 1).astype(jnp.int32),
        "moduli_table": jnp.clip(jnp.exp(jax.random.uniform(key_list[3], (NMAT,), jnp.float32, math.log(1.0), math.log(30.0))), 1.0, 30.0),
        "influence": bell_draw(key_list[4], (NR, NX, NY, NZ), 1.0, 6.0, ((0, 4), (1, 64))),
    }


LOW_RATIO = 0.02

def shift_ahead(field, axis):
    length_axis = field.shape[axis]
    kept_part = lax.slice_in_dim(field, 1, length_axis, axis=axis)
    zero_part = jnp.zeros_like(lax.slice_in_dim(field, 0, 1, axis=axis))
    return jnp.concatenate([kept_part, zero_part], axis=axis)

def shift_behind(field, axis):
    length_axis = field.shape[axis]
    kept_part = lax.slice_in_dim(field, 0, length_axis - 1, axis=axis)
    zero_part = jnp.zeros_like(lax.slice_in_dim(field, 0, 1, axis=axis))
    return jnp.concatenate([zero_part, kept_part], axis=axis)

def element_forces(extended, moduli_field):
    planes = moduli_field.shape[0]
    corners = []
    for corner in range(8):
        first = corner >> 2
        pieces = extended[:, first:first + planes]
        if corner >> 1 & 1:
            pieces = shift_ahead(pieces, 2)
        if corner & 1:
            pieces = shift_ahead(pieces, 3)
        corners.append(pieces)
    corner_sum = corners[0]
    for corner in range(1, 8):
        corner_sum = corner_sum + corners[corner]
    lower_sum = jnp.zeros_like(corners[0])
    upper_sum = jnp.zeros_like(corners[0])
    for corner in range(8):
        edge_sum = corners[corner ^ 1] + corners[corner ^ 2] + corners[corner ^ 4]
        forces = moduli_field * (5.0 / 12.0 * corners[corner] - corner_sum / 12.0 + edge_sum / 12.0)
        if corner & 1:
            forces = shift_behind(forces, 3)
        if corner >> 1 & 1:
            forces = shift_behind(forces, 2)
        if corner >> 2:
            upper_sum = upper_sum + forces
        else:
            lower_sum = lower_sum + forces
    blank_plane = jnp.zeros_like(lower_sum[:, :1])
    return jnp.concatenate([lower_sum, blank_plane], 1) + jnp.concatenate([blank_plane, upper_sum], 1)

def reference(start_block, node_mass, material_ids, moduli_table, influence):
    element_moduli = moduli_table[material_ids]
    upper_bound = 16.0 / 3.0 * jnp.max(moduli_table) / jnp.min(node_mass)
    lower_bound = LOW_RATIO * upper_bound
    half_width = (upper_bound - lower_bound) / 2.0
    centre = (upper_bound + lower_bound) / 2.0

    def stiffness(field):
        extended = jnp.concatenate([field, jnp.zeros_like(field[:, :1])], 1)
        return element_forces(extended, element_moduli)[:, :-1]

    def filter_block(block):
        previous = block
        current = (stiffness(block) / node_mass - centre * block) / half_width
        for degree_step in range(DEGREE - 1):
            following = 2.0 * (stiffness(current) / node_mass - centre * current) / half_width - previous
            previous, current = (current, following)
        return (current, stiffness(current))
    block_cols = 32
    grouped = start_block.reshape((COLS // block_cols, block_cols) + start_block.shape[1:])
    filtered, stiffened = lax.map(filter_block, grouped)
    block_flat = filtered.reshape(COLS, -1)
    stiff_flat = stiffened.reshape(COLS, -1)
    mass_flat = node_mass.reshape(1, -1)
    mass_times = block_flat * mass_flat
    contract = (((1,), (1,)), ((), ()))
    gram_k = lax.dot_general(block_flat.astype(jnp.float32), stiff_flat.astype(jnp.float32), contract, precision=lax.Precision.HIGHEST, preferred_element_type=jnp.float32)
    gram_m = lax.dot_general(block_flat.astype(jnp.float32), mass_times.astype(jnp.float32), contract, precision=lax.Precision.HIGHEST, preferred_element_type=jnp.float32)
    factor = jnp.linalg.cholesky(gram_m)
    inverse = lax.linalg.triangular_solve(factor, jnp.eye(COLS, dtype=jnp.float32), left_side=True, lower=True)
    ritz_matrix = jnp.dot(jnp.dot(inverse, gram_k, precision=lax.Precision.HIGHEST), inverse.T, precision=lax.Precision.HIGHEST)
    norm_scale = jnp.sqrt(jnp.float32(NX * NY * NZ))
    modes_flat = norm_scale * jnp.dot(inverse, block_flat, precision=lax.Precision.HIGHEST)
    weighted = (modes_flat * mass_flat).astype(jnp.bfloat16)
    targets = influence.reshape(NR, -1)
    participation = lax.dot_general(weighted.astype(jnp.float32), targets.astype(jnp.float32), contract, preferred_element_type=jnp.float32) / norm_scale
    return (modes_flat.reshape(start_block.shape), ritz_matrix, participation)
```

```python
import functools

import jax
import jax.numpy as jnp
import numpy as np
from jax import lax
from jax.experimental import pallas as pl
from jax.experimental.pallas import tpu as pltpu
from jax.sharding import PartitionSpec as P

DEGREE = 4
LOW_RATIO = 0.02
F32, BF16 = jnp.float32, jnp.bfloat16
VMEM = pl.BlockSpec(memory_space=pltpu.VMEM)
SMEM = pl.BlockSpec(memory_space=pltpu.SMEM)
WIDTH = 128
PARAMS = pltpu.CompilerParams(vmem_limit_bytes=48 * 1024 * 1024)
H4, HZ, HZ4, E, EZ, G, GZ, AM, MI, MS = range(10)


def shape(rows, lanes, dtype=F32):
    return jax.ShapeDtypeStruct((rows, lanes), dtype)


def lanes_of(y):
    return slice(y * WIDTH, (y + 1) * WIDTH)


def rows_of(group, size=16):
    return pl.ds(pl.multiple_of(group * size, size), size)


def twice(c):
    return jnp.concatenate([c, c], axis=0)


def stiffness_rows(width_y, u_at, v_at, w_at, coef):
    def with_roll(x):
        return x, pltpu.roll(x, WIDTH - 1, 1)

    u0, u1 = with_roll(u_at(0))
    v0, v1 = with_roll(v_at(0))
    w0, w1 = with_roll(w_at(0))
    kept = kept_z = None
    for y in range(width_y):
        c = functools.partial(coef, y)
        h4, hz, hz4 = c(H4), c(HZ), c(HZ4)
        ez, gz = c(EZ), c(GZ)
        p00 = ez * v0 + gz * w0
        p01 = ez * v1 + gz * w1
        if y + 1 < width_y:
            e, g = c(E), c(G)
            n0, n1 = with_roll(u_at(y + 1))
            x0, x1 = with_roll(v_at(y + 1))
            z0, z1 = with_roll(w_at(y + 1))
            p10 = ez * x0 + gz * z0
            p11 = ez * x1 + gz * z1
            q00 = e * v0 + g * w0
            q10 = e * x0 + g * z0
            side, other = p01 + p11, p00 + p10
            r00 = h4 * u0 - hz * n1 - q10 - side
            r10 = h4 * n0 - hz * u1 - q00 - side
            r01 = hz4 * u1 - hz * n0 - other - p11
            r11 = hz4 * n1 - hz * u0 - other - p01
        else:
            r00 = h4 * u0 - p01
            r01 = hz4 * u1 - p00
        here = r00 if kept is None else r00 + kept
        moved = r01 if kept_z is None else r01 + kept_z
        yield y, u0, here + pltpu.roll(moved, 1, 1)
        if y + 1 < width_y:
            kept, kept_z = r10, r11
            u0, u1, v0, v1, w0, w1 = n0, n1, x0, x1, z0, z1


def prepare(start_ref, ids_ref, mass_ref, field_ref, pay_ref, least_ref):
    width_y = ids_ref.shape[0]
    cols = field_ref.shape[0]
    for y in range(width_y):
        plane = start_ref[pl.ds(y, cols, stride=width_y), :]
        field_ref[:, lanes_of(y)] = plane
        pay_ref[:cols, lanes_of(y)] = plane.astype(BF16)
        code = (ids_ref[y : y + 1, :] + 1).astype(F32)
        pay_ref[cols:, lanes_of(y)] = jnp.broadcast_to(code, (16, WIDTH)).astype(BF16)
    least = jnp.min(jnp.min(mass_ref[...], axis=0, keepdims=True), axis=1, keepdims=True)
    least_ref[...] = jnp.broadcast_to(least, least_ref.shape)


def first_step(field_ref, next_ref, back_ref, ids_ref, mass_ref, least_ref, table_ref, out_ref, pay_ref, coef_ref, shift_ref):
    cols, width_y = field_ref.shape[0], ids_ref.shape[0]
    materials = table_ref.shape[0]
    top = table_ref[0]
    for k in range(1, materials):
        top = jnp.maximum(top, table_ref[k])
    least = jnp.min(jnp.min(least_ref[...], axis=0, keepdims=True), axis=1, keepdims=True)
    upper = jnp.broadcast_to(16.0 / 3.0 * top / least, (8, WIDTH))
    lower = LOW_RATIO * upper
    half = (upper - lower) / 2.0
    shift = (upper + lower) / 2.0 / half
    shift_ref[...] = shift
    inner = lax.broadcasted_iota(jnp.int32, (8, WIDTH), 1) < WIDTH - 1

    def moduli(code):
        e = jnp.zeros(code.shape, F32)
        for k in range(materials):
            e = jnp.where(code == k + 1, table_ref[k], e)
        return e / 12.0

    for y in range(width_y):
        at = lanes_of(y)
        own = moduli(jnp.broadcast_to(ids_ref[y : y + 1, :] + 1, (8, WIDTH)))
        back = moduli(back_ref[cols:, at].astype(F32)[:8].astype(jnp.int32))
        mass = jnp.broadcast_to(mass_ref[y : y + 1, :], (8, WIDTH))
        both = own + back
        both_z = jnp.where(inner, both, 0.0)
        values = {
            H4: 4.0 * both,
            HZ: both_z,
            HZ4: 4.0 * both_z,
            E: own,
            EZ: jnp.where(inner, own, 0.0),
            G: back,
            GZ: jnp.where(inner, back, 0.0),
            AM: 1.0 / (mass * half),
            MI: 1.0 / mass,
            MS: mass,
        }
        for place, value in values.items():
            coef_ref[8 * place : 8 * place + 8, at] = value

    def coef(y, place):
        return twice(coef_ref[8 * place : 8 * place + 8, lanes_of(y)])

    def group(i, carry):
        at = rows_of(i)
        rows = stiffness_rows(
            width_y,
            lambda y: field_ref[at, lanes_of(y)],
            lambda y: next_ref[at, lanes_of(y)].astype(F32),
            lambda y: back_ref[at, lanes_of(y)].astype(F32),
            coef,
        )
        shift2 = twice(shift)
        for y, u, forces in rows:
            result = forces * coef(y, AM) - shift2 * u
            out_ref[at, lanes_of(y)] = result
            pay_ref[at, lanes_of(y)] = result.astype(BF16)
        return carry

    lax.fori_loop(0, cols // 16, group, 0)


def later_step(last, field_ref, before_ref, next_ref, back_ref, coef_ref, shift_ref, out_ref, pay_ref, *heavy_ref):
    cols = field_ref.shape[0]
    width_y = field_ref.shape[1] // WIDTH

    def coef(y, place):
        return twice(coef_ref[8 * place : 8 * place + 8, lanes_of(y)])

    def group(i, carry):
        at = rows_of(i)
        rows = stiffness_rows(
            width_y,
            lambda y: field_ref[at, lanes_of(y)],
            lambda y: next_ref[at, lanes_of(y)].astype(F32),
            lambda y: back_ref[at, lanes_of(y)].astype(F32),
            coef,
        )
        shift2 = twice(shift_ref[...])
        for y, u, forces in rows:
            result = 2.0 * (forces * coef(y, AM) - shift2 * u) - before_ref[at, lanes_of(y)]
            out_ref[at, lanes_of(y)] = result
            pay_ref[at, lanes_of(y)] = result.astype(BF16)
            if last:
                heavy_ref[0][at, lanes_of(y)] = (result * coef(y, MS)).astype(BF16)
        return carry

    lax.fori_loop(0, cols // 16, group, 0)


def dot_nt(a, b):
    return lax.dot_general(a, b, (((1,), (1,)), ((), ())), preferred_element_type=F32)


def products(field_ref, next_ref, back_ref, coef_ref, own_ref, one_ref, two_ref, three_ref, target_ref, place_ref, keep_ref, send_ref, all_ref, high_ref, low_ref):
    cols = field_ref.shape[0]
    width_y = field_ref.shape[1] // WIDTH
    core, col = place_ref[0], place_ref[1]
    for step, ref in enumerate((own_ref, one_ref, two_ref, three_ref)):
        all_ref[rows_of(lax.rem(col + 4 - step, 4), cols), :] = ref[...]

    def coef(y, place):
        return twice(coef_ref[8 * place : 8 * place + 8, lanes_of(y)])

    def group(i, carry):
        at = rows_of(i)
        rows = stiffness_rows(
            width_y,
            lambda y: field_ref[at, lanes_of(y)],
            lambda y: next_ref[at, lanes_of(y)].astype(F32),
            lambda y: back_ref[at, lanes_of(y)].astype(F32),
            coef,
        )
        for y, u, forces in rows:
            scaled = forces * coef(y, MI)
            high = scaled.astype(BF16)
            high_ref[0, at, lanes_of(y)] = high
            low_ref[0, at, lanes_of(y)] = (scaled - high.astype(F32)).astype(BF16)
            high = u.astype(BF16)
            high_ref[1, at, lanes_of(y)] = high
            low_ref[1, at, lanes_of(y)] = (u - high.astype(F32)).astype(BF16)
        return carry

    lax.fori_loop(0, cols // 16, group, 0)
    everything = all_ref[...]
    half = target_ref.shape[0] // 2
    for side, ref in ((core, keep_ref), (1 - core, send_ref)):
        targets = dot_nt(target_ref[rows_of(side, half), :], everything)
        gram = dot_nt(high_ref[side], everything) + dot_nt(low_ref[side], everything)
        chunks = ref.shape[0]
        t, g = half // chunks, cols // chunks
        for z in range(chunks):
            ref[z, :t, :] = targets[z * t : (z + 1) * t]
            ref[z, t:, :] = gram[z * g : (z + 1) * g]


def finish(field_ref, all_ref, own_ref, coef_ref, rows_ref, block_ref, few_ref, targets_ref, modes_ref, part_ref):
    cols = field_ref.shape[0]
    width_y = field_ref.shape[1] // WIDTH
    norm = jnp.float32(np.sqrt(np.float32(64 * width_y * WIDTH)))
    weights = rows_ref[...]
    high = weights.astype(BF16)
    low = (weights - high.astype(F32)).astype(BF16)
    block = block_ref[...].astype(BF16)
    for y in range(width_y):
        at = lanes_of(y)
        everything = all_ref[:, at]
        mass = coef_ref[8 * MS : 8 * MS + 8, at]
        mass = jnp.concatenate([mass] * (cols // 8), axis=0)
        inverse = coef_ref[8 * MI : 8 * MI + 8, at]
        inverse = jnp.concatenate([inverse] * (cols // 8), axis=0)
        rest = (field_ref[:, at] * mass - own_ref[:, at].astype(F32)).astype(BF16)
        total = (
            jnp.dot(high, everything, preferred_element_type=F32)
            + jnp.dot(low, everything, preferred_element_type=F32)
            + jnp.dot(block, rest, preferred_element_type=F32)
        )
        modes_ref[pl.ds(y, cols, stride=width_y), :] = total * inverse * norm
    part_ref[...] = lax.dot_general(
        few_ref[...], targets_ref[...], (((1,), (1,)), ((), ())), precision=lax.Precision.HIGHEST, preferred_element_type=F32
    )


def local(start_block, node_mass, material_ids, moduli_table, influence):
    cols, _, width_y, width_z = start_block.shape
    lanes = width_y * width_z
    doms, groups = lax.axis_size("dom"), lax.axis_size("col")
    total_cols = cols * groups
    me, col = lax.axis_index("dom"), lax.axis_index("col")
    core = me % 2
    along_z, along_x = 8, 4
    up = [(i, i + 1) for i in range(doms - 1)]
    down = [(i + 1, i) for i in range(doms - 1)]
    pair = [(i, i ^ 1) for i in range(doms)]
    z_groups = [[z * 2 * along_x + r for z in range(along_z)] for r in range(2 * along_x)]

    def x_ring(step):
        return [(i, i - i % 8 + (i + 2 * step) % 8) for i in range(doms)]

    def col_ring(step):
        return [(i, (i + step) % groups) for i in range(groups)]

    ids = material_ids.reshape(width_y, width_z)
    mass = node_mass.reshape(width_y, width_z)
    targets = influence.reshape(influence.shape[0], lanes)

    field, pay, least = pl.pallas_call(
        prepare,
        out_shape=(shape(cols, lanes), shape(cols + 16, lanes, BF16), shape(doms, WIDTH)),
        in_specs=[VMEM] * 3,
        out_specs=(VMEM,) * 3,
        compiler_params=PARAMS,
    )(start_block.reshape(cols * width_y, width_z), ids, mass)
    ahead = lax.ppermute(pay, "dom", down)
    behind = lax.ppermute(pay, "dom", up)
    least = lax.all_to_all(least, "dom", 0, 0, tiled=True)

    current, pay, coef, shift = pl.pallas_call(
        first_step,
        out_shape=(shape(cols, lanes), shape(cols, lanes, BF16), shape(80, lanes), shape(8, WIDTH)),
        in_specs=[VMEM] * 6 + [SMEM],
        out_specs=(VMEM,) * 4,
        compiler_params=PARAMS,
    )(field, ahead, behind, ids, mass, least, moduli_table)
    previous = field
    for step in range(DEGREE - 1):
        last = step == DEGREE - 2
        ahead = lax.ppermute(pay, "dom", down)
        behind = lax.ppermute(pay, "dom", up)
        outs = pl.pallas_call(
            functools.partial(later_step, last),
            out_shape=(shape(cols, lanes),) + (shape(cols, lanes, BF16),) * (2 if last else 1),
            in_specs=[VMEM] * 6,
            out_specs=(VMEM,) * (3 if last else 2),
            compiler_params=PARAMS,
        )(current, previous, ahead, behind, coef, shift)
        previous, current, pay = current, outs[0], outs[1]
    heavy = outs[2]
    others = [lax.ppermute(heavy, "col", col_ring(step)) for step in (1, 2, 3)]
    ahead = lax.ppermute(pay, "dom", down)
    behind = lax.ppermute(pay, "dom", up)
    place = jnp.stack([core, col]).astype(jnp.int32)
    half = targets.shape[0] // 2
    t_rows, g_rows = half // along_z, cols // along_z
    chunk = jax.ShapeDtypeStruct((along_z, t_rows + g_rows, total_cols), F32)
    keep, send, everything = pl.pallas_call(
        products,
        out_shape=(chunk, chunk, shape(total_cols, lanes, BF16)),
        in_specs=[VMEM] * 9 + [SMEM],
        out_specs=(VMEM,) * 3,
        scratch_shapes=[pltpu.VMEM((2, cols, lanes), BF16)] * 2,
        compiler_params=PARAMS,
    )(current, ahead, behind, coef, heavy, *others, targets, place)

    summed = keep + lax.ppermute(send, "dom", pair)
    summed = lax.all_to_all(summed, "dom", 0, 0, tiled=True, axis_index_groups=z_groups)
    summed = jnp.sum(summed, axis=0)
    one, two, three = [lax.ppermute(summed, "dom", x_ring(step)) for step in (1, 2, 3)]
    summed = (summed + two) + (one + three)
    gram = summed[t_rows:]
    found = [gram] + [lax.ppermute(gram, "col", col_ring(step)) for step in (1, 2, 3)]
    stack = jnp.stack(found)
    stack = jnp.take(stack, (col - jnp.arange(groups)) % groups, axis=0)
    block = jnp.concatenate([summed[:t_rows], stack.reshape(groups * g_rows, total_cols)], 0)
    block = jnp.broadcast_to(block[None], (along_z,) + block.shape)
    mine = lax.all_to_all(block, "dom", 0, 0, tiled=True, axis_index_groups=z_groups)
    theirs = lax.ppermute(mine, "dom", pair)
    first = core == 0
    low, high = jnp.where(first, mine, theirs), jnp.where(first, theirs, mine)
    all_targets = jnp.concatenate([low[:, :t_rows], high[:, :t_rows]], 0).reshape(2 * half, total_cols)

    def gram_of(part):
        part = part[:, t_rows:].reshape(along_z, groups, g_rows, total_cols)
        return jnp.transpose(part, (1, 0, 2, 3)).reshape(total_cols, total_cols)

    gram_k, gram_m = gram_of(low), gram_of(high)
    factor = jnp.linalg.cholesky(gram_m)
    inverse = lax.linalg.triangular_solve(
        factor, jnp.eye(total_cols, dtype=F32), left_side=True, lower=True
    )
    ritz_matrix = jnp.dot(
        jnp.dot(inverse, gram_k, precision=lax.Precision.HIGHEST), inverse.T, precision=lax.Precision.HIGHEST
    )
    own_rows = lax.dynamic_slice_in_dim(inverse, col * cols, cols, 0)
    own_block = lax.dynamic_slice_in_dim(own_rows, col * cols, cols, 1)
    part_rows = total_cols // doms
    few = lax.dynamic_slice_in_dim(inverse, me * part_rows, part_rows, 0)
    modes, participation = pl.pallas_call(
        finish,
        out_shape=(shape(cols * width_y, width_z), shape(part_rows, 2 * half)),
        in_specs=[VMEM] * 8,
        out_specs=(VMEM,) * 2,
        compiler_params=PARAMS,
    )(current, everything, heavy, coef, own_rows, own_block, few, all_targets)
    return (modes.reshape(start_block.shape), ritz_matrix, participation)


def solution(mesh):
    placed = (
        P("col", "dom", None, None),
        P("dom", None, None),
        P("dom", None, None),
        P(),
        P("col", "dom", None, None),
    )
    return jax.shard_map(
        local,
        mesh=mesh,
        in_specs=placed,
        out_specs=(P("col", "dom", None, None), P(), P("dom", "col")),
        check_vma=False,
    )
```

```python
import functools

import jax
import jax.numpy as jnp
import numpy as np
from jax import lax
from jax.experimental import pallas as pl
from jax.experimental.pallas import tpu as pltpu
from jax.sharding import PartitionSpec as P

DEGREE = 4
LOW_RATIO = 0.02
F32, BF16 = jnp.float32, jnp.bfloat16
VMEM = pl.BlockSpec(memory_space=pltpu.VMEM)
SMEM = pl.BlockSpec(memory_space=pltpu.SMEM)
WIDTH = 128
PARAMS = pltpu.CompilerParams(vmem_limit_bytes=48 * 1024 * 1024)
H4, HZ, HZ4, E, EZ, G, GZ, AM, MI, MS = range(10)


def shape(rows, lanes, dtype=F32):
    return jax.ShapeDtypeStruct((rows, lanes), dtype)


def lanes_of(y):
    return slice(y * WIDTH, (y + 1) * WIDTH)


def rows_of(group, size=16):
    return pl.ds(pl.multiple_of(group * size, size), size)


def twice(c):
    return jnp.concatenate([c, c], axis=0)


def stiffness_rows(width_y, u_at, v_at, w_at, coef):
    def with_roll(x):
        return x, pltpu.roll(x, WIDTH - 1, 1)

    u0, u1 = with_roll(u_at(0))
    v0, v1 = with_roll(v_at(0))
    w0, w1 = with_roll(w_at(0))
    kept = kept_z = None
    for y in range(width_y):
        c = functools.partial(coef, y)
        h4, hz, hz4 = c(H4), c(HZ), c(HZ4)
        ez, gz = c(EZ), c(GZ)
        p00 = ez * v0 + gz * w0
        p01 = ez * v1 + gz * w1
        if y + 1 < width_y:
            e, g = c(E), c(G)
            n0, n1 = with_roll(u_at(y + 1))
            x0, x1 = with_roll(v_at(y + 1))
            z0, z1 = with_roll(w_at(y + 1))
            p10 = ez * x0 + gz * z0
            p11 = ez * x1 + gz * z1
            q00 = e * v0 + g * w0
            q10 = e * x0 + g * z0
            side, other = p01 + p11, p00 + p10
            r00 = h4 * u0 - hz * n1 - q10 - side
            r10 = h4 * n0 - hz * u1 - q00 - side
            r01 = hz4 * u1 - hz * n0 - other - p11
            r11 = hz4 * n1 - hz * u0 - other - p01
        else:
            r00 = h4 * u0 - p01
            r01 = hz4 * u1 - p00
        here = r00 if kept is None else r00 + kept
        moved = r01 if kept_z is None else r01 + kept_z
        yield y, u0, here + pltpu.roll(moved, 1, 1)
        if y + 1 < width_y:
            kept, kept_z = r10, r11
            u0, u1, v0, v1, w0, w1 = n0, n1, x0, x1, z0, z1


def prepare(start_ref, ids_ref, mass_ref, field_ref, pay_ref, least_ref):
    width_y = ids_ref.shape[0]
    cols = field_ref.shape[0]
    for y in range(width_y):
        plane = start_ref[pl.ds(y, cols, stride=width_y), :]
        field_ref[:, lanes_of(y)] = plane
        pay_ref[:cols, lanes_of(y)] = plane.astype(BF16)
        code = (ids_ref[y : y + 1, :] + 1).astype(F32)
        pay_ref[cols:, lanes_of(y)] = jnp.broadcast_to(code, (16, WIDTH)).astype(BF16)
    least = jnp.min(jnp.min(mass_ref[...], axis=0, keepdims=True), axis=1, keepdims=True)
    least_ref[...] = jnp.broadcast_to(least, least_ref.shape)


def first_step(field_ref, next_ref, back_ref, ids_ref, mass_ref, least_ref, table_ref, out_ref, pay_ref, coef_ref, shift_ref):
    cols, width_y = field_ref.shape[0], ids_ref.shape[0]
    materials = table_ref.shape[0]
    top = table_ref[0]
    for k in range(1, materials):
        top = jnp.maximum(top, table_ref[k])
    least = jnp.min(jnp.min(least_ref[...], axis=0, keepdims=True), axis=1, keepdims=True)
    upper = jnp.broadcast_to(16.0 / 3.0 * top / least, (8, WIDTH))
    lower = LOW_RATIO * upper
    half = (upper - lower) / 2.0
    shift = (upper + lower) / 2.0 / half
    shift_ref[...] = shift
    inner = lax.broadcasted_iota(jnp.int32, (8, WIDTH), 1) < WIDTH - 1

    def moduli(code):
        e = jnp.zeros(code.shape, F32)
        for k in range(materials):
            e = jnp.where(code == k + 1, table_ref[k], e)
        return e / 12.0

    for y in range(width_y):
        at = lanes_of(y)
        own = moduli(jnp.broadcast_to(ids_ref[y : y + 1, :] + 1, (8, WIDTH)))
        back = moduli(back_ref[cols:, at].astype(F32)[:8].astype(jnp.int32))
        mass = jnp.broadcast_to(mass_ref[y : y + 1, :], (8, WIDTH))
        both = own + back
        both_z = jnp.where(inner, both, 0.0)
        values = {
            H4: 4.0 * both,
            HZ: both_z,
            HZ4: 4.0 * both_z,
            E: own,
            EZ: jnp.where(inner, own, 0.0),
            G: back,
            GZ: jnp.where(inner, back, 0.0),
            AM: 1.0 / (mass * half),
            MI: 1.0 / mass,
            MS: mass,
        }
        for place, value in values.items():
            coef_ref[8 * place : 8 * place + 8, at] = value

    def coef(y, place):
        return twice(coef_ref[8 * place : 8 * place + 8, lanes_of(y)])

    def group(i, carry):
        at = rows_of(i)
        rows = stiffness_rows(
            width_y,
            lambda y: field_ref[at, lanes_of(y)],
            lambda y: next_ref[at, lanes_of(y)].astype(F32),
            lambda y: back_ref[at, lanes_of(y)].astype(F32),
            coef,
        )
        shift2 = twice(shift)
        for y, u, forces in rows:
            result = forces * coef(y, AM) - shift2 * u
            out_ref[at, lanes_of(y)] = result
            pay_ref[at, lanes_of(y)] = result.astype(BF16)
        return carry

    lax.fori_loop(0, cols // 16, group, 0)


def later_step(last, field_ref, before_ref, next_ref, back_ref, coef_ref, shift_ref, out_ref, pay_ref, *heavy_ref):
    cols = field_ref.shape[0]
    width_y = field_ref.shape[1] // WIDTH

    def coef(y, place):
        return twice(coef_ref[8 * place : 8 * place + 8, lanes_of(y)])

    def group(i, carry):
        at = rows_of(i)
        rows = stiffness_rows(
            width_y,
            lambda y: field_ref[at, lanes_of(y)],
            lambda y: next_ref[at, lanes_of(y)].astype(F32),
            lambda y: back_ref[at, lanes_of(y)].astype(F32),
            coef,
        )
        shift2 = twice(shift_ref[...])
        for y, u, forces in rows:
            result = 2.0 * (forces * coef(y, AM) - shift2 * u) - before_ref[at, lanes_of(y)]
            out_ref[at, lanes_of(y)] = result
            pay_ref[at, lanes_of(y)] = result.astype(BF16)
            if last:
                heavy_ref[0][at, lanes_of(y)] = (result * coef(y, MS)).astype(BF16)
        return carry

    lax.fori_loop(0, cols // 16, group, 0)


def dot_nt(a, b):
    return lax.dot_general(a, b, (((1,), (1,)), ((), ())), preferred_element_type=F32)


def products(field_ref, next_ref, back_ref, coef_ref, own_ref, one_ref, two_ref, three_ref, target_ref, place_ref, keep_ref, send_ref, all_ref, high_ref, low_ref):
    cols = field_ref.shape[0]
    width_y = field_ref.shape[1] // WIDTH
    core, col = place_ref[0], place_ref[1]
    for step, ref in enumerate((own_ref, one_ref, two_ref, three_ref)):
        all_ref[rows_of(lax.rem(col + 4 - step, 4), cols), :] = ref[...]

    def coef(y, place):
        return twice(coef_ref[8 * place : 8 * place + 8, lanes_of(y)])

    def group(i, carry):
        at = rows_of(i)
        rows = stiffness_rows(
            width_y,
            lambda y: field_ref[at, lanes_of(y)],
            lambda y: next_ref[at, lanes_of(y)].astype(F32),
            lambda y: back_ref[at, lanes_of(y)].astype(F32),
            coef,
        )
        for y, u, forces in rows:
            scaled = forces * coef(y, MI)
            high = scaled.astype(BF16)
            high_ref[0, at, lanes_of(y)] = high
            low_ref[0, at, lanes_of(y)] = (scaled - high.astype(F32)).astype(BF16)
            high = u.astype(BF16)
            high_ref[1, at, lanes_of(y)] = high
            low_ref[1, at, lanes_of(y)] = (u - high.astype(F32)).astype(BF16)
        return carry

    lax.fori_loop(0, cols // 16, group, 0)
    everything = all_ref[...]
    half = target_ref.shape[0] // 2
    for side, ref in ((core, keep_ref), (1 - core, send_ref)):
        targets = dot_nt(target_ref[rows_of(side, half), :], everything)
        gram = dot_nt(high_ref[side], everything) + dot_nt(low_ref[side], everything)
        chunks = ref.shape[0]
        t, g = half // chunks, cols // chunks
        for z in range(chunks):
            ref[z, :t, :] = targets[z * t : (z + 1) * t]
            ref[z, t:, :] = gram[z * g : (z + 1) * g]


def split(x):
    high = x.astype(BF16)
    return high, (x - high.astype(F32)).astype(BF16)


def dot_split(a, b, dims):
    (ah, al), (bh, bl) = split(a), split(b)
    dot = functools.partial(lax.dot_general, dimension_numbers=(dims, ((), ())), preferred_element_type=F32)
    return dot(ah, bh) + (dot(ah, bl) + dot(al, bh))


def inverse_factor(work_ref, panel, few):
    n = work_ref.shape[0]
    tiles = n // WIDTH
    lane = lax.broadcasted_iota(jnp.int32, (panel, WIDTH), 1)
    row = lax.broadcasted_iota(jnp.int32, (panel, WIDTH), 0)
    for start in range(0, n, panel):
        at = slice(start, start + panel)
        lines = [work_ref[at, lanes_of(t)] for t in range(tiles)]
        pivots = jnp.zeros((panel, WIDTH), F32)
        for first in range(0, panel, few):
            columns, factors = [], []
            for place in range(start + first, start + first + few):
                tile, inside = divmod(place, WIDTH)
                columns.append(jnp.broadcast_to(lines[tile][:, inside : inside + 1], (panel, WIDTH)))
            for k in range(few):
                p = first + k
                pivot = columns[k][p : p + 1, :]
                factor = jnp.where(row > p, columns[k] * (1.0 / pivot), 0.0)
                pivots = jnp.where(row == p, pivot, pivots)
                for l in range(k + 1, few):
                    columns[l] = columns[l] - factor * columns[l][p : p + 1, :]
                factors.append(factor)
            for k in range(few):
                p = first + k
                tile, inside = divmod(start + p, WIDTH)
                for t in range(tiles):
                    line = lines[t][p : p + 1, :]
                    if t == tile:
                        line = line + jnp.where(lane[:1] == inside, 1.0, 0.0)
                    lines[t] = lines[t] - factors[k] * line
        scale = 1.0 / jnp.sqrt(pivots)
        factor_rows, update_rows = [], []
        for t in range(tiles):
            place = lane + t * WIDTH
            full = jnp.where(place == row + start, scale, lines[t] * scale)
            inverse = jnp.where(place <= row + start, full, 0.0)
            work_ref[at, lanes_of(t)] = inverse
            factor_rows.append(full)
            update_rows.append(jnp.where((place >= start) & (place < start + panel), inverse, full))
        rest = n - start - panel
        if rest:
            update = dot_split(jnp.concatenate(factor_rows, 1), jnp.concatenate(update_rows, 1), ((0,), (0,)))
            for t in range(tiles):
                old = work_ref[start + panel :, lanes_of(t)]
                place = lax.broadcasted_iota(jnp.int32, old.shape, 1) + t * WIDTH
                old = jnp.where((place >= start) & (place < start + panel), 0.0, old)
                work_ref[start + panel :, lanes_of(t)] = old - update[start + panel :, lanes_of(t)]


def finish(field_ref, all_ref, own_ref, coef_ref, mine_ref, theirs_ref, place_ref, modes_ref, ritz_ref, part_ref, mass_ref, stiff_ref, targets_ref, work_ref):
    core, col, me = place_ref[0], place_ref[1], place_ref[2]
    cols = field_ref.shape[0]
    width_y = field_ref.shape[1] // WIDTH
    total = work_ref.shape[0]
    groups = total // cols
    chunks = mine_ref.shape[0]
    g = cols // chunks
    t = mine_ref.shape[1] - groups * g
    half = targets_ref.shape[0] // 2
    low_first = core == 0
    for z in range(chunks):
        for side in (0, 1):
            chosen = (low_first == (side == 0))
            part = jnp.where(chosen, mine_ref[z], theirs_ref[z])
            targets_ref[side * half + z * t : side * half + (z + 1) * t, :] = part[:t]
            into = mass_ref if side else stiff_ref
            for step in range(groups):
                place = lax.rem(col + groups - step, groups) * cols + z * g
                into[pl.ds(pl.multiple_of(place, g), g), :] = part[t + step * g : t + (step + 1) * g]
    gram = mass_ref[...]
    on = lax.broadcasted_iota(jnp.int32, gram.shape, 0) == lax.broadcasted_iota(jnp.int32, gram.shape, 1)
    diagonal = jnp.where(on, gram, 0.0)
    across = 1.0 / jnp.sqrt(jnp.sum(diagonal, axis=0, keepdims=True))
    down = 1.0 / jnp.sqrt(jnp.sum(diagonal, axis=1, keepdims=True))
    work_ref[...] = gram * across * down
    inverse_factor(work_ref, 64, 16)
    inverse = work_ref[...] * across
    work_ref[...] = inverse
    ritz_ref[...] = dot_split(dot_split(inverse, stiff_ref[...], ((1,), (1,))), inverse, ((1,), (1,)))

    rows = work_ref[pl.ds(pl.multiple_of(me // 2 * 8, 8), 8), :]
    part = dot_split(rows, targets_ref[...], ((1,), (1,)))
    part_ref[...] = jnp.where(low_first, part[:4], part[4:])

    norm = jnp.float32(np.sqrt(np.float32(64 * width_y * WIDTH)))
    weights = work_ref[rows_of(col, cols), :]
    block = jnp.zeros((cols, cols), F32)
    for k in range(groups):
        block = jnp.where(col == k, weights[:, k * cols : (k + 1) * cols], block)
    block = block.astype(BF16)
    high, low = split(weights)
    for y in range(width_y):
        at = lanes_of(y)
        everything = all_ref[:, at]
        mass = jnp.concatenate([coef_ref[8 * MS : 8 * MS + 8, at]] * (cols // 8), axis=0)
        light = jnp.concatenate([coef_ref[8 * MI : 8 * MI + 8, at]] * (cols // 8), axis=0)
        rest = (field_ref[:, at] * mass - own_ref[:, at].astype(F32)).astype(BF16)
        result = (
            jnp.dot(high, everything, preferred_element_type=F32)
            + jnp.dot(low, everything, preferred_element_type=F32)
            + jnp.dot(block, rest, preferred_element_type=F32)
        )
        modes_ref[pl.ds(y, cols, stride=width_y), :] = result * light * norm


def local(start_block, node_mass, material_ids, moduli_table, influence):
    cols, _, width_y, width_z = start_block.shape
    lanes = width_y * width_z
    doms, groups = lax.axis_size("dom"), lax.axis_size("col")
    total_cols = cols * groups
    me, col = lax.axis_index("dom"), lax.axis_index("col")
    core = me % 2
    along_z, along_x = 8, 4
    up = [(i, i + 1) for i in range(doms - 1)]
    down = [(i + 1, i) for i in range(doms - 1)]
    pair = [(i, i ^ 1) for i in range(doms)]
    z_groups = [[z * 2 * along_x + r for z in range(along_z)] for r in range(2 * along_x)]

    def x_ring(step):
        return [(i, i - i % 8 + (i + 2 * step) % 8) for i in range(doms)]

    def col_ring(step):
        return [(i, (i + step) % groups) for i in range(groups)]

    ids = material_ids.reshape(width_y, width_z)
    mass = node_mass.reshape(width_y, width_z)
    targets = influence.reshape(influence.shape[0], lanes)

    field, pay, least = pl.pallas_call(
        prepare,
        out_shape=(shape(cols, lanes), shape(cols + 16, lanes, BF16), shape(doms, WIDTH)),
        in_specs=[VMEM] * 3,
        out_specs=(VMEM,) * 3,
        compiler_params=PARAMS,
    )(start_block.reshape(cols * width_y, width_z), ids, mass)
    ahead = lax.ppermute(pay, "dom", down)
    behind = lax.ppermute(pay, "dom", up)
    least = lax.all_to_all(least, "dom", 0, 0, tiled=True)

    current, pay, coef, shift = pl.pallas_call(
        first_step,
        out_shape=(shape(cols, lanes), shape(cols, lanes, BF16), shape(80, lanes), shape(8, WIDTH)),
        in_specs=[VMEM] * 6 + [SMEM],
        out_specs=(VMEM,) * 4,
        compiler_params=PARAMS,
    )(field, ahead, behind, ids, mass, least, moduli_table)
    previous = field
    for step in range(DEGREE - 1):
        last = step == DEGREE - 2
        ahead = lax.ppermute(pay, "dom", down)
        behind = lax.ppermute(pay, "dom", up)
        outs = pl.pallas_call(
            functools.partial(later_step, last),
            out_shape=(shape(cols, lanes),) + (shape(cols, lanes, BF16),) * (2 if last else 1),
            in_specs=[VMEM] * 6,
            out_specs=(VMEM,) * (3 if last else 2),
            compiler_params=PARAMS,
        )(current, previous, ahead, behind, coef, shift)
        previous, current, pay = current, outs[0], outs[1]
    heavy = outs[2]
    others = [lax.ppermute(heavy, "col", col_ring(step)) for step in (1, 2, 3)]
    ahead = lax.ppermute(pay, "dom", down)
    behind = lax.ppermute(pay, "dom", up)
    place = jnp.stack([core, col, me]).astype(jnp.int32)
    half = targets.shape[0] // 2
    t_rows, g_rows = half // along_z, cols // along_z
    chunk = jax.ShapeDtypeStruct((along_z, t_rows + g_rows, total_cols), F32)
    keep, send, everything = pl.pallas_call(
        products,
        out_shape=(chunk, chunk, shape(total_cols, lanes, BF16)),
        in_specs=[VMEM] * 9 + [SMEM],
        out_specs=(VMEM,) * 3,
        scratch_shapes=[pltpu.VMEM((2, cols, lanes), BF16)] * 2,
        compiler_params=PARAMS,
    )(current, ahead, behind, coef, heavy, *others, targets, place)

    summed = keep + lax.ppermute(send, "dom", pair)
    summed = lax.all_to_all(summed, "dom", 0, 0, tiled=True, axis_index_groups=z_groups)
    summed = jnp.sum(summed, axis=0)
    one, two, three = [lax.ppermute(summed, "dom", x_ring(step)) for step in (1, 2, 3)]
    summed = (summed + two) + (one + three)
    gram = summed[t_rows:]
    found = [gram] + [lax.ppermute(gram, "col", col_ring(step)) for step in (1, 2, 3)]
    block = jnp.concatenate([summed[:t_rows]] + found, 0)
    block = jnp.broadcast_to(block[None], (along_z,) + block.shape)
    mine = lax.all_to_all(block, "dom", 0, 0, tiled=True, axis_index_groups=z_groups)
    theirs = lax.ppermute(mine, "dom", pair)
    modes, ritz_matrix, participation = pl.pallas_call(
        finish,
        out_shape=(shape(cols * width_y, width_z), shape(total_cols, total_cols), shape(total_cols // doms, 2 * half)),
        in_specs=[VMEM] * 6 + [SMEM],
        out_specs=(VMEM,) * 3,
        scratch_shapes=[pltpu.VMEM((rows, total_cols), F32) for rows in (total_cols, total_cols, 2 * half, total_cols)],
        compiler_params=PARAMS,
    )(current, everything, heavy, coef, mine, theirs, place)
    return (modes.reshape(start_block.shape), ritz_matrix, participation)


def solution(mesh):
    placed = (
        P("col", "dom", None, None),
        P("dom", None, None),
        P("dom", None, None),
        P(),
        P("col", "dom", None, None),
    )
    return jax.shard_map(
        local,
        mesh=mesh,
        in_specs=placed,
        out_specs=(P("col", "dom", None, None), P(), P("dom", "col")),
        check_vma=False,
    )
```

```python
import functools

import jax
import jax.numpy as jnp
import numpy as np
from jax import lax
from jax.experimental import pallas as pl
from jax.experimental.pallas import tpu as pltpu
from jax.sharding import PartitionSpec as P

DEGREE = 4
LOW_RATIO = 0.02
F32, BF16 = jnp.float32, jnp.bfloat16
VMEM = pl.BlockSpec(memory_space=pltpu.VMEM)
SMEM = pl.BlockSpec(memory_space=pltpu.SMEM)
WIDTH = 128
PARAMS = pltpu.CompilerParams(vmem_limit_bytes=48 * 1024 * 1024)
H4, HZ, HZ4, E, EZ, G, GZ, AM, MI, MS = range(10)


def shape(rows, lanes, dtype=F32):
    return jax.ShapeDtypeStruct((rows, lanes), dtype)


def lanes_of(y):
    return slice(y * WIDTH, (y + 1) * WIDTH)


def rows_of(group, size=16):
    return pl.ds(pl.multiple_of(group * size, size), size)


def twice(c):
    return jnp.concatenate([c, c], axis=0)


def stiffness_rows(width_y, u_at, v_at, w_at, coef):
    def with_roll(x):
        return x, pltpu.roll(x, WIDTH - 1, 1)

    u0, u1 = with_roll(u_at(0))
    v0, v1 = with_roll(v_at(0))
    w0, w1 = with_roll(w_at(0))
    kept = kept_z = None
    for y in range(width_y):
        c = functools.partial(coef, y)
        h4, hz, hz4 = c(H4), c(HZ), c(HZ4)
        ez, gz = c(EZ), c(GZ)
        p00 = ez * v0 + gz * w0
        p01 = ez * v1 + gz * w1
        if y + 1 < width_y:
            e, g = c(E), c(G)
            n0, n1 = with_roll(u_at(y + 1))
            x0, x1 = with_roll(v_at(y + 1))
            z0, z1 = with_roll(w_at(y + 1))
            p10 = ez * x0 + gz * z0
            p11 = ez * x1 + gz * z1
            q00 = e * v0 + g * w0
            q10 = e * x0 + g * z0
            side, other = p01 + p11, p00 + p10
            r00 = h4 * u0 - hz * n1 - q10 - side
            r10 = h4 * n0 - hz * u1 - q00 - side
            r01 = hz4 * u1 - hz * n0 - other - p11
            r11 = hz4 * n1 - hz * u0 - other - p01
        else:
            r00 = h4 * u0 - p01
            r01 = hz4 * u1 - p00
        here = r00 if kept is None else r00 + kept
        moved = r01 if kept_z is None else r01 + kept_z
        yield y, u0, here + pltpu.roll(moved, 1, 1)
        if y + 1 < width_y:
            kept, kept_z = r10, r11
            u0, u1, v0, v1, w0, w1 = n0, n1, x0, x1, z0, z1


def prepare(start_ref, ids_ref, mass_ref, field_ref, pay_ref, least_ref):
    width_y = ids_ref.shape[0]
    cols = field_ref.shape[0]
    for y in range(width_y):
        plane = start_ref[pl.ds(y, cols, stride=width_y), :]
        field_ref[:, lanes_of(y)] = plane
        pay_ref[:cols, lanes_of(y)] = plane.astype(BF16)
        code = (ids_ref[y : y + 1, :] + 1).astype(F32)
        pay_ref[cols:, lanes_of(y)] = jnp.broadcast_to(code, (16, WIDTH)).astype(BF16)
    least = jnp.min(jnp.min(mass_ref[...], axis=0, keepdims=True), axis=1, keepdims=True)
    least_ref[...] = jnp.broadcast_to(least, least_ref.shape)


def first_step(field_ref, near_ref, far_ref, ids_ref, mass_ref, least_ref, table_ref, place_ref, out_ref, pay_ref, coef_ref, shift_ref):
    cols, width_y = field_ref.shape[0], ids_ref.shape[0]
    materials = table_ref.shape[0]
    top = table_ref[0]
    for k in range(1, materials):
        top = jnp.maximum(top, table_ref[k])
    least = jnp.min(jnp.min(least_ref[...], axis=0, keepdims=True), axis=1, keepdims=True)
    upper = jnp.broadcast_to(16.0 / 3.0 * top / least, (8, WIDTH))
    lower = LOW_RATIO * upper
    half = (upper - lower) / 2.0
    shift = (upper + lower) / 2.0 / half
    shift_ref[...] = shift
    inner = lax.broadcasted_iota(jnp.int32, (8, WIDTH), 1) < WIDTH - 1

    def moduli(code):
        e = jnp.zeros(code.shape, F32)
        for k in range(materials):
            e = jnp.where(code == k + 1, table_ref[k], e)
        return e / 12.0

    for y in range(width_y):
        at = lanes_of(y)
        own = moduli(jnp.broadcast_to(ids_ref[y : y + 1, :] + 1, (8, WIDTH)))
        first = place_ref[0] == 0
        code = jnp.where(first, far_ref[cols:, at].astype(F32), near_ref[cols:, at].astype(F32))
        below = moduli(code[:8].astype(jnp.int32))
        near, far = jnp.where(first, own, below), jnp.where(first, below, own)
        mass = jnp.broadcast_to(mass_ref[y : y + 1, :], (8, WIDTH))
        both = near + far
        both_z = jnp.where(inner, both, 0.0)
        values = {
            H4: 4.0 * both,
            HZ: both_z,
            HZ4: 4.0 * both_z,
            E: near,
            EZ: jnp.where(inner, near, 0.0),
            G: far,
            GZ: jnp.where(inner, far, 0.0),
            AM: 1.0 / (mass * half),
            MI: 1.0 / mass,
            MS: mass,
        }
        for place, value in values.items():
            coef_ref[8 * place : 8 * place + 8, at] = value

    def coef(y, place):
        return twice(coef_ref[8 * place : 8 * place + 8, lanes_of(y)])

    def group(i, carry):
        at = rows_of(i)
        rows = stiffness_rows(
            width_y,
            lambda y: field_ref[at, lanes_of(y)],
            lambda y: near_ref[at, lanes_of(y)].astype(F32),
            lambda y: far_ref[at, lanes_of(y)].astype(F32),
            coef,
        )
        shift2 = twice(shift)
        for y, u, forces in rows:
            result = forces * coef(y, AM) - shift2 * u
            out_ref[at, lanes_of(y)] = result
            pay_ref[at, lanes_of(y)] = result.astype(BF16)
        return carry

    lax.fori_loop(0, cols // 16, group, 0)


def later_step(last, field_ref, before_ref, near_ref, far_ref, coef_ref, shift_ref, out_ref, pay_ref, *heavy_ref):
    cols = field_ref.shape[0]
    width_y = field_ref.shape[1] // WIDTH

    def coef(y, place):
        return twice(coef_ref[8 * place : 8 * place + 8, lanes_of(y)])

    def group(i, carry):
        at = rows_of(i)
        rows = stiffness_rows(
            width_y,
            lambda y: field_ref[at, lanes_of(y)],
            lambda y: near_ref[at, lanes_of(y)].astype(F32),
            lambda y: far_ref[at, lanes_of(y)].astype(F32),
            coef,
        )
        shift2 = twice(shift_ref[...])
        for y, u, forces in rows:
            result = 2.0 * (forces * coef(y, AM) - shift2 * u) - before_ref[at, lanes_of(y)]
            out_ref[at, lanes_of(y)] = result
            pay_ref[at, lanes_of(y)] = result.astype(BF16)
            if last:
                heavy_ref[0][at, lanes_of(y)] = (result * coef(y, MS)).astype(BF16)
        return carry

    lax.fori_loop(0, cols // 16, group, 0)


def dot_nt(a, b):
    return lax.dot_general(a, b, (((1,), (1,)), ((), ())), preferred_element_type=F32)


def products(field_ref, near_ref, far_ref, coef_ref, own_ref, one_ref, three_ref, two_low_ref, two_high_ref, target_ref, place_ref, keep_ref, send_ref, all_ref, high_ref, low_ref):
    cols = field_ref.shape[0]
    width_y = field_ref.shape[1] // WIDTH
    core, col = place_ref[0], place_ref[1]
    for step, ref in ((0, own_ref), (1, one_ref), (3, three_ref)):
        all_ref[rows_of(lax.rem(col + 4 - step, 4), cols), :] = ref[...]
    opposite = lax.rem(col + 2, 4) * 2
    all_ref[rows_of(opposite, cols // 2), :] = two_low_ref[...]
    all_ref[rows_of(opposite + 1, cols // 2), :] = two_high_ref[...]

    def coef(y, place):
        return twice(coef_ref[8 * place : 8 * place + 8, lanes_of(y)])

    def group(i, carry):
        at = rows_of(i)
        rows = stiffness_rows(
            width_y,
            lambda y: field_ref[at, lanes_of(y)],
            lambda y: near_ref[at, lanes_of(y)].astype(F32),
            lambda y: far_ref[at, lanes_of(y)].astype(F32),
            coef,
        )
        for y, u, forces in rows:
            scaled = forces * coef(y, MI)
            high = scaled.astype(BF16)
            high_ref[0, at, lanes_of(y)] = high
            low_ref[0, at, lanes_of(y)] = (scaled - high.astype(F32)).astype(BF16)
            high = u.astype(BF16)
            high_ref[1, at, lanes_of(y)] = high
            low_ref[1, at, lanes_of(y)] = (u - high.astype(F32)).astype(BF16)
        return carry

    lax.fori_loop(0, cols // 16, group, 0)
    everything = all_ref[...]
    half = target_ref.shape[0] // 2
    for side, ref in ((core, keep_ref), (1 - core, send_ref)):
        targets = dot_nt(target_ref[rows_of(side, half), :], everything)
        gram = dot_nt(high_ref[side], everything) + dot_nt(low_ref[side], everything)
        chunks = ref.shape[0]
        pad = jnp.zeros((2, gram.shape[1]), F32)
        for q in range(chunks):
            ref[q, :8, :] = targets[8 * q : 8 * q + 8]
            rest = targets[8 * chunks + 4 * q : 8 * chunks + 4 * q + 4]
            ref[q, 8:, :] = jnp.concatenate([rest, gram[2 * q : 2 * q + 2], pad], 0)


def split(x):
    high = x.astype(BF16)
    return high, (x - high.astype(F32)).astype(BF16)


def dot_split(a, b, dims):
    (ah, al), (bh, bl) = split(a), split(b)
    dot = functools.partial(lax.dot_general, dimension_numbers=(dims, ((), ())), preferred_element_type=F32)
    return dot(ah, bh) + (dot(ah, bl) + dot(al, bh))


def inverse_factor(work_ref, panel, few):
    n = work_ref.shape[0]
    tiles = n // WIDTH
    lane = lax.broadcasted_iota(jnp.int32, (panel, WIDTH), 1)
    row = lax.broadcasted_iota(jnp.int32, (panel, WIDTH), 0)
    for start in range(0, n, panel):
        at = slice(start, start + panel)
        lines = [work_ref[at, lanes_of(t)] for t in range(tiles)]
        pivots = jnp.zeros((panel, WIDTH), F32)
        for first in range(0, panel, few):
            columns, factors = [], []
            for place in range(start + first, start + first + few):
                tile, inside = divmod(place, WIDTH)
                columns.append(jnp.broadcast_to(lines[tile][:, inside : inside + 1], (panel, WIDTH)))
            for k in range(few):
                p = first + k
                pivot = columns[k][p : p + 1, :]
                factor = jnp.where(row > p, columns[k] * (1.0 / pivot), 0.0)
                pivots = jnp.where(row == p, pivot, pivots)
                for l in range(k + 1, few):
                    columns[l] = columns[l] - factor * columns[l][p : p + 1, :]
                factors.append(factor)
            for k in range(few):
                p = first + k
                tile, inside = divmod(start + p, WIDTH)
                for t in range(tiles):
                    line = lines[t][p : p + 1, :]
                    if t == tile:
                        line = line + jnp.where(lane[:1] == inside, 1.0, 0.0)
                    lines[t] = lines[t] - factors[k] * line
        scale = 1.0 / jnp.sqrt(pivots)
        factor_rows, update_rows = [], []
        for t in range(tiles):
            place = lane + t * WIDTH
            full = jnp.where(place == row + start, scale, lines[t] * scale)
            inverse = jnp.where(place <= row + start, full, 0.0)
            work_ref[at, lanes_of(t)] = inverse
            factor_rows.append(full)
            update_rows.append(jnp.where((place >= start) & (place < start + panel), inverse, full))
        rest = n - start - panel
        if rest:
            update = dot_split(jnp.concatenate(factor_rows, 1), jnp.concatenate(update_rows, 1), ((0,), (0,)))
            for t in range(tiles):
                old = work_ref[start + panel :, lanes_of(t)]
                place = lax.broadcasted_iota(jnp.int32, old.shape, 1) + t * WIDTH
                old = jnp.where((place >= start) & (place < start + panel), 0.0, old)
                work_ref[start + panel :, lanes_of(t)] = old - update[start + panel :, lanes_of(t)]


def finish(field_ref, all_ref, own_ref, coef_ref, mine_ref, theirs_ref, place_ref, modes_ref, ritz_ref, part_ref, mass_ref, stiff_ref, targets_ref, work_ref):
    core, col, me = place_ref[0], place_ref[1], place_ref[2]
    cols = field_ref.shape[0]
    width_y = field_ref.shape[1] // WIDTH
    total = work_ref.shape[0]
    groups = total // cols
    chunks = mine_ref.shape[0]
    half = targets_ref.shape[0] // 2
    low_first = core == 0
    for side in (0, 1):
        chosen = low_first == (side == 0)
        parts = [jnp.where(chosen, mine_ref[q], theirs_ref[q]) for q in range(chunks)]
        for q, part in enumerate(parts):
            targets_ref[side * half + 8 * q : side * half + 8 * q + 8, :] = part[:8]
        for q in range(0, chunks, 2):
            to = side * half + 8 * chunks + 4 * q
            targets_ref[to : to + 8, :] = jnp.concatenate([parts[q][8:12], parts[q + 1][8:12]], 0)
        into = mass_ref if side else stiff_ref
        for step in range(groups):
            at = 12 if step == 0 else 14 + 2 * step
            rows = jnp.concatenate([part[at : at + 2] for part in parts], 0)
            into[rows_of(lax.bitwise_xor(col, step), cols), :] = rows
    gram = mass_ref[...]
    on = lax.broadcasted_iota(jnp.int32, gram.shape, 0) == lax.broadcasted_iota(jnp.int32, gram.shape, 1)
    diagonal = jnp.where(on, gram, 0.0)
    across = 1.0 / jnp.sqrt(jnp.sum(diagonal, axis=0, keepdims=True))
    down = 1.0 / jnp.sqrt(jnp.sum(diagonal, axis=1, keepdims=True))
    work_ref[...] = gram * across * down
    inverse_factor(work_ref, 64, 16)
    inverse = work_ref[...] * across
    work_ref[...] = inverse
    ritz_ref[...] = dot_split(dot_split(inverse, stiff_ref[...], ((1,), (1,))), inverse, ((1,), (1,)))

    rows = work_ref[pl.ds(pl.multiple_of(me // 2 * 8, 8), 8), :]
    part = dot_split(rows, targets_ref[...], ((1,), (1,)))
    part_ref[...] = jnp.where(low_first, part[:4], part[4:])

    norm = jnp.float32(np.sqrt(np.float32(64 * width_y * WIDTH)))
    weights = work_ref[rows_of(col, cols), :]
    block = jnp.zeros((cols, cols), F32)
    for k in range(groups):
        block = jnp.where(col == k, weights[:, k * cols : (k + 1) * cols], block)
    block = block.astype(BF16)
    high, low = split(weights)
    for y in range(width_y):
        at = lanes_of(y)
        everything = all_ref[:, at]
        mass = jnp.concatenate([coef_ref[8 * MS : 8 * MS + 8, at]] * (cols // 8), axis=0)
        light = jnp.concatenate([coef_ref[8 * MI : 8 * MI + 8, at]] * (cols // 8), axis=0)
        rest = (field_ref[:, at] * mass - own_ref[:, at].astype(F32)).astype(BF16)
        result = (
            jnp.dot(high, everything, preferred_element_type=F32)
            + jnp.dot(low, everything, preferred_element_type=F32)
            + jnp.dot(block, rest, preferred_element_type=F32)
        )
        modes_ref[pl.ds(y, cols, stride=width_y), :] = result * light * norm


def local(start_block, node_mass, material_ids, moduli_table, influence):
    cols, _, width_y, width_z = start_block.shape
    lanes = width_y * width_z
    doms, groups = lax.axis_size("dom"), lax.axis_size("col")
    total_cols = cols * groups
    me, col = lax.axis_index("dom"), lax.axis_index("col")
    core = me % 2
    pair = [(i, i ^ 1) for i in range(doms)]
    across = [(i, i + 1 if i % 2 else i - 1) for i in range(1, doms - 1)]
    plane_groups = [list(range(r, doms, 2)) for r in range(2)]
    chunks = doms // 2

    def exchange(payload):
        far = lax.ppermute(payload, "dom", across)
        return lax.ppermute(payload, "dom", pair), far

    def col_ring(step):
        return [(i, (i + step) % groups) for i in range(groups)]

    def col_swap(step):
        return [(i, i ^ step) for i in range(groups)]

    place = jnp.stack([core, col, me]).astype(jnp.int32)
    ids = material_ids.reshape(width_y, width_z)
    mass = node_mass.reshape(width_y, width_z)
    targets = influence.reshape(influence.shape[0], lanes)

    field, pay, least = pl.pallas_call(
        prepare,
        out_shape=(shape(cols, lanes), shape(cols + 16, lanes, BF16), shape(doms, WIDTH)),
        in_specs=[VMEM] * 3,
        out_specs=(VMEM,) * 3,
        compiler_params=PARAMS,
    )(start_block.reshape(cols * width_y, width_z), ids, mass)
    near, far = exchange(pay)
    least = lax.all_to_all(least, "dom", 0, 0, tiled=True)

    current, pay, coef, shift = pl.pallas_call(
        first_step,
        out_shape=(shape(cols, lanes), shape(cols, lanes, BF16), shape(80, lanes), shape(8, WIDTH)),
        in_specs=[VMEM] * 6 + [SMEM] * 2,
        out_specs=(VMEM,) * 4,
        compiler_params=PARAMS,
    )(field, near, far, ids, mass, least, moduli_table, place)
    previous = field
    for step in range(DEGREE - 1):
        last = step == DEGREE - 2
        near, far = exchange(pay)
        outs = pl.pallas_call(
            functools.partial(later_step, last),
            out_shape=(shape(cols, lanes),) + (shape(cols, lanes, BF16),) * (2 if last else 1),
            in_specs=[VMEM] * 6,
            out_specs=(VMEM,) * (3 if last else 2),
            compiler_params=PARAMS,
        )(current, previous, near, far, coef, shift)
        previous, current, pay = current, outs[0], outs[1]
    heavy = outs[2]
    near, far = exchange(pay)
    one, three = lax.ppermute(heavy, "col", col_ring(1)), lax.ppermute(heavy, "col", col_ring(3))
    two_low = lax.ppermute(one[: cols // 2], "col", col_ring(1))
    two_high = lax.ppermute(three[cols // 2 :], "col", col_ring(3))
    half = targets.shape[0] // 2
    chunk = jax.ShapeDtypeStruct((chunks, 16, total_cols), F32)
    keep, send, everything = pl.pallas_call(
        products,
        out_shape=(chunk, chunk, shape(total_cols, lanes, BF16)),
        in_specs=[VMEM] * 10 + [SMEM],
        out_specs=(VMEM,) * 3,
        scratch_shapes=[pltpu.VMEM((2, cols, lanes), BF16)] * 2,
        compiler_params=PARAMS,
    )(current, near, far, coef, heavy, one, three, two_low, two_high, targets, place)

    summed = keep + lax.ppermute(send, "dom", pair)
    summed = lax.all_to_all(summed, "dom", 0, 0, tiled=True, axis_index_groups=plane_groups)
    summed = jnp.sum(summed, axis=0)
    found = [lax.ppermute(summed[8:], "col", col_swap(step))[4:6] for step in (1, 2, 3)]
    block = jnp.concatenate([summed] + found + [jnp.zeros((2, total_cols), F32)], 0)
    block = jnp.broadcast_to(block[None], (chunks,) + block.shape)
    mine = lax.all_to_all(block, "dom", 0, 0, tiled=True, axis_index_groups=plane_groups)
    theirs = lax.ppermute(mine, "dom", pair)
    modes, ritz_matrix, participation = pl.pallas_call(
        finish,
        out_shape=(shape(cols * width_y, width_z), shape(total_cols, total_cols), shape(total_cols // doms, 2 * half)),
        in_specs=[VMEM] * 6 + [SMEM],
        out_specs=(VMEM,) * 3,
        scratch_shapes=[pltpu.VMEM((rows, total_cols), F32) for rows in (total_cols, total_cols, 2 * half, total_cols)],
        compiler_params=PARAMS,
    )(current, everything, heavy, coef, mine, theirs, place)
    return (modes.reshape(start_block.shape), ritz_matrix, participation)


def solution(mesh):
    placed = (
        P("col", "dom", None, None),
        P("dom", None, None),
        P("dom", None, None),
        P(),
        P("col", "dom", None, None),
    )
    return jax.shard_map(
        local,
        mesh=mesh,
        in_specs=placed,
        out_specs=(P("col", "dom", None, None), P(), P("dom", "col")),
        check_vma=False,
    )
```

```python
import functools

import jax
import jax.numpy as jnp
import numpy as np
from jax import lax
from jax.experimental import pallas as pl
from jax.experimental.pallas import tpu as pltpu
from jax.sharding import PartitionSpec as P

DEGREE = 4
LOW_RATIO = 0.02
F32, BF16 = jnp.float32, jnp.bfloat16
VMEM = pl.BlockSpec(memory_space=pltpu.VMEM)
SMEM = pl.BlockSpec(memory_space=pltpu.SMEM)
WIDTH = 128
PARAMS = pltpu.CompilerParams(vmem_limit_bytes=24 * 1024 * 1024)
H4, HZ, HZ4, E, EZ, G, GZ, AM, MI, MS = range(10)


def shape(rows, lanes, dtype=F32):
    return jax.ShapeDtypeStruct((rows, lanes), dtype)


def lanes_of(y):
    return slice(y * WIDTH, (y + 1) * WIDTH)


def rows_of(group, size=16):
    return pl.ds(pl.multiple_of(group * size, size), size)


def twice(c):
    return jnp.concatenate([c, c], axis=0)


def stiffness_rows(width_y, u_at, v_at, w_at, coef):
    def with_roll(x):
        return x, pltpu.roll(x, WIDTH - 1, 1)

    u0, u1 = with_roll(u_at(0))
    v0, v1 = with_roll(v_at(0))
    w0, w1 = with_roll(w_at(0))
    kept = kept_z = None
    for y in range(width_y):
        c = functools.partial(coef, y)
        h4, hz, hz4 = c(H4), c(HZ), c(HZ4)
        ez, gz = c(EZ), c(GZ)
        p00 = ez * v0 + gz * w0
        p01 = ez * v1 + gz * w1
        if y + 1 < width_y:
            e, g = c(E), c(G)
            n0, n1 = with_roll(u_at(y + 1))
            x0, x1 = with_roll(v_at(y + 1))
            z0, z1 = with_roll(w_at(y + 1))
            p10 = ez * x0 + gz * z0
            p11 = ez * x1 + gz * z1
            q00 = e * v0 + g * w0
            q10 = e * x0 + g * z0
            side, other = p01 + p11, p00 + p10
            r00 = h4 * u0 - hz * n1 - q10 - side
            r10 = h4 * n0 - hz * u1 - q00 - side
            r01 = hz4 * u1 - hz * n0 - other - p11
            r11 = hz4 * n1 - hz * u0 - other - p01
        else:
            r00 = h4 * u0 - p01
            r01 = hz4 * u1 - p00
        here = r00 if kept is None else r00 + kept
        moved = r01 if kept_z is None else r01 + kept_z
        yield y, u0, here + pltpu.roll(moved, 1, 1)
        if y + 1 < width_y:
            kept, kept_z = r10, r11
            u0, u1, v0, v1, w0, w1 = n0, n1, x0, x1, z0, z1


def prepare(table_ref, start_hbm, ids_hbm, mass_hbm, field_ref, pay_ref, least_ref, own_ref, start_ref, ids_ref, mass_ref, sems):
    copies = [
        pltpu.make_async_copy(source, target, sems.at[i])
        for i, (source, target) in enumerate(((start_hbm, start_ref), (ids_hbm, ids_ref), (mass_hbm, mass_ref)))
    ]
    for copy in copies:
        copy.start()
    width_y = ids_ref.shape[0]
    cols = field_ref.shape[0]
    materials = table_ref.shape[0]
    top = table_ref[0]
    for k in range(1, materials):
        top = jnp.maximum(top, table_ref[k])
    own_ref[16:, :] = jnp.broadcast_to(top, (8, own_ref.shape[1]))
    copies[1].wait()
    copies[2].wait()
    ids, mass = ids_ref[...], mass_ref[...]
    least = jnp.min(jnp.min(mass, axis=0, keepdims=True), axis=1, keepdims=True)
    least_ref[...] = jnp.broadcast_to(least[None], least_ref.shape)
    moduli = jnp.zeros(ids.shape, F32)
    for k in range(materials):
        moduli = jnp.where(ids == k, table_ref[k], moduli)
    moduli = moduli / 12.0
    high = moduli.astype(BF16).astype(F32)
    middle = (moduli - high).astype(BF16).astype(F32)
    low = moduli - high - middle
    pad = jnp.zeros((13, WIDTH), F32)
    for y in range(width_y):
        at = lanes_of(y)
        own_ref[:8, at] = jnp.broadcast_to(moduli[y : y + 1], (8, WIDTH))
        own_ref[8:16, at] = jnp.broadcast_to(mass[y : y + 1], (8, WIDTH))
        parts = jnp.concatenate([high[y : y + 1], middle[y : y + 1], low[y : y + 1], pad], 0)
        pay_ref[cols:, at] = parts.astype(BF16)
    copies[0].wait()
    for y in range(width_y):
        plane = start_ref[pl.ds(y, cols, stride=width_y), :]
        field_ref[:, lanes_of(y)] = plane
        pay_ref[:cols, lanes_of(y)] = plane.astype(BF16)


def first_step(far_ref, near_ref, field_ref, own_ref, least_ref, place_ref, out_ref, pay_ref, coef_ref, shift_ref):
    cols = field_ref.shape[0]
    width_y = field_ref.shape[1] // WIDTH
    least = jnp.min(jnp.min(least_ref[...], axis=0), axis=1, keepdims=True)
    upper = 16.0 / 3.0 * own_ref[16:, :WIDTH] / least
    lower = LOW_RATIO * upper
    half = (upper - lower) / 2.0
    shift = (upper + lower) / 2.0 / half
    shift_ref[...] = shift
    inner = lax.broadcasted_iota(jnp.int32, (8, WIDTH), 1) < WIDTH - 1
    first = place_ref[0] == 0
    for y in range(width_y):
        at = lanes_of(y)
        own, mass = own_ref[:8, at], own_ref[8:16, at]
        parts = jnp.where(first, far_ref[cols:, at].astype(F32), near_ref[cols:, at].astype(F32))
        below = jnp.broadcast_to(parts[0:1] + parts[1:2] + parts[2:3], (8, WIDTH))
        near, far = jnp.where(first, own, below), jnp.where(first, below, own)
        both = near + far
        both_z = jnp.where(inner, both, 0.0)
        values = {
            H4: 4.0 * both,
            HZ: both_z,
            HZ4: 4.0 * both_z,
            E: near,
            EZ: jnp.where(inner, near, 0.0),
            G: far,
            GZ: jnp.where(inner, far, 0.0),
            AM: 1.0 / (mass * half),
            MI: 1.0 / mass,
            MS: mass,
        }
        for place, value in values.items():
            coef_ref[8 * place : 8 * place + 8, at] = value

    def coef(y, place):
        return twice(coef_ref[8 * place : 8 * place + 8, lanes_of(y)])

    def group(i, carry):
        at = rows_of(i)
        rows = stiffness_rows(
            width_y,
            lambda y: field_ref[at, lanes_of(y)],
            lambda y: near_ref[at, lanes_of(y)].astype(F32),
            lambda y: far_ref[at, lanes_of(y)].astype(F32),
            coef,
        )
        shift2 = twice(shift)
        for y, u, forces in rows:
            result = forces * coef(y, AM) - shift2 * u
            out_ref[at, lanes_of(y)] = result
            pay_ref[at, lanes_of(y)] = result.astype(BF16)
        return carry

    lax.fori_loop(0, cols // 16, group, 0)


def later_step(last, far_ref, near_ref, field_ref, before_ref, coef_ref, shift_ref, out_ref, pay_ref, *heavy_ref):
    cols = field_ref.shape[0]
    width_y = field_ref.shape[1] // WIDTH

    def coef(y, place):
        return twice(coef_ref[8 * place : 8 * place + 8, lanes_of(y)])

    def group(i, carry):
        at = rows_of(i)
        rows = stiffness_rows(
            width_y,
            lambda y: field_ref[at, lanes_of(y)],
            lambda y: near_ref[at, lanes_of(y)].astype(F32),
            lambda y: far_ref[at, lanes_of(y)].astype(F32),
            coef,
        )
        shift2 = twice(shift_ref[...])
        for y, u, forces in rows:
            result = 2.0 * (forces * coef(y, AM) - shift2 * u) - before_ref[at, lanes_of(y)]
            out_ref[at, lanes_of(y)] = result
            pay_ref[at, lanes_of(y)] = result.astype(BF16)
            if last:
                heavy_ref[0][at, lanes_of(y)] = (result * coef(y, MS)).astype(BF16)
        return carry

    lax.fori_loop(0, cols // 16, group, 0)


def dot_nt(a, b):
    return lax.dot_general(a, b, (((1,), (1,)), ((), ())), preferred_element_type=F32)


def spread(ref, lanes, targets, gram):
    chunks = ref.shape[0]
    pad = jnp.zeros((2, gram.shape[1]), F32)
    for q in range(chunks):
        ref[q, :8, lanes] = targets[8 * q : 8 * q + 8]
        rest = targets[8 * chunks + 4 * q : 8 * chunks + 4 * q + 4]
        ref[q, 8:, lanes] = jnp.concatenate([rest, gram[2 * q : 2 * q + 2], pad], 0)


def products(far_ref, near_ref, one_ref, three_ref, field_ref, coef_ref, own_ref, target_ref, place_ref, keep_ref, send_ref, high_ref, low_ref, all_ref):
    cols = field_ref.shape[0]
    width_y = field_ref.shape[1] // WIDTH
    core = place_ref[0]
    all_ref[:cols] = own_ref[...]
    all_ref[cols : 2 * cols] = three_ref[...]
    all_ref[2 * cols : 3 * cols] = jnp.zeros((cols, all_ref.shape[1]), BF16)
    all_ref[3 * cols :] = one_ref[...]

    def coef(y, place):
        return twice(coef_ref[8 * place : 8 * place + 8, lanes_of(y)])

    def group(i, carry):
        at = rows_of(i)
        rows = stiffness_rows(
            width_y,
            lambda y: field_ref[at, lanes_of(y)],
            lambda y: near_ref[at, lanes_of(y)].astype(F32),
            lambda y: far_ref[at, lanes_of(y)].astype(F32),
            coef,
        )
        for y, u, forces in rows:
            scaled = forces * coef(y, MI)
            high = scaled.astype(BF16)
            high_ref[0, at, lanes_of(y)] = high
            low_ref[0, at, lanes_of(y)] = (scaled - high.astype(F32)).astype(BF16)
            high = u.astype(BF16)
            high_ref[1, at, lanes_of(y)] = high
            low_ref[1, at, lanes_of(y)] = (u - high.astype(F32)).astype(BF16)
        return carry

    lax.fori_loop(0, cols // 16, group, 0)
    everything = all_ref[...]
    half = target_ref.shape[0] // 2
    for side, ref in ((core, keep_ref), (1 - core, send_ref)):
        targets = dot_nt(target_ref[rows_of(side, half), :], everything)
        gram = dot_nt(high_ref[side], everything) + dot_nt(low_ref[side], everything)
        spread(ref, slice(None), targets, gram)


def opposite(keep_in, send_in, high_ref, low_ref, two_low_ref, two_high_ref, target_ref, place_ref, keep_ref, send_ref):
    core = place_ref[0]
    cols = high_ref.shape[1]
    two = jnp.concatenate([two_low_ref[...], two_high_ref[...]], 0)
    half = target_ref.shape[0] // 2
    for side, ref in ((core, keep_ref), (1 - core, send_ref)):
        targets = dot_nt(target_ref[rows_of(side, half), :], two)
        gram = dot_nt(high_ref[side], two) + dot_nt(low_ref[side], two)
        spread(ref, slice(2 * cols, 3 * cols), targets, gram)


def turned(x, steps, cols):
    groups = x.shape[1] // cols

    def by(k):
        return jnp.concatenate([x[:, (groups - k) * cols :], x[:, : (groups - k) * cols]], 1)

    result = x
    for k in range(1, groups):
        result = jnp.where(steps == k, by(k), result)
    return result


def split(x):
    high = x.astype(BF16)
    return high, (x - high.astype(F32)).astype(BF16)


def dot_split(a, b, dims):
    (ah, al), (bh, bl) = split(a), split(b)
    dot = functools.partial(lax.dot_general, dimension_numbers=(dims, ((), ())), preferred_element_type=F32)
    return dot(ah, bh) + (dot(ah, bl) + dot(al, bh))


def inverse_factor(work_ref, panel, few):
    n = work_ref.shape[0]
    tiles = n // WIDTH
    lane = lax.broadcasted_iota(jnp.int32, (panel, WIDTH), 1)
    row = lax.broadcasted_iota(jnp.int32, (panel, WIDTH), 0)
    for start in range(0, n, panel):
        at = slice(start, start + panel)
        lines = [work_ref[at, lanes_of(t)] for t in range(tiles)]
        pivots = jnp.zeros((panel, WIDTH), F32)
        for first in range(0, panel, few):
            columns, factors = [], []
            for place in range(start + first, start + first + few):
                tile, inside = divmod(place, WIDTH)
                columns.append(jnp.broadcast_to(lines[tile][:, inside : inside + 1], (panel, WIDTH)))
            for k in range(few):
                p = first + k
                pivot = columns[k][p : p + 1, :]
                factor = jnp.where(row > p, columns[k] * (1.0 / pivot), 0.0)
                pivots = jnp.where(row == p, pivot, pivots)
                for l in range(k + 1, few):
                    columns[l] = columns[l] - factor * columns[l][p : p + 1, :]
                factors.append(factor)
            for k in range(few):
                p = first + k
                tile, inside = divmod(start + p, WIDTH)
                for t in range(tiles):
                    line = lines[t][p : p + 1, :]
                    if t == tile:
                        line = line + jnp.where(lane[:1] == inside, 1.0, 0.0)
                    lines[t] = lines[t] - factors[k] * line
        scale = 1.0 / jnp.sqrt(pivots)
        factor_rows, update_rows = [], []
        for t in range(tiles):
            place = lane + t * WIDTH
            full = jnp.where(place == row + start, scale, lines[t] * scale)
            inverse = jnp.where(place <= row + start, full, 0.0)
            work_ref[at, lanes_of(t)] = inverse
            factor_rows.append(full)
            update_rows.append(jnp.where((place >= start) & (place < start + panel), inverse, full))
        rest = n - start - panel
        if rest:
            update = dot_split(jnp.concatenate(factor_rows, 1), jnp.concatenate(update_rows, 1), ((0,), (0,)))
            for t in range(tiles):
                old = work_ref[start + panel :, lanes_of(t)]
                place = lax.broadcasted_iota(jnp.int32, old.shape, 1) + t * WIDTH
                old = jnp.where((place >= start) & (place < start + panel), 0.0, old)
                work_ref[start + panel :, lanes_of(t)] = old - update[start + panel :, lanes_of(t)]


def finish(field_ref, own_ref, three_ref, two_low_ref, two_high_ref, one_ref, coef_ref, mine_ref, theirs_ref, place_ref, modes_ref, ritz_ref, part_ref, mass_ref, stiff_ref, targets_ref, work_ref):
    core, col, me = place_ref[0], place_ref[1], place_ref[2]
    cols = field_ref.shape[0]
    width_y = field_ref.shape[1] // WIDTH
    total = work_ref.shape[0]
    groups = total // cols
    chunks = mine_ref.shape[0]
    half = targets_ref.shape[0] // 2
    low_first = core == 0
    for side in (0, 1):
        chosen = low_first == (side == 0)
        parts = [jnp.where(chosen, mine_ref[q], theirs_ref[q]) for q in range(chunks)]
        for q, part in enumerate(parts):
            targets_ref[side * half + 8 * q : side * half + 8 * q + 8, :] = part[:8]
        for q in range(0, chunks, 2):
            to = side * half + 8 * chunks + 4 * q
            targets_ref[to : to + 8, :] = jnp.concatenate([parts[q][8:12], parts[q + 1][8:12]], 0)
        into = mass_ref if side else stiff_ref
        for step in range(groups):
            at = 12 if step == 0 else 14 + 2 * step
            rows = jnp.concatenate([part[at : at + 2] for part in parts], 0)
            source = lax.bitwise_xor(col, step)
            into[rows_of(source, cols), :] = turned(rows, source, cols)
    gram = mass_ref[...]
    on = lax.broadcasted_iota(jnp.int32, gram.shape, 0) == lax.broadcasted_iota(jnp.int32, gram.shape, 1)
    diagonal = jnp.where(on, gram, 0.0)
    across = 1.0 / jnp.sqrt(jnp.sum(diagonal, axis=0, keepdims=True))
    down = 1.0 / jnp.sqrt(jnp.sum(diagonal, axis=1, keepdims=True))
    work_ref[...] = gram * across * down
    inverse_factor(work_ref, 64, 16)
    inverse = work_ref[...] * across
    work_ref[...] = inverse
    ritz_ref[...] = dot_split(dot_split(inverse, stiff_ref[...], ((1,), (1,))), inverse, ((1,), (1,)))

    rows = work_ref[pl.ds(pl.multiple_of(me // 2 * 8, 8), 8), :]
    back = lax.rem(groups - col, groups)
    part = dot_split(turned(rows, back, cols), targets_ref[...], ((1,), (1,)))
    part_ref[...] = jnp.where(low_first, part[:4], part[4:])

    norm = jnp.float32(np.sqrt(np.float32(64 * width_y * WIDTH)))
    weights = turned(work_ref[rows_of(col, cols), :], back, cols)
    block = weights[:, :cols].astype(BF16)
    high, low = split(weights)
    held = (own_ref, three_ref, two_low_ref, two_high_ref, one_ref)
    for y in range(width_y):
        at = lanes_of(y)
        everything = jnp.concatenate([ref[:, at] for ref in held], 0)
        mass = jnp.concatenate([coef_ref[8 * MS : 8 * MS + 8, at]] * (cols // 8), axis=0)
        light = jnp.concatenate([coef_ref[8 * MI : 8 * MI + 8, at]] * (cols // 8), axis=0)
        rest = (field_ref[:, at] * mass - own_ref[:, at].astype(F32)).astype(BF16)
        result = (
            jnp.dot(high, everything, preferred_element_type=F32)
            + jnp.dot(low, everything, preferred_element_type=F32)
            + jnp.dot(block, rest, preferred_element_type=F32)
        )
        modes_ref[pl.ds(y, cols, stride=width_y), :] = result * light * norm


def local(start_block, node_mass, material_ids, moduli_table, influence):
    cols, _, width_y, width_z = start_block.shape
    lanes = width_y * width_z
    doms, groups = lax.axis_size("dom"), lax.axis_size("col")
    total_cols = cols * groups
    me, col = lax.axis_index("dom"), lax.axis_index("col")
    core = me % 2
    pair = [(i, i ^ 1) for i in range(doms)]
    across = [(i, i + 1 if i % 2 else i - 1) for i in range(1, doms - 1)]
    plane_groups = [list(range(r, doms, 2)) for r in range(2)]
    chunks = doms // 2

    def exchange(payload):
        near = lax.ppermute(payload, "dom", pair)
        return near, lax.ppermute(payload, "dom", across)

    def col_ring(step):
        return [(i, (i + step) % groups) for i in range(groups)]

    def col_swap(step):
        return [(i, i ^ step) for i in range(groups)]

    place = jnp.stack([core, col, me]).astype(jnp.int32)
    ids = material_ids.reshape(width_y, width_z)
    mass = node_mass.reshape(width_y, width_z)
    targets = influence.reshape(influence.shape[0], lanes)

    field, pay, least, own = pl.pallas_call(
        prepare,
        out_shape=(
            shape(cols, lanes),
            shape(cols + 16, lanes, BF16),
            jax.ShapeDtypeStruct((doms, 1, WIDTH), F32),
            shape(24, lanes),
        ),
        in_specs=[SMEM] + [pl.BlockSpec(memory_space=pltpu.HBM)] * 3,
        out_specs=(VMEM,) * 4,
        scratch_shapes=[
            pltpu.VMEM((cols * width_y, width_z), F32),
            pltpu.VMEM((width_y, width_z), jnp.int32),
            pltpu.VMEM((width_y, width_z), F32),
            pltpu.SemaphoreType.DMA((3,)),
        ],
        compiler_params=PARAMS,
    )(moduli_table, start_block.reshape(cols * width_y, width_z), ids, mass)
    near, far = exchange(pay)
    least = lax.all_to_all(least, "dom", 0, 0, tiled=True)

    current, pay, coef, shift = pl.pallas_call(
        first_step,
        out_shape=(shape(cols, lanes), shape(cols, lanes, BF16), shape(80, lanes), shape(8, WIDTH)),
        in_specs=[VMEM] * 5 + [SMEM],
        out_specs=(VMEM,) * 4,
        compiler_params=PARAMS,
    )(far, near, field, own, least, place)
    previous = field
    for step in range(DEGREE - 1):
        last = step == DEGREE - 2
        near, far = exchange(pay)
        outs = pl.pallas_call(
            functools.partial(later_step, last),
            out_shape=(shape(cols, lanes),) + (shape(cols, lanes, BF16),) * (2 if last else 1),
            in_specs=[VMEM] * 6,
            out_specs=(VMEM,) * (3 if last else 2),
            compiler_params=PARAMS,
        )(far, near, current, previous, coef, shift)
        previous, current, pay = current, outs[0], outs[1]
    heavy = outs[2]
    near, far = exchange(pay)
    one, three = lax.ppermute(heavy, "col", col_ring(1)), lax.ppermute(heavy, "col", col_ring(3))
    two_low = lax.ppermute(one[: cols // 2], "col", col_ring(1))
    two_high = lax.ppermute(three[cols // 2 :], "col", col_ring(3))
    half = targets.shape[0] // 2
    chunk = jax.ShapeDtypeStruct((chunks, 16, total_cols), F32)
    parts = jax.ShapeDtypeStruct((2, cols, lanes), BF16)
    keep, send, high, low = pl.pallas_call(
        products,
        out_shape=(chunk, chunk, parts, parts),
        in_specs=[VMEM] * 8 + [SMEM],
        out_specs=(VMEM,) * 4,
        scratch_shapes=[pltpu.VMEM((total_cols, lanes), BF16)],
        compiler_params=PARAMS,
    )(far, near, one, three, current, coef, heavy, targets, place)
    keep, send = pl.pallas_call(
        opposite,
        out_shape=(chunk, chunk),
        in_specs=[VMEM] * 7 + [SMEM],
        out_specs=(VMEM,) * 2,
        input_output_aliases={0: 0, 1: 1},
        compiler_params=PARAMS,
    )(keep, send, high, low, two_low, two_high, targets, place)

    summed = keep + lax.ppermute(send, "dom", pair)
    summed = lax.all_to_all(summed, "dom", 0, 0, tiled=True, axis_index_groups=plane_groups)
    summed = jnp.sum(summed, axis=0)
    found = [lax.ppermute(summed[8:], "col", col_swap(step))[4:6] for step in (1, 2, 3)]
    block = jnp.concatenate([summed] + found + [jnp.zeros((2, total_cols), F32)], 0)
    block = jnp.broadcast_to(block[None], (chunks,) + block.shape)
    mine = lax.all_to_all(block, "dom", 0, 0, tiled=True, axis_index_groups=plane_groups)
    theirs = lax.ppermute(mine, "dom", pair)
    modes, ritz_matrix, participation = pl.pallas_call(
        finish,
        out_shape=(shape(cols * width_y, width_z), shape(total_cols, total_cols), shape(total_cols // doms, 2 * half)),
        in_specs=[VMEM] * 9 + [SMEM],
        out_specs=(VMEM,) * 3,
        scratch_shapes=[pltpu.VMEM((rows, total_cols), F32) for rows in (total_cols, total_cols, 2 * half, total_cols)],
        compiler_params=PARAMS,
    )(current, heavy, three, two_low, two_high, one, coef, mine, theirs, place)
    return (modes.reshape(start_block.shape), ritz_matrix, participation)


def solution(mesh):
    placed = (
        P("col", "dom", None, None),
        P("dom", None, None),
        P("dom", None, None),
        P(),
        P("col", "dom", None, None),
    )
    return jax.shard_map(
        local,
        mesh=mesh,
        in_specs=placed,
        out_specs=(P("col", "dom", None, None), P(), P("dom", "col")),
        check_vma=False,
    )
```

```python
import functools

import jax
import jax.numpy as jnp
import numpy as np
from jax import lax
from jax.experimental import pallas as pl
from jax.experimental.pallas import tpu as pltpu
from jax.sharding import PartitionSpec as P

DEGREE = 4
LOW_RATIO = 0.02
F32, BF16 = jnp.float32, jnp.bfloat16
VMEM = pl.BlockSpec(memory_space=pltpu.VMEM)
SMEM = pl.BlockSpec(memory_space=pltpu.SMEM)
WIDTH = 128
PARAMS = pltpu.CompilerParams(vmem_limit_bytes=24 * 1024 * 1024)
H4, HZ, HZ4, E, EZ, G, GZ, AM, MI, MS = range(10)


def shape(rows, lanes, dtype=F32):
    return jax.ShapeDtypeStruct((rows, lanes), dtype)


def lanes_of(y):
    return slice(y * WIDTH, (y + 1) * WIDTH)


def rows_of(group, size=16):
    return pl.ds(pl.multiple_of(group * size, size), size)


def twice(c):
    return jnp.concatenate([c, c], axis=0)


def stiffness_rows(width_y, u_at, v_at, w_at, coef):
    def with_roll(x):
        return x, pltpu.roll(x, WIDTH - 1, 1)

    u0, u1 = with_roll(u_at(0))
    v0, v1 = with_roll(v_at(0))
    w0, w1 = with_roll(w_at(0))
    kept = kept_z = None
    for y in range(width_y):
        c = functools.partial(coef, y)
        h4, hz, hz4 = c(H4), c(HZ), c(HZ4)
        ez, gz = c(EZ), c(GZ)
        p00 = ez * v0 + gz * w0
        p01 = ez * v1 + gz * w1
        if y + 1 < width_y:
            e, g = c(E), c(G)
            n0, n1 = with_roll(u_at(y + 1))
            x0, x1 = with_roll(v_at(y + 1))
            z0, z1 = with_roll(w_at(y + 1))
            p10 = ez * x0 + gz * z0
            p11 = ez * x1 + gz * z1
            q00 = e * v0 + g * w0
            q10 = e * x0 + g * z0
            side, other = p01 + p11, p00 + p10
            r00 = h4 * u0 - hz * n1 - q10 - side
            r10 = h4 * n0 - hz * u1 - q00 - side
            r01 = hz4 * u1 - hz * n0 - other - p11
            r11 = hz4 * n1 - hz * u0 - other - p01
        else:
            r00 = h4 * u0 - p01
            r01 = hz4 * u1 - p00
        here = r00 if kept is None else r00 + kept
        moved = r01 if kept_z is None else r01 + kept_z
        yield y, u0, here + pltpu.roll(moved, 1, 1)
        if y + 1 < width_y:
            kept, kept_z = r10, r11
            u0, u1, v0, v1, w0, w1 = n0, n1, x0, x1, z0, z1


def prepare(table_ref, start_hbm, ids_hbm, mass_hbm, field_ref, pay_ref, least_ref, own_ref, start_ref, ids_ref, mass_ref, sems):
    copies = [
        pltpu.make_async_copy(source, target, sems.at[i])
        for i, (source, target) in enumerate(((start_hbm, start_ref), (ids_hbm, ids_ref), (mass_hbm, mass_ref)))
    ]
    for copy in copies:
        copy.start()
    width_y = ids_ref.shape[0]
    cols = field_ref.shape[0]
    materials = table_ref.shape[0]
    top = table_ref[0]
    for k in range(1, materials):
        top = jnp.maximum(top, table_ref[k])
    own_ref[16:, :] = jnp.broadcast_to(top, (8, own_ref.shape[1]))
    copies[1].wait()
    copies[2].wait()
    ids, mass = ids_ref[...], mass_ref[...]
    least = jnp.min(jnp.min(mass, axis=0, keepdims=True), axis=1, keepdims=True)
    least_ref[...] = jnp.broadcast_to(least[None], least_ref.shape)
    moduli = jnp.zeros(ids.shape, F32)
    for k in range(materials):
        moduli = jnp.where(ids == k, table_ref[k], moduli)
    moduli = moduli / 12.0
    high = moduli.astype(BF16).astype(F32)
    middle = (moduli - high).astype(BF16).astype(F32)
    low = moduli - high - middle
    pad = jnp.zeros((13, WIDTH), F32)
    for y in range(width_y):
        at = lanes_of(y)
        own_ref[:8, at] = jnp.broadcast_to(moduli[y : y + 1], (8, WIDTH))
        own_ref[8:16, at] = jnp.broadcast_to(mass[y : y + 1], (8, WIDTH))
        parts = jnp.concatenate([high[y : y + 1], middle[y : y + 1], low[y : y + 1], pad], 0)
        pay_ref[cols:, at] = parts.astype(BF16)
    copies[0].wait()
    for y in range(width_y):
        plane = start_ref[pl.ds(y, cols, stride=width_y), :]
        field_ref[:, lanes_of(y)] = plane
        pay_ref[:cols, lanes_of(y)] = plane.astype(BF16)


def first_step(far_ref, near_ref, field_ref, own_ref, least_ref, place_ref, out_ref, pay_ref, coef_ref, shift_ref):
    cols = field_ref.shape[0]
    width_y = field_ref.shape[1] // WIDTH
    least = jnp.min(jnp.min(least_ref[...], axis=0), axis=1, keepdims=True)
    upper = 16.0 / 3.0 * own_ref[16:, :WIDTH] / least
    lower = LOW_RATIO * upper
    half = (upper - lower) / 2.0
    shift = (upper + lower) / 2.0 / half
    shift_ref[...] = shift
    inner = lax.broadcasted_iota(jnp.int32, (8, WIDTH), 1) < WIDTH - 1
    first = place_ref[0] == 0
    for y in range(width_y):
        at = lanes_of(y)
        own, mass = own_ref[:8, at], own_ref[8:16, at]
        parts = jnp.where(first, far_ref[cols:, at].astype(F32), near_ref[cols:, at].astype(F32))
        below = jnp.broadcast_to(parts[0:1] + parts[1:2] + parts[2:3], (8, WIDTH))
        near, far = jnp.where(first, own, below), jnp.where(first, below, own)
        both = near + far
        both_z = jnp.where(inner, both, 0.0)
        values = {
            H4: 4.0 * both,
            HZ: both_z,
            HZ4: 4.0 * both_z,
            E: near,
            EZ: jnp.where(inner, near, 0.0),
            G: far,
            GZ: jnp.where(inner, far, 0.0),
            AM: 1.0 / (mass * half),
            MI: 1.0 / mass,
            MS: mass,
        }
        for place, value in values.items():
            coef_ref[8 * place : 8 * place + 8, at] = value

    def coef(y, place):
        return twice(coef_ref[8 * place : 8 * place + 8, lanes_of(y)])

    def group(i, carry):
        at = rows_of(i)
        rows = stiffness_rows(
            width_y,
            lambda y: field_ref[at, lanes_of(y)],
            lambda y: near_ref[at, lanes_of(y)].astype(F32),
            lambda y: far_ref[at, lanes_of(y)].astype(F32),
            coef,
        )
        shift2 = twice(shift)
        for y, u, forces in rows:
            result = forces * coef(y, AM) - shift2 * u
            out_ref[at, lanes_of(y)] = result
            pay_ref[at, lanes_of(y)] = result.astype(BF16)
        return carry

    lax.fori_loop(0, cols // 16, group, 0)


def later_step(last, far_ref, near_ref, field_ref, before_ref, coef_ref, shift_ref, out_ref, pay_ref, *heavy_ref):
    cols = field_ref.shape[0]
    width_y = field_ref.shape[1] // WIDTH

    def coef(y, place):
        return twice(coef_ref[8 * place : 8 * place + 8, lanes_of(y)])

    def group(i, carry):
        at = rows_of(i)
        rows = stiffness_rows(
            width_y,
            lambda y: field_ref[at, lanes_of(y)],
            lambda y: near_ref[at, lanes_of(y)].astype(F32),
            lambda y: far_ref[at, lanes_of(y)].astype(F32),
            coef,
        )
        shift2 = twice(shift_ref[...])
        for y, u, forces in rows:
            result = 2.0 * (forces * coef(y, AM) - shift2 * u) - before_ref[at, lanes_of(y)]
            out_ref[at, lanes_of(y)] = result
            pay_ref[at, lanes_of(y)] = result.astype(BF16)
            if last:
                heavy_ref[0][at, lanes_of(y)] = (result * coef(y, MS)).astype(BF16)
        return carry

    lax.fori_loop(0, cols // 16, group, 0)


def dot_nt(a, b):
    return lax.dot_general(a, b, (((1,), (1,)), ((), ())), preferred_element_type=F32)


def spread(ref, lanes, targets, gram):
    parts = ref.shape[0]
    t, g = targets.shape[0] // parts, gram.shape[0] // parts
    for x in range(parts):
        ref[x, :t, lanes] = targets[x * t : (x + 1) * t]
        ref[x, t:, lanes] = gram[x * g : (x + 1) * g]


def products(far_ref, near_ref, one_ref, three_ref, field_ref, coef_ref, own_ref, target_ref, place_ref, keep_ref, send_ref, high_ref, low_ref, all_ref):
    cols = field_ref.shape[0]
    width_y = field_ref.shape[1] // WIDTH
    core = place_ref[0]
    all_ref[:cols] = own_ref[...]
    all_ref[cols : 2 * cols] = three_ref[...]
    all_ref[2 * cols : 3 * cols] = jnp.zeros((cols, all_ref.shape[1]), BF16)
    all_ref[3 * cols :] = one_ref[...]

    def coef(y, place):
        return twice(coef_ref[8 * place : 8 * place + 8, lanes_of(y)])

    def group(i, carry):
        at = rows_of(i)
        rows = stiffness_rows(
            width_y,
            lambda y: field_ref[at, lanes_of(y)],
            lambda y: near_ref[at, lanes_of(y)].astype(F32),
            lambda y: far_ref[at, lanes_of(y)].astype(F32),
            coef,
        )
        for y, u, forces in rows:
            scaled = forces * coef(y, MI)
            high = scaled.astype(BF16)
            high_ref[0, at, lanes_of(y)] = high
            low_ref[0, at, lanes_of(y)] = (scaled - high.astype(F32)).astype(BF16)
            high = u.astype(BF16)
            high_ref[1, at, lanes_of(y)] = high
            low_ref[1, at, lanes_of(y)] = (u - high.astype(F32)).astype(BF16)
        return carry

    lax.fori_loop(0, cols // 16, group, 0)
    everything = all_ref[...]
    half = target_ref.shape[0] // 2
    for side, ref in ((core, keep_ref), (1 - core, send_ref)):
        targets = dot_nt(target_ref[rows_of(side, half), :], everything)
        gram = dot_nt(high_ref[side], everything) + dot_nt(low_ref[side], everything)
        spread(ref, slice(None), targets, gram)


def opposite(keep_in, send_in, high_ref, low_ref, two_low_ref, two_high_ref, target_ref, place_ref, keep_ref, send_ref):
    core = place_ref[0]
    cols = high_ref.shape[1]
    two = jnp.concatenate([two_low_ref[...], two_high_ref[...]], 0)
    half = target_ref.shape[0] // 2
    for side, ref in ((core, keep_ref), (1 - core, send_ref)):
        targets = dot_nt(target_ref[rows_of(side, half), :], two)
        gram = dot_nt(high_ref[side], two) + dot_nt(low_ref[side], two)
        spread(ref, slice(2 * cols, 3 * cols), targets, gram)


def turned(x, steps, cols):
    groups = x.shape[1] // cols

    def by(k):
        return jnp.concatenate([x[:, (groups - k) * cols :], x[:, : (groups - k) * cols]], 1)

    result = x
    for k in range(1, groups):
        result = jnp.where(steps == k, by(k), result)
    return result


def split(x):
    high = x.astype(BF16)
    return high, (x - high.astype(F32)).astype(BF16)


def dot_split(a, b, dims):
    (ah, al), (bh, bl) = split(a), split(b)
    dot = functools.partial(lax.dot_general, dimension_numbers=(dims, ((), ())), preferred_element_type=F32)
    return dot(ah, bh) + (dot(ah, bl) + dot(al, bh))


def inverse_factor(work_ref, panel, few):
    n = work_ref.shape[0]
    tiles = n // WIDTH
    lane = lax.broadcasted_iota(jnp.int32, (panel, WIDTH), 1)
    row = lax.broadcasted_iota(jnp.int32, (panel, WIDTH), 0)
    for start in range(0, n, panel):
        at = slice(start, start + panel)
        lines = [work_ref[at, lanes_of(t)] for t in range(tiles)]
        pivots = jnp.zeros((panel, WIDTH), F32)
        for first in range(0, panel, few):
            columns, factors = [], []
            for place in range(start + first, start + first + few):
                tile, inside = divmod(place, WIDTH)
                columns.append(jnp.broadcast_to(lines[tile][:, inside : inside + 1], (panel, WIDTH)))
            for k in range(few):
                p = first + k
                pivot = columns[k][p : p + 1, :]
                factor = jnp.where(row > p, columns[k] * (1.0 / pivot), 0.0)
                pivots = jnp.where(row == p, pivot, pivots)
                for l in range(k + 1, few):
                    columns[l] = columns[l] - factor * columns[l][p : p + 1, :]
                factors.append(factor)
            for k in range(few):
                p = first + k
                tile, inside = divmod(start + p, WIDTH)
                for t in range(tiles):
                    line = lines[t][p : p + 1, :]
                    if t == tile:
                        line = line + jnp.where(lane[:1] == inside, 1.0, 0.0)
                    lines[t] = lines[t] - factors[k] * line
        scale = 1.0 / jnp.sqrt(pivots)
        factor_rows, update_rows = [], []
        for t in range(tiles):
            place = lane + t * WIDTH
            full = jnp.where(place == row + start, scale, lines[t] * scale)
            inverse = jnp.where(place <= row + start, full, 0.0)
            work_ref[at, lanes_of(t)] = inverse
            factor_rows.append(full)
            update_rows.append(jnp.where((place >= start) & (place < start + panel), inverse, full))
        rest = n - start - panel
        if rest:
            update = dot_split(jnp.concatenate(factor_rows, 1), jnp.concatenate(update_rows, 1), ((0,), (0,)))
            for t in range(tiles):
                old = work_ref[start + panel :, lanes_of(t)]
                place = lax.broadcasted_iota(jnp.int32, old.shape, 1) + t * WIDTH
                old = jnp.where((place >= start) & (place < start + panel), 0.0, old)
                work_ref[start + panel :, lanes_of(t)] = old - update[start + panel :, lanes_of(t)]


def along_z(parts_ref, out_ref):
    total = jnp.sum(parts_ref[...], axis=0)
    planes, rows = out_ref.shape[:2]
    g = rows // 2
    t = (total.shape[0] - g) // planes
    for z in range(planes):
        out_ref[z, :t, :] = total[z * t : (z + 1) * t]
        out_ref[z, t:g, :] = jnp.zeros((g - t, total.shape[1]), F32)
        out_ref[z, g:, :] = total[planes * t :]


def along_chips(parts_ref, target_ref, gram_ref):
    total = jnp.sum(parts_ref[...], axis=0)
    g = gram_ref.shape[1]
    t = target_ref.shape[0] // 2
    target_ref[...] = jnp.concatenate([total[:t, :WIDTH], total[:t, WIDTH:]], 0)
    for chip in range(gram_ref.shape[0]):
        gram_ref[chip] = total[g:]


def for_all(rows_ref, earlier_ref, copies_ref):
    rows = rows_ref[...]
    for i in range(copies_ref.shape[0]):
        copies_ref[i] = rows


def solve(mine_ref, theirs_ref, place_ref, inverse_ref, ritz_ref, mass_ref, stiff_ref, work_ref):
    core = place_ref[0]
    total = work_ref.shape[0]
    chips, g = mine_ref.shape[:2]
    cols = total // 4
    along_x = cols // g
    for side, into in ((0, stiff_ref), (1, mass_ref)):
        chosen = core == side
        for q in range(total // cols):
            for x in range(along_x):
                chip = x * (total // cols) + q
                rows = jnp.where(chosen, mine_ref[chip], theirs_ref[chip])
                rows = jnp.concatenate([rows[:, total - q * cols :], rows[:, : total - q * cols]], 1) if q else rows
                into[q * cols + x * g : q * cols + (x + 1) * g, :] = rows
    gram = mass_ref[...]
    on = lax.broadcasted_iota(jnp.int32, gram.shape, 0) == lax.broadcasted_iota(jnp.int32, gram.shape, 1)
    diagonal = jnp.where(on, gram, 0.0)
    across = 1.0 / jnp.sqrt(jnp.sum(diagonal, axis=0, keepdims=True))
    down = 1.0 / jnp.sqrt(jnp.sum(diagonal, axis=1, keepdims=True))
    work_ref[...] = gram * across * down
    inverse_factor(work_ref, 64, 16)
    inverse = work_ref[...] * across
    inverse_ref[...] = inverse
    ritz_ref[...] = dot_split(dot_split(inverse, stiff_ref[...], ((1,), (1,))), inverse, ((1,), (1,)))


def participate(targets_in, inverse_ref, place_ref, keep_ref, send_ref, targets_ref):
    core, col, me = place_ref[0], place_ref[1], place_ref[2]
    groups = 4
    cols = inverse_ref.shape[0] // groups
    deep, wide = 8, targets_in.shape[0] // 8
    t = targets_in.shape[1] // 2
    for x in range(wide):
        for tile in range(2):
            rows = [targets_in[z * wide + x, tile * t : (tile + 1) * t] for z in range(deep)]
            targets_ref[x * deep * t : (x + 1) * deep * t, lanes_of(tile)] = jnp.concatenate(rows, 0)
    rows = inverse_ref[pl.ds(pl.multiple_of(me // 2 * 8, 8), 8), :]
    part = dot_split(turned(rows, lax.rem(groups - col, groups), cols), targets_ref[...], ((1,), (1,)))
    keep_ref[...] = jnp.where(core == 0, part[:4], part[4:])
    send_ref[...] = jnp.where(core == 0, part[4:], part[:4])


def combine(field_ref, own_ref, three_ref, two_low_ref, two_high_ref, one_ref, coef_ref, inverse_ref, place_ref, modes_ref):
    col = place_ref[1]
    cols = field_ref.shape[0]
    groups = inverse_ref.shape[0] // cols
    width_y = field_ref.shape[1] // WIDTH
    norm = jnp.float32(np.sqrt(np.float32(64 * width_y * WIDTH)))
    back = lax.rem(groups - col, groups)
    weights = turned(inverse_ref[rows_of(col, cols), :], back, cols)
    block = weights[:, :cols].astype(BF16)
    high, low = split(weights)
    held = (own_ref, three_ref, two_low_ref, two_high_ref, one_ref)
    for y in range(width_y):
        at = lanes_of(y)
        everything = jnp.concatenate([ref[:, at] for ref in held], 0)
        mass = jnp.concatenate([coef_ref[8 * MS : 8 * MS + 8, at]] * (cols // 8), axis=0)
        light = jnp.concatenate([coef_ref[8 * MI : 8 * MI + 8, at]] * (cols // 8), axis=0)
        rest = (field_ref[:, at] * mass - own_ref[:, at].astype(F32)).astype(BF16)
        result = (
            jnp.dot(high, everything, preferred_element_type=F32)
            + jnp.dot(low, everything, preferred_element_type=F32)
            + jnp.dot(block, rest, preferred_element_type=F32)
        )
        modes_ref[pl.ds(y, cols, stride=width_y), :] = result * light * norm


def local(start_block, node_mass, material_ids, moduli_table, influence):
    cols, _, width_y, width_z = start_block.shape
    lanes = width_y * width_z
    doms, groups = lax.axis_size("dom"), lax.axis_size("col")
    total_cols = cols * groups
    me, col = lax.axis_index("dom"), lax.axis_index("col")
    core = me % 2
    pair = [(i, i ^ 1) for i in range(doms)]
    across = [(i, i + 1 if i % 2 else i - 1) for i in range(1, doms - 1)]
    wide, deep = 4, 8
    place_of = np.arange(doms).reshape(deep, wide, 2)
    plane_groups = [place_of[:, :, c].reshape(-1).tolist() for c in range(2)]
    x_groups = [place_of[z, :, c].tolist() for z in range(deep) for c in range(2)]
    z_groups = [place_of[:, x, c].tolist() for x in range(wide) for c in range(2)]
    chip_of = place_of[..., None] * groups + np.arange(groups)
    chip_groups = [chip_of[z, :, c].reshape(-1).tolist() for z in range(deep) for c in range(2)]

    def exchange(payload):
        near = lax.ppermute(payload, "dom", pair)
        return near, lax.ppermute(payload, "dom", across)

    def col_ring(step):
        return [(i, (i + step) % groups) for i in range(groups)]

    place = jnp.stack([core, col, me]).astype(jnp.int32)
    ids = material_ids.reshape(width_y, width_z)
    mass = node_mass.reshape(width_y, width_z)
    targets = influence.reshape(influence.shape[0], lanes)

    field, pay, least, own = pl.pallas_call(
        prepare,
        out_shape=(
            shape(cols, lanes),
            shape(cols + 16, lanes, BF16),
            jax.ShapeDtypeStruct((doms, 1, WIDTH), F32),
            shape(24, lanes),
        ),
        in_specs=[SMEM] + [pl.BlockSpec(memory_space=pltpu.HBM)] * 3,
        out_specs=(VMEM,) * 4,
        scratch_shapes=[
            pltpu.VMEM((cols * width_y, width_z), F32),
            pltpu.VMEM((width_y, width_z), jnp.int32),
            pltpu.VMEM((width_y, width_z), F32),
            pltpu.SemaphoreType.DMA((3,)),
        ],
        compiler_params=PARAMS,
    )(moduli_table, start_block.reshape(cols * width_y, width_z), ids, mass)
    near, far = exchange(pay)
    least = lax.all_to_all(least, "dom", 0, 0, tiled=True)

    current, pay, coef, shift = pl.pallas_call(
        first_step,
        out_shape=(shape(cols, lanes), shape(cols, lanes, BF16), shape(80, lanes), shape(8, WIDTH)),
        in_specs=[VMEM] * 5 + [SMEM],
        out_specs=(VMEM,) * 4,
        compiler_params=PARAMS,
    )(far, near, field, own, least, place)
    previous = field
    for step in range(DEGREE - 1):
        last = step == DEGREE - 2
        near, far = exchange(pay)
        outs = pl.pallas_call(
            functools.partial(later_step, last),
            out_shape=(shape(cols, lanes),) + (shape(cols, lanes, BF16),) * (2 if last else 1),
            in_specs=[VMEM] * 6,
            out_specs=(VMEM,) * (3 if last else 2),
            compiler_params=PARAMS,
        )(far, near, current, previous, coef, shift)
        previous, current, pay = current, outs[0], outs[1]
    heavy = outs[2]
    near, far = exchange(pay)
    one, three = lax.ppermute(heavy, "col", col_ring(1)), lax.ppermute(heavy, "col", col_ring(3))
    two_low = lax.ppermute(one[: cols // 2], "col", col_ring(1))
    two_high = lax.ppermute(three[cols // 2 :], "col", col_ring(3))
    half = targets.shape[0] // 2
    t_rows, g_rows = half // wide, cols // wide
    chunk = jax.ShapeDtypeStruct((wide, t_rows + g_rows, total_cols), F32)
    parts = jax.ShapeDtypeStruct((2, cols, lanes), BF16)
    keep, send, high, low = pl.pallas_call(
        products,
        out_shape=(chunk, chunk, parts, parts),
        in_specs=[VMEM] * 8 + [SMEM],
        out_specs=(VMEM,) * 4,
        scratch_shapes=[pltpu.VMEM((total_cols, lanes), BF16)],
        compiler_params=PARAMS,
    )(far, near, one, three, current, coef, heavy, targets, place)
    keep, send = pl.pallas_call(
        opposite,
        out_shape=(chunk, chunk),
        in_specs=[VMEM] * 7 + [SMEM],
        out_specs=(VMEM,) * 2,
        input_output_aliases={0: 0, 1: 1},
        compiler_params=PARAMS,
    )(keep, send, high, low, two_low, two_high, targets, place)

    summed = keep + lax.ppermute(send, "dom", pair)
    summed = lax.all_to_all(summed, "dom", 0, 0, tiled=True, axis_index_groups=x_groups)
    summed = pl.pallas_call(
        along_z,
        out_shape=jax.ShapeDtypeStruct((deep, 2 * g_rows, total_cols), F32),
        in_specs=[VMEM],
        out_specs=VMEM,
        compiler_params=PARAMS,
    )(summed)
    summed = lax.all_to_all(summed, "dom", 0, 0, tiled=True, axis_index_groups=z_groups)
    few = t_rows // deep
    target, gram = pl.pallas_call(
        along_chips,
        out_shape=(
            shape(2 * few, WIDTH),
            jax.ShapeDtypeStruct((wide * groups, g_rows, total_cols), F32),
        ),
        in_specs=[VMEM],
        out_specs=(VMEM,) * 2,
        compiler_params=PARAMS,
    )(summed)
    mine = lax.all_to_all(gram, ("dom", "col"), 0, 0, tiled=True, axis_index_groups=chip_groups)
    theirs = lax.ppermute(mine, "dom", pair)
    target = pl.pallas_call(
        for_all,
        out_shape=jax.ShapeDtypeStruct((deep * wide, 2 * few, WIDTH), F32),
        in_specs=[VMEM] * 2,
        out_specs=VMEM,
        compiler_params=PARAMS,
    )(target, mine)
    target = lax.all_to_all(target, "dom", 0, 0, tiled=True, axis_index_groups=plane_groups)
    inverse, ritz_matrix = pl.pallas_call(
        solve,
        out_shape=(shape(total_cols, total_cols),) * 2,
        in_specs=[VMEM] * 2 + [SMEM],
        out_specs=(VMEM,) * 2,
        scratch_shapes=[pltpu.VMEM((total_cols, total_cols), F32)] * 3,
        compiler_params=PARAMS,
    )(mine, theirs, place)
    part_rows = total_cols // doms
    kept, sent = pl.pallas_call(
        participate,
        out_shape=(shape(part_rows, half),) * 2,
        in_specs=[VMEM] * 2 + [SMEM],
        out_specs=(VMEM,) * 2,
        scratch_shapes=[pltpu.VMEM((half, total_cols), F32)],
        compiler_params=PARAMS,
    )(target, inverse, place)
    got = lax.ppermute(sent, "dom", pair)
    modes = pl.pallas_call(
        combine,
        out_shape=shape(cols * width_y, width_z),
        in_specs=[VMEM] * 8 + [SMEM],
        out_specs=VMEM,
        compiler_params=PARAMS,
    )(current, heavy, three, two_low, two_high, one, coef, inverse, place)
    first = core == 0
    participation = jnp.concatenate([jnp.where(first, kept, got), jnp.where(first, got, kept)], 1)
    return (modes.reshape(start_block.shape), ritz_matrix, participation)


def solution(mesh):
    placed = (
        P("col", "dom", None, None),
        P("dom", None, None),
        P("dom", None, None),
        P(),
        P("col", "dom", None, None),
    )
    return jax.shard_map(
        local,
        mesh=mesh,
        in_specs=placed,
        out_specs=(P("col", "dom", None, None), P(), P("dom", "col")),
        check_vma=False,
    )
```

```python
import functools

import jax
import jax.numpy as jnp
import numpy as np
from jax import lax
from jax.experimental import pallas as pl
from jax.experimental.pallas import tpu as pltpu
from jax.sharding import PartitionSpec as P

DEGREE = 4
LOW_RATIO = 0.02
F32, BF16 = jnp.float32, jnp.bfloat16
VMEM = pl.BlockSpec(memory_space=pltpu.VMEM)
SMEM = pl.BlockSpec(memory_space=pltpu.SMEM)
WIDTH = 128
PARAMS = pltpu.CompilerParams(vmem_limit_bytes=24 * 1024 * 1024)
H4, HZ, HZ4, E, EZ, G, GZ, AM, MI, MS = range(10)


def shape(rows, lanes, dtype=F32):
    return jax.ShapeDtypeStruct((rows, lanes), dtype)


def lanes_of(y):
    return slice(y * WIDTH, (y + 1) * WIDTH)


def rows_of(group, size=16):
    return pl.ds(pl.multiple_of(group * size, size), size)


def twice(c):
    return jnp.concatenate([c, c], axis=0)


def stiffness_rows(width_y, u_at, v_at, w_at, coef):
    def with_roll(x):
        return x, pltpu.roll(x, WIDTH - 1, 1)

    u0, u1 = with_roll(u_at(0))
    v0, v1 = with_roll(v_at(0))
    w0, w1 = with_roll(w_at(0))
    kept = kept_z = None
    for y in range(width_y):
        c = functools.partial(coef, y)
        h4, hz, hz4 = c(H4), c(HZ), c(HZ4)
        ez, gz = c(EZ), c(GZ)
        p00 = ez * v0 + gz * w0
        p01 = ez * v1 + gz * w1
        if y + 1 < width_y:
            e, g = c(E), c(G)
            n0, n1 = with_roll(u_at(y + 1))
            x0, x1 = with_roll(v_at(y + 1))
            z0, z1 = with_roll(w_at(y + 1))
            p10 = ez * x0 + gz * z0
            p11 = ez * x1 + gz * z1
            q00 = e * v0 + g * w0
            q10 = e * x0 + g * z0
            side, other = p01 + p11, p00 + p10
            r00 = h4 * u0 - hz * n1 - q10 - side
            r10 = h4 * n0 - hz * u1 - q00 - side
            r01 = hz4 * u1 - hz * n0 - other - p11
            r11 = hz4 * n1 - hz * u0 - other - p01
        else:
            r00 = h4 * u0 - p01
            r01 = hz4 * u1 - p00
        here = r00 if kept is None else r00 + kept
        moved = r01 if kept_z is None else r01 + kept_z
        yield y, u0, here + pltpu.roll(moved, 1, 1)
        if y + 1 < width_y:
            kept, kept_z = r10, r11
            u0, u1, v0, v1, w0, w1 = n0, n1, x0, x1, z0, z1


def prepare(table_ref, start_hbm, ids_hbm, mass_hbm, field_ref, pay_ref, least_ref, own_ref, start_ref, ids_ref, mass_ref, sems):
    copies = [
        pltpu.make_async_copy(source, target, sems.at[i])
        for i, (source, target) in enumerate(((start_hbm, start_ref), (ids_hbm, ids_ref), (mass_hbm, mass_ref)))
    ]
    for copy in copies:
        copy.start()
    width_y = ids_ref.shape[0]
    cols = field_ref.shape[0]
    materials = table_ref.shape[0]
    top = table_ref[0]
    for k in range(1, materials):
        top = jnp.maximum(top, table_ref[k])
    own_ref[16:, :] = jnp.broadcast_to(top, (8, own_ref.shape[1]))
    copies[1].wait()
    copies[2].wait()
    ids, mass = ids_ref[...], mass_ref[...]
    least = jnp.min(jnp.min(mass, axis=0, keepdims=True), axis=1, keepdims=True)
    least_ref[...] = jnp.broadcast_to(least[None], least_ref.shape)
    moduli = jnp.zeros(ids.shape, F32)
    for k in range(materials):
        moduli = jnp.where(ids == k, table_ref[k], moduli)
    moduli = moduli / 12.0
    high = moduli.astype(BF16).astype(F32)
    middle = (moduli - high).astype(BF16).astype(F32)
    low = moduli - high - middle
    pad = jnp.zeros((13, WIDTH), F32)
    for y in range(width_y):
        at = lanes_of(y)
        own_ref[:8, at] = jnp.broadcast_to(moduli[y : y + 1], (8, WIDTH))
        own_ref[8:16, at] = jnp.broadcast_to(mass[y : y + 1], (8, WIDTH))
        parts = jnp.concatenate([high[y : y + 1], middle[y : y + 1], low[y : y + 1], pad], 0)
        pay_ref[cols:, at] = parts.astype(BF16)
    copies[0].wait()
    for y in range(width_y):
        plane = start_ref[pl.ds(y, cols, stride=width_y), :]
        field_ref[:, lanes_of(y)] = plane
        pay_ref[:cols, lanes_of(y)] = plane.astype(BF16)


def first_step(far_ref, near_ref, field_ref, own_ref, least_ref, place_ref, out_ref, pay_ref, coef_ref, shift_ref):
    cols = field_ref.shape[0]
    width_y = field_ref.shape[1] // WIDTH
    least = jnp.min(jnp.min(least_ref[...], axis=0), axis=1, keepdims=True)
    upper = 16.0 / 3.0 * own_ref[16:, :WIDTH] / least
    lower = LOW_RATIO * upper
    half = (upper - lower) / 2.0
    shift = (upper + lower) / 2.0 / half
    shift_ref[...] = shift
    inner = lax.broadcasted_iota(jnp.int32, (8, WIDTH), 1) < WIDTH - 1
    first = place_ref[0] == 0
    for y in range(width_y):
        at = lanes_of(y)
        own, mass = own_ref[:8, at], own_ref[8:16, at]
        parts = jnp.where(first, far_ref[cols:, at].astype(F32), near_ref[cols:, at].astype(F32))
        below = jnp.broadcast_to(parts[0:1] + parts[1:2] + parts[2:3], (8, WIDTH))
        near, far = jnp.where(first, own, below), jnp.where(first, below, own)
        both = near + far
        both_z = jnp.where(inner, both, 0.0)
        values = {
            H4: 4.0 * both,
            HZ: both_z,
            HZ4: 4.0 * both_z,
            E: near,
            EZ: jnp.where(inner, near, 0.0),
            G: far,
            GZ: jnp.where(inner, far, 0.0),
            AM: 1.0 / (mass * half),
            MI: 1.0 / mass,
            MS: mass,
        }
        for place, value in values.items():
            coef_ref[8 * place : 8 * place + 8, at] = value

    def coef(y, place):
        return twice(coef_ref[8 * place : 8 * place + 8, lanes_of(y)])

    def group(i, carry):
        at = rows_of(i)
        rows = stiffness_rows(
            width_y,
            lambda y: field_ref[at, lanes_of(y)],
            lambda y: near_ref[at, lanes_of(y)].astype(F32),
            lambda y: far_ref[at, lanes_of(y)].astype(F32),
            coef,
        )
        shift2 = twice(shift)
        for y, u, forces in rows:
            result = forces * coef(y, AM) - shift2 * u
            out_ref[at, lanes_of(y)] = result
            pay_ref[at, lanes_of(y)] = result.astype(BF16)
        return carry

    lax.fori_loop(0, cols // 16, group, 0)


def later_step(last, far_ref, near_ref, field_ref, before_ref, coef_ref, shift_ref, target_ref, out_ref, pay_ref, *heavy_ref):
    cols = field_ref.shape[0]
    width_y = field_ref.shape[1] // WIDTH

    def coef(y, place):
        return twice(coef_ref[8 * place : 8 * place + 8, lanes_of(y)])

    def group(i, carry):
        at = rows_of(i)
        rows = stiffness_rows(
            width_y,
            lambda y: field_ref[at, lanes_of(y)],
            lambda y: near_ref[at, lanes_of(y)].astype(F32),
            lambda y: far_ref[at, lanes_of(y)].astype(F32),
            coef,
        )
        shift2 = twice(shift_ref[...])
        for y, u, forces in rows:
            result = 2.0 * (forces * coef(y, AM) - shift2 * u) - before_ref[at, lanes_of(y)]
            out_ref[at, lanes_of(y)] = result
            pay_ref[at, lanes_of(y)] = result.astype(BF16)
            if last:
                heavy_ref[0][at, lanes_of(y)] = (result * coef(y, MS)).astype(BF16)
        return carry

    lax.fori_loop(0, cols // 16, group, 0)


def dot_nt(a, b):
    return lax.dot_general(a, b, (((1,), (1,)), ((), ())), preferred_element_type=F32)


def spread(ref, lanes, targets, gram):
    parts = ref.shape[0]
    t, g = targets.shape[0] // parts, gram.shape[0] // parts
    for x in range(parts):
        ref[x, :t, lanes] = targets[x * t : (x + 1) * t]
        ref[x, t:, lanes] = gram[x * g : (x + 1) * g]


def halves(x):
    high = x.astype(BF16)
    return high, (x - high.astype(F32)).astype(BF16)


def early(field_ref, own_ref, one_ref, three_ref, target_ref, place_ref, keep_ref, send_ref, all_ref):
    cols = field_ref.shape[0]
    core = place_ref[0]
    all_ref[:cols] = own_ref[...]
    all_ref[cols : 2 * cols] = three_ref[...]
    all_ref[2 * cols : 3 * cols] = jnp.zeros((cols, all_ref.shape[1]), BF16)
    all_ref[3 * cols :] = one_ref[...]
    everything = all_ref[...]
    high, low = halves(field_ref[...])
    gram = dot_nt(high, everything) + dot_nt(low, everything)
    half = target_ref.shape[0] // 2
    for side, ref in ((core, keep_ref), (1 - core, send_ref)):
        spread(ref, slice(None), dot_nt(target_ref[rows_of(side, half), :], everything), gram)


def stiff_rows(core, stiff, lanes, keep_ref, send_ref):
    parts = keep_ref.shape[0]
    g = stiff.shape[0] // parts
    t = keep_ref.shape[1] - g

    def put(ref):
        for x in range(parts):
            ref[x, t:, lanes] = stiff[x * g : (x + 1) * g]

    pl.when(core == 0)(lambda: put(keep_ref))
    pl.when(core != 0)(lambda: put(send_ref))


def middle(keep_in, send_in, far_ref, near_ref, field_ref, coef_ref, own_ref, one_ref, three_ref, place_ref, keep_ref, send_ref, high_ref, low_ref, all_ref):
    cols = field_ref.shape[0]
    width_y = field_ref.shape[1] // WIDTH

    def coef(y, place):
        return twice(coef_ref[8 * place : 8 * place + 8, lanes_of(y)])

    def group(i, carry):
        at = rows_of(i)
        rows = stiffness_rows(
            width_y,
            lambda y: field_ref[at, lanes_of(y)],
            lambda y: near_ref[at, lanes_of(y)].astype(F32),
            lambda y: far_ref[at, lanes_of(y)].astype(F32),
            coef,
        )
        for y, u, forces in rows:
            high_ref[at, lanes_of(y)], low_ref[at, lanes_of(y)] = halves(forces * coef(y, MI))
        return carry

    lax.fori_loop(0, cols // 16, group, 0)
    all_ref[:cols] = own_ref[...]
    all_ref[cols : 2 * cols] = three_ref[...]
    all_ref[2 * cols : 3 * cols] = jnp.zeros((cols, all_ref.shape[1]), BF16)
    all_ref[3 * cols :] = one_ref[...]
    everything = all_ref[...]
    stiff = dot_nt(high_ref[...], everything) + dot_nt(low_ref[...], everything)
    stiff_rows(place_ref[0], stiff, slice(None), keep_ref, send_ref)


def late(keep_in, send_in, two_low_ref, two_high_ref, field_ref, high_ref, low_ref, target_ref, place_ref, keep_ref, send_ref):
    cols = field_ref.shape[0]
    core = place_ref[0]
    two = jnp.concatenate([two_low_ref[...], two_high_ref[...]], 0)
    stiff = dot_nt(high_ref[...], two) + dot_nt(low_ref[...], two)
    high, low = halves(field_ref[...])
    heavy = dot_nt(high, two) + dot_nt(low, two)
    half = target_ref.shape[0] // 2
    lanes = slice(2 * cols, 3 * cols)
    for side, ref in ((core, keep_ref), (1 - core, send_ref)):
        spread(ref, lanes, dot_nt(target_ref[rows_of(side, half), :], two), heavy)
    stiff_rows(core, stiff, lanes, keep_ref, send_ref)


def turned(x, steps, cols):
    groups = x.shape[1] // cols

    def by(k):
        return jnp.concatenate([x[:, (groups - k) * cols :], x[:, : (groups - k) * cols]], 1)

    result = x
    for k in range(1, groups):
        result = jnp.where(steps == k, by(k), result)
    return result


def split(x):
    high = x.astype(BF16)
    return high, (x - high.astype(F32)).astype(BF16)


def dot_split(a, b, dims):
    (ah, al), (bh, bl) = split(a), split(b)
    dot = functools.partial(lax.dot_general, dimension_numbers=(dims, ((), ())), preferred_element_type=F32)
    return dot(ah, bh) + (dot(ah, bl) + dot(al, bh))


def inverse_factor(work_ref, panel, few):
    n = work_ref.shape[0]
    tiles, strips = n // WIDTH, panel // 8
    row = lax.broadcasted_iota(jnp.int32, (8, WIDTH), 0)
    lane = lax.broadcasted_iota(jnp.int32, (8, WIDTH), 1)
    for start in range(0, n, panel):
        lines = [[work_ref[start + 8 * r : start + 8 * r + 8, lanes_of(t)] for r in range(strips)] for t in range(tiles)]
        pivots = [jnp.ones((8, WIDTH), F32)] * strips
        for first in range(0, panel, few):
            columns, factors = [], []
            for place in range(start + first, start + first + few):
                tile, inside = divmod(place, WIDTH)
                spread_out = {
                    r: jnp.broadcast_to(lines[tile][r][:, inside : inside + 1], (8, WIDTH)) for r in range(first // 8, strips)
                }
                columns.append(spread_out)
            for k in range(0, few, 2):
                at, i = divmod(first + k, 8)
                left, right = columns[k], columns[k + 1]
                pivot, below = left[at][i : i + 1], left[at][i + 1 : i + 2]
                beside = right[at][i : i + 1]
                minor = pivot * right[at][i + 1 : i + 2] - below * beside
                over = 1.0 / pivot
                slope, scale = below * over, pivot * (1.0 / minor)
                one = {r: left[r] * over for r in range(at, strips)}
                one[at] = jnp.where(row > i, one[at], 0.0)
                two = {r: (right[r] - one[r] * beside) * scale for r in range(at, strips)}
                two[at] = jnp.where(row > i + 1, two[at], 0.0)
                pivots[at] = jnp.where(row == i, pivot, jnp.where(row == i + 1, minor * over, pivots[at]))
                for l in range(k + 2, few):
                    u = columns[l][at][i : i + 1]
                    v = columns[l][at][i + 1 : i + 2] - slope * u
                    for r in range(at, strips):
                        columns[l][r] = columns[l][r] - one[r] * u - two[r] * v
                factors.append((at, i, one, two, slope))
            for k, (at, i, one, two, slope) in enumerate(factors):
                tile, inside = divmod(start + first + 2 * k, WIDTH)
                for t in range(tiles):
                    u, v = lines[t][at][i : i + 1], lines[t][at][i + 1 : i + 2]
                    if t == tile:
                        u = u + jnp.where(lane[:1] == inside, 1.0, 0.0)
                    v = v - slope * u
                    if t == tile:
                        v = v + jnp.where(lane[:1] == inside + 1, 1.0, 0.0)
                    for r in range(at, strips):
                        lines[t][r] = lines[t][r] - one[r] * u - two[r] * v
        factor_rows = [[] for _ in range(tiles)]
        update_rows = [[] for _ in range(tiles)]
        for r in range(strips):
            scale = 1.0 / jnp.sqrt(pivots[r])
            here = row + start + 8 * r
            for t in range(tiles):
                place = lane + t * WIDTH
                full = jnp.where(place == here, scale, lines[t][r] * scale)
                inverse = jnp.where(place <= here, full, 0.0)
                work_ref[start + 8 * r : start + 8 * r + 8, lanes_of(t)] = inverse
                factor_rows[t].append(full)
                update_rows[t].append(jnp.where((place >= start) & (place < start + panel), inverse, full))
        rest = n - start - panel
        if rest:
            factor, rows = (
                jnp.concatenate([jnp.concatenate(strip, 0) for strip in side], 1) for side in (factor_rows, update_rows)
            )
            update = dot_split(factor, rows, ((0,), (0,)))
            for t in range(tiles):
                old = work_ref[start + panel :, lanes_of(t)]
                place = lax.broadcasted_iota(jnp.int32, old.shape, 1) + t * WIDTH
                old = jnp.where((place >= start) & (place < start + panel), 0.0, old)
                work_ref[start + panel :, lanes_of(t)] = old - update[start + panel :, lanes_of(t)]


def along_z(parts_ref, out_ref):
    total = jnp.sum(parts_ref[...], axis=0)
    planes, rows = out_ref.shape[0], out_ref.shape[1] // 2
    g = (total.shape[0] - planes * rows) // (1 - planes)
    t = rows - g
    gram = total[planes * t :]
    for z in range(planes):
        mine = total[z * t : (z + 1) * t]
        out_ref[z, : 2 * t, :] = jnp.concatenate([mine[:, :WIDTH], mine[:, WIDTH:]], 0)
        out_ref[z, 2 * t : 2 * t + g, :] = gram[:, :WIDTH]
        out_ref[z, 2 * t + g :, :] = gram[:, WIDTH:]


def along_chips(parts_ref, target_ref, gram_ref):
    total = jnp.sum(parts_ref[...], axis=0)
    g = gram_ref.shape[1]
    t = target_ref.shape[0]
    target_ref[...] = total[:t]
    for chip in range(gram_ref.shape[0]):
        gram_ref[chip, :, :WIDTH] = total[t : t + g]
        gram_ref[chip, :, WIDTH:] = total[t + g :]


def for_all(rows_ref, earlier_ref, copies_ref):
    rows = rows_ref[...]
    for i in range(copies_ref.shape[0]):
        copies_ref[i] = rows


def solve(mine_ref, theirs_ref, place_ref, inverse_ref, ritz_ref, mass_ref, stiff_ref, work_ref):
    core = place_ref[0]
    total = work_ref.shape[0]
    chips, g = mine_ref.shape[:2]
    cols = total // 4
    along_x = cols // g
    for side, into in ((0, stiff_ref), (1, mass_ref)):
        chosen = core == side
        for q in range(total // cols):
            for x in range(along_x):
                chip = x * (total // cols) + q
                rows = jnp.where(chosen, mine_ref[chip], theirs_ref[chip])
                rows = jnp.concatenate([rows[:, total - q * cols :], rows[:, : total - q * cols]], 1) if q else rows
                into[q * cols + x * g : q * cols + (x + 1) * g, :] = rows
    gram = mass_ref[...]
    on = lax.broadcasted_iota(jnp.int32, gram.shape, 0) == lax.broadcasted_iota(jnp.int32, gram.shape, 1)
    diagonal = jnp.where(on, gram, 0.0)
    across = 1.0 / jnp.sqrt(jnp.sum(diagonal, axis=0, keepdims=True))
    down = 1.0 / jnp.sqrt(jnp.sum(diagonal, axis=1, keepdims=True))
    work_ref[...] = gram * across * down
    inverse_factor(work_ref, 64, 16)
    inverse = work_ref[...] * across
    inverse_ref[...] = inverse
    ritz_ref[...] = dot_split(dot_split(inverse, stiff_ref[...], ((1,), (1,))), inverse, ((1,), (1,)))


def participate(targets_in, inverse_ref, place_ref, keep_ref, send_ref, targets_ref):
    core, col, me = place_ref[0], place_ref[1], place_ref[2]
    groups = 4
    cols = inverse_ref.shape[0] // groups
    deep, wide = 8, targets_in.shape[0] // 8
    t = targets_in.shape[1] // 2
    for x in range(wide):
        for tile in range(2):
            rows = [targets_in[z * wide + x, tile * t : (tile + 1) * t] for z in range(deep)]
            targets_ref[x * deep * t : (x + 1) * deep * t, lanes_of(tile)] = jnp.concatenate(rows, 0)
    rows = inverse_ref[pl.ds(pl.multiple_of(me // 2 * 8, 8), 8), :]
    part = dot_split(turned(rows, lax.rem(groups - col, groups), cols), targets_ref[...], ((1,), (1,)))
    keep_ref[...] = jnp.where(core == 0, part[:4], part[4:])
    send_ref[...] = jnp.where(core == 0, part[4:], part[:4])


def combine(field_ref, own_ref, three_ref, two_low_ref, two_high_ref, one_ref, coef_ref, inverse_ref, place_ref, modes_ref):
    col = place_ref[1]
    cols = field_ref.shape[0]
    groups = inverse_ref.shape[0] // cols
    width_y = field_ref.shape[1] // WIDTH
    norm = jnp.float32(np.sqrt(np.float32(64 * width_y * WIDTH)))
    back = lax.rem(groups - col, groups)
    weights = turned(inverse_ref[rows_of(col, cols), :], back, cols)
    block = weights[:, :cols].astype(BF16)
    high, low = split(weights)
    held = (own_ref, three_ref, two_low_ref, two_high_ref, one_ref)
    for y in range(width_y):
        at = lanes_of(y)
        everything = jnp.concatenate([ref[:, at] for ref in held], 0)
        mass = jnp.concatenate([coef_ref[8 * MS : 8 * MS + 8, at]] * (cols // 8), axis=0)
        light = jnp.concatenate([coef_ref[8 * MI : 8 * MI + 8, at]] * (cols // 8), axis=0)
        rest = (field_ref[:, at] * mass - own_ref[:, at].astype(F32)).astype(BF16)
        result = (
            jnp.dot(high, everything, preferred_element_type=F32)
            + jnp.dot(low, everything, preferred_element_type=F32)
            + jnp.dot(block, rest, preferred_element_type=F32)
        )
        modes_ref[pl.ds(y, cols, stride=width_y), :] = result * light * norm


def local(start_block, node_mass, material_ids, moduli_table, influence):
    cols, _, width_y, width_z = start_block.shape
    lanes = width_y * width_z
    doms, groups = lax.axis_size("dom"), lax.axis_size("col")
    total_cols = cols * groups
    me, col = lax.axis_index("dom"), lax.axis_index("col")
    core = me % 2
    pair = [(i, i ^ 1) for i in range(doms)]
    across = [(i, i + 1 if i % 2 else i - 1) for i in range(1, doms - 1)]
    wide, deep = 4, 8
    place_of = np.arange(doms).reshape(deep, wide, 2)
    plane_groups = [place_of[:, :, c].reshape(-1).tolist() for c in range(2)]
    x_groups = [place_of[z, :, c].tolist() for z in range(deep) for c in range(2)]
    z_groups = [place_of[:, x, c].tolist() for x in range(wide) for c in range(2)]
    chip_of = place_of[..., None] * groups + np.arange(groups)
    chip_groups = [chip_of[z, :, c].reshape(-1).tolist() for z in range(deep) for c in range(2)]

    def exchange(payload):
        near = lax.ppermute(payload, "dom", pair)
        return near, lax.ppermute(payload, "dom", across)

    def col_ring(step):
        return [(i, (i + step) % groups) for i in range(groups)]

    place = jnp.stack([core, col, me]).astype(jnp.int32)
    ids = material_ids.reshape(width_y, width_z)
    mass = node_mass.reshape(width_y, width_z)
    targets = influence.reshape(influence.shape[0], lanes)

    field, pay, least, own = pl.pallas_call(
        prepare,
        out_shape=(
            shape(cols, lanes),
            shape(cols + 16, lanes, BF16),
            jax.ShapeDtypeStruct((doms, 1, WIDTH), F32),
            shape(24, lanes),
        ),
        in_specs=[SMEM] + [pl.BlockSpec(memory_space=pltpu.HBM)] * 3,
        out_specs=(VMEM,) * 4,
        scratch_shapes=[
            pltpu.VMEM((cols * width_y, width_z), F32),
            pltpu.VMEM((width_y, width_z), jnp.int32),
            pltpu.VMEM((width_y, width_z), F32),
            pltpu.SemaphoreType.DMA((3,)),
        ],
        compiler_params=PARAMS,
    )(moduli_table, start_block.reshape(cols * width_y, width_z), ids, mass)
    near, far = exchange(pay)
    least = lax.all_to_all(least, "dom", 0, 0, tiled=True)

    current, pay, coef, shift = pl.pallas_call(
        first_step,
        out_shape=(shape(cols, lanes), shape(cols, lanes, BF16), shape(80, lanes), shape(8, WIDTH)),
        in_specs=[VMEM] * 5 + [SMEM],
        out_specs=(VMEM,) * 4,
        compiler_params=PARAMS,
    )(far, near, field, own, least, place)
    previous = field
    for step in range(DEGREE - 1):
        last = step == DEGREE - 2
        near, far = exchange(pay)
        outs = pl.pallas_call(
            functools.partial(later_step, last),
            out_shape=(shape(cols, lanes),) + (shape(cols, lanes, BF16),) * (2 if last else 1),
            in_specs=[VMEM] * 7,
            out_specs=(VMEM,) * (3 if last else 2),
            compiler_params=PARAMS,
        )(far, near, current, previous, coef, shift, targets if last else shift)
        previous, current, pay = current, outs[0], outs[1]
    heavy = outs[2]
    near, far = exchange(pay)
    one, three = lax.ppermute(heavy, "col", col_ring(1)), lax.ppermute(heavy, "col", col_ring(3))
    two_low = lax.ppermute(one[: cols // 2], "col", col_ring(1))
    two_high = lax.ppermute(three[cols // 2 :], "col", col_ring(3))
    half = targets.shape[0] // 2
    t_rows, g_rows = half // wide, cols // wide
    chunk = jax.ShapeDtypeStruct((wide, t_rows + g_rows, total_cols), F32)
    keep, send = pl.pallas_call(
        early,
        out_shape=(chunk, chunk),
        in_specs=[VMEM] * 5 + [SMEM],
        out_specs=(VMEM,) * 2,
        scratch_shapes=[pltpu.VMEM((total_cols, lanes), BF16)],
        compiler_params=PARAMS,
    )(current, heavy, one, three, targets, place)
    split_field = (shape(cols, lanes, BF16),) * 2
    keep, send, high, low = pl.pallas_call(
        middle,
        out_shape=(chunk, chunk) + split_field,
        in_specs=[VMEM] * 9 + [SMEM],
        out_specs=(VMEM,) * 4,
        scratch_shapes=[pltpu.VMEM((total_cols, lanes), BF16)],
        input_output_aliases={0: 0, 1: 1},
        compiler_params=PARAMS,
    )(keep, send, far, near, current, coef, heavy, one, three, place)
    keep, send = pl.pallas_call(
        late,
        out_shape=(chunk, chunk),
        in_specs=[VMEM] * 8 + [SMEM],
        out_specs=(VMEM,) * 2,
        input_output_aliases={0: 0, 1: 1},
        compiler_params=PARAMS,
    )(keep, send, two_low, two_high, current, high, low, targets, place)

    summed = keep + lax.ppermute(send, "dom", pair)
    summed = lax.all_to_all(summed, "dom", 0, 0, tiled=True, axis_index_groups=x_groups)
    summed = pl.pallas_call(
        along_z,
        out_shape=jax.ShapeDtypeStruct((deep, 2 * (t_rows // deep + g_rows), WIDTH), F32),
        in_specs=[VMEM],
        out_specs=VMEM,
        compiler_params=PARAMS,
    )(summed)
    summed = lax.all_to_all(summed, "dom", 0, 0, tiled=True, axis_index_groups=z_groups)
    few = t_rows // deep
    target, gram = pl.pallas_call(
        along_chips,
        out_shape=(
            shape(2 * few, WIDTH),
            jax.ShapeDtypeStruct((wide * groups, g_rows, total_cols), F32),
        ),
        in_specs=[VMEM],
        out_specs=(VMEM,) * 2,
        compiler_params=PARAMS,
    )(summed)
    mine = lax.all_to_all(gram, ("dom", "col"), 0, 0, tiled=True, axis_index_groups=chip_groups)
    theirs = lax.ppermute(mine, "dom", pair)
    target = pl.pallas_call(
        for_all,
        out_shape=jax.ShapeDtypeStruct((deep * wide, 2 * few, WIDTH), F32),
        in_specs=[VMEM] * 2,
        out_specs=VMEM,
        compiler_params=PARAMS,
    )(target, mine)
    target = lax.all_to_all(target, "dom", 0, 0, tiled=True, axis_index_groups=plane_groups)
    inverse, ritz_matrix = pl.pallas_call(
        solve,
        out_shape=(shape(total_cols, total_cols),) * 2,
        in_specs=[VMEM] * 2 + [SMEM],
        out_specs=(VMEM,) * 2,
        scratch_shapes=[pltpu.VMEM((total_cols, total_cols), F32)] * 3,
        compiler_params=PARAMS,
    )(mine, theirs, place)
    part_rows = total_cols // doms
    kept, sent = pl.pallas_call(
        participate,
        out_shape=(shape(part_rows, half),) * 2,
        in_specs=[VMEM] * 2 + [SMEM],
        out_specs=(VMEM,) * 2,
        scratch_shapes=[pltpu.VMEM((half, total_cols), F32)],
        compiler_params=PARAMS,
    )(target, inverse, place)
    got = lax.ppermute(sent, "dom", pair)
    modes = pl.pallas_call(
        combine,
        out_shape=shape(cols * width_y, width_z),
        in_specs=[VMEM] * 8 + [SMEM],
        out_specs=VMEM,
        compiler_params=PARAMS,
    )(current, heavy, three, two_low, two_high, one, coef, inverse, place)
    first = core == 0
    participation = jnp.concatenate([jnp.where(first, kept, got), jnp.where(first, got, kept)], 1)
    return (modes.reshape(start_block.shape), ritz_matrix, participation)


def solution(mesh):
    placed = (
        P("col", "dom", None, None),
        P("dom", None, None),
        P("dom", None, None),
        P(),
        P("col", "dom", None, None),
    )
    return jax.shard_map(
        local,
        mesh=mesh,
        in_specs=placed,
        out_specs=(P("col", "dom", None, None), P(), P("dom", "col")),
        check_vma=False,
    )
```

```python
import functools

import jax
import jax.numpy as jnp
import numpy as np
from jax import lax
from jax.experimental import pallas as pl
from jax.experimental.pallas import tpu as pltpu
from jax.sharding import PartitionSpec as P

DEGREE = 4
LOW_RATIO = 0.02
F32, BF16 = jnp.float32, jnp.bfloat16
VMEM = pl.BlockSpec(memory_space=pltpu.VMEM)
SMEM = pl.BlockSpec(memory_space=pltpu.SMEM)
WIDTH = 128
PARAMS = pltpu.CompilerParams(vmem_limit_bytes=24 * 1024 * 1024)
H4, HZ, HZ4, E, EZ, G, GZ, MI, MS = range(9)


def shape(rows, lanes, dtype=F32):
    return jax.ShapeDtypeStruct((rows, lanes), dtype)


def lanes_of(y):
    return slice(y * WIDTH, (y + 1) * WIDTH)


def rows_of(group, size=16):
    return pl.ds(pl.multiple_of(group * size, size), size)


def twice(c):
    return jnp.concatenate([c, c], axis=0)


def stiffness_rows(width_y, u_at, v_at, w_at, coef):
    def with_roll(x):
        return x, pltpu.roll(x, WIDTH - 1, 1)

    u0, u1 = with_roll(u_at(0))
    v0, v1 = with_roll(v_at(0))
    w0, w1 = with_roll(w_at(0))
    kept = kept_z = None
    for y in range(width_y):
        c = functools.partial(coef, y)
        h4, hz, hz4 = c(H4), c(HZ), c(HZ4)
        ez, gz = c(EZ), c(GZ)
        p00 = ez * v0 + gz * w0
        p01 = ez * v1 + gz * w1
        if y + 1 < width_y:
            e, g = c(E), c(G)
            n0, n1 = with_roll(u_at(y + 1))
            x0, x1 = with_roll(v_at(y + 1))
            z0, z1 = with_roll(w_at(y + 1))
            p10 = ez * x0 + gz * z0
            p11 = ez * x1 + gz * z1
            q00 = e * v0 + g * w0
            q10 = e * x0 + g * z0
            side, other = p01 + p11, p00 + p10
            r00 = h4 * u0 - hz * n1 - q10 - side
            r10 = h4 * n0 - hz * u1 - q00 - side
            r01 = hz4 * u1 - hz * n0 - other - p11
            r11 = hz4 * n1 - hz * u0 - other - p01
        else:
            r00 = h4 * u0 - p01
            r01 = hz4 * u1 - p00
        here = r00 if kept is None else r00 + kept
        moved = r01 if kept_z is None else r01 + kept_z
        yield y, u0, here + pltpu.roll(moved, 1, 1)
        if y + 1 < width_y:
            kept, kept_z = r10, r11
            u0, u1, v0, v1, w0, w1 = n0, n1, x0, x1, z0, z1


def prepare(start_hbm, mass_hbm, ids_hbm, table_hbm, base_ref, pay_ref, least_ref, start_ref, mass_ref, ids_ref, table_ref, sems):
    pairs = ((mass_hbm, mass_ref), (ids_hbm, ids_ref), (table_hbm, table_ref), (start_hbm, start_ref))
    copies = [pltpu.make_async_copy(source, target, sems.at[i]) for i, (source, target) in enumerate(pairs)]
    for copy in copies:
        copy.start()
    cols = base_ref.shape[0] - 24
    width_y = ids_ref.shape[0]
    for copy in copies[:3]:
        copy.wait()
    mass, ids, table = mass_ref[...], ids_ref[...], table_ref[...]
    base_ref[cols + 16 :, :] = jnp.broadcast_to(jnp.max(table, axis=1, keepdims=True), (8, base_ref.shape[1]))
    least = jnp.min(jnp.min(mass, axis=0, keepdims=True), axis=1, keepdims=True)
    least_ref[...] = jnp.broadcast_to(least[None], least_ref.shape)
    moduli = jnp.zeros(ids.shape, F32)
    for k in range(table.shape[1]):
        moduli = jnp.where(ids == k, table[:, k : k + 1], moduli)
    moduli = moduli / 12.0
    high = moduli.astype(BF16).astype(F32)
    middle = (moduli - high).astype(BF16).astype(F32)
    low = moduli - high - middle
    pad = jnp.zeros((13, WIDTH), F32)
    for y in range(width_y):
        at = lanes_of(y)
        base_ref[cols : cols + 8, at] = jnp.broadcast_to(moduli[y : y + 1], (8, WIDTH))
        base_ref[cols + 8 : cols + 16, at] = jnp.broadcast_to(mass[y : y + 1], (8, WIDTH))
        parts = jnp.concatenate([high[y : y + 1], middle[y : y + 1], low[y : y + 1], pad], 0)
        pay_ref[cols:, at] = parts.astype(BF16)
    copies[3].wait()
    for y in range(width_y):
        plane = start_ref[pl.ds(y, cols, stride=width_y), :]
        base_ref[:cols, lanes_of(y)] = plane
        pay_ref[:cols, lanes_of(y)] = plane.astype(BF16)


def first_forces(far_ref, near_ref, base_ref, place_ref, forces_ref, coef_ref, field_ref, top_ref):
    cols = field_ref.shape[0]
    top_ref[...] = base_ref[cols + 16 :, :WIDTH]
    width_y = field_ref.shape[1] // WIDTH
    inner = lax.broadcasted_iota(jnp.int32, (8, WIDTH), 1) < WIDTH - 1
    first = place_ref[0] == 0
    for y in range(width_y):
        at = lanes_of(y)
        own, mass = base_ref[cols : cols + 8, at], base_ref[cols + 8 : cols + 16, at]
        parts = jnp.where(first, far_ref[cols:, at].astype(F32), near_ref[cols:, at].astype(F32))
        below = jnp.broadcast_to(parts[0:1] + parts[1:2] + parts[2:3], (8, WIDTH))
        near, far = jnp.where(first, own, below), jnp.where(first, below, own)
        both = near + far
        both_z = jnp.where(inner, both, 0.0)
        values = {
            H4: 4.0 * both,
            HZ: both_z,
            HZ4: 4.0 * both_z,
            E: near,
            EZ: jnp.where(inner, near, 0.0),
            G: far,
            GZ: jnp.where(inner, far, 0.0),
            MI: 1.0 / mass,
            MS: mass,
        }
        for place, value in values.items():
            coef_ref[8 * place : 8 * place + 8, at] = value

    def coef(y, place):
        return twice(coef_ref[8 * place : 8 * place + 8, lanes_of(y)])

    def group(i, carry):
        at = rows_of(i)
        rows = stiffness_rows(
            width_y,
            lambda y: base_ref[at, lanes_of(y)],
            lambda y: near_ref[at, lanes_of(y)].astype(F32),
            lambda y: far_ref[at, lanes_of(y)].astype(F32),
            coef,
        )
        for y, u, forces in rows:
            forces_ref[at, lanes_of(y)] = forces
            field_ref[at, lanes_of(y)] = u
        return carry

    lax.fori_loop(0, cols // 16, group, 0)


def first_step(least_ref, forces_ref, field_ref, coef_ref, top_ref, out_ref, pay_ref, scale_ref, shift_ref):
    cols = field_ref.shape[0]
    width_y = field_ref.shape[1] // WIDTH
    least = jnp.min(jnp.min(least_ref[...], axis=0), axis=1, keepdims=True)
    upper = 16.0 / 3.0 * top_ref[...] / least
    lower = LOW_RATIO * upper
    half = (upper - lower) / 2.0
    shift = (upper + lower) / 2.0 / half
    shift_ref[...] = shift
    for y in range(width_y):
        at = lanes_of(y)
        scale = 1.0 / (coef_ref[8 * MS : 8 * MS + 8, at] * half)
        scale_ref[:, at] = scale
        scale, shifts = (jnp.concatenate([x] * (cols // 8), 0) for x in (scale, shift))
        result = forces_ref[:, at] * scale - shifts * field_ref[:, at]
        out_ref[:, at] = result
        pay_ref[:, at] = result.astype(BF16)


def later_step(last, far_ref, near_ref, field_ref, before_ref, coef_ref, scale_ref, shift_ref, target_ref, out_ref, pay_ref, *heavy_ref):
    cols = field_ref.shape[0]
    width_y = field_ref.shape[1] // WIDTH

    def coef(y, place):
        return twice(coef_ref[8 * place : 8 * place + 8, lanes_of(y)])

    def group(i, carry):
        at = rows_of(i)
        rows = stiffness_rows(
            width_y,
            lambda y: field_ref[at, lanes_of(y)],
            lambda y: near_ref[at, lanes_of(y)].astype(F32),
            lambda y: far_ref[at, lanes_of(y)].astype(F32),
            coef,
        )
        shift2 = twice(shift_ref[...])
        for y, u, forces in rows:
            result = 2.0 * (forces * twice(scale_ref[:, lanes_of(y)]) - shift2 * u) - before_ref[at, lanes_of(y)]
            out_ref[at, lanes_of(y)] = result
            pay_ref[at, lanes_of(y)] = result.astype(BF16)
            if last:
                heavy_ref[0][at, lanes_of(y)] = (result * coef(y, MS)).astype(BF16)
        return carry

    lax.fori_loop(0, cols // 16, group, 0)


def dot_nt(a, b):
    return lax.dot_general(a, b, (((1,), (1,)), ((), ())), preferred_element_type=F32)


def spread(ref, lanes, targets, gram):
    parts = ref.shape[0]
    t, g = targets.shape[0] // parts, gram.shape[0] // parts
    for x in range(parts):
        ref[x, :t, lanes] = targets[x * t : (x + 1) * t]
        ref[x, t:, lanes] = gram[x * g : (x + 1) * g]


def halves(x):
    high = x.astype(BF16)
    return high, (x - high.astype(F32)).astype(BF16)


def early(field_ref, own_ref, one_ref, three_ref, target_ref, place_ref, keep_ref, send_ref, all_ref):
    cols = field_ref.shape[0]
    core = place_ref[0]
    all_ref[:cols] = own_ref[...]
    all_ref[cols : 2 * cols] = three_ref[...]
    all_ref[2 * cols : 3 * cols] = jnp.zeros((cols, all_ref.shape[1]), BF16)
    all_ref[3 * cols :] = one_ref[...]
    everything = all_ref[...]
    high, low = halves(field_ref[...])
    gram = dot_nt(high, everything) + dot_nt(low, everything)
    half = target_ref.shape[0] // 2
    for side, ref in ((core, keep_ref), (1 - core, send_ref)):
        spread(ref, slice(None), dot_nt(target_ref[rows_of(side, half), :], everything), gram)


def stiff_rows(core, stiff, lanes, keep_ref, send_ref):
    parts = keep_ref.shape[0]
    g = stiff.shape[0] // parts
    t = keep_ref.shape[1] - g

    def put(ref):
        for x in range(parts):
            ref[x, t:, lanes] = stiff[x * g : (x + 1) * g]

    pl.when(core == 0)(lambda: put(keep_ref))
    pl.when(core != 0)(lambda: put(send_ref))


def middle(keep_in, send_in, far_ref, near_ref, field_ref, coef_ref, own_ref, one_ref, three_ref, place_ref, keep_ref, send_ref, high_ref, low_ref, all_ref):
    cols = field_ref.shape[0]
    width_y = field_ref.shape[1] // WIDTH

    def coef(y, place):
        return twice(coef_ref[8 * place : 8 * place + 8, lanes_of(y)])

    def group(i, carry):
        at = rows_of(i)
        rows = stiffness_rows(
            width_y,
            lambda y: field_ref[at, lanes_of(y)],
            lambda y: near_ref[at, lanes_of(y)].astype(F32),
            lambda y: far_ref[at, lanes_of(y)].astype(F32),
            coef,
        )
        for y, u, forces in rows:
            high_ref[at, lanes_of(y)], low_ref[at, lanes_of(y)] = halves(forces * coef(y, MI))
        return carry

    lax.fori_loop(0, cols // 16, group, 0)
    all_ref[:cols] = own_ref[...]
    all_ref[cols : 2 * cols] = three_ref[...]
    all_ref[2 * cols : 3 * cols] = jnp.zeros((cols, all_ref.shape[1]), BF16)
    all_ref[3 * cols :] = one_ref[...]
    everything = all_ref[...]
    stiff = dot_nt(high_ref[...], everything) + dot_nt(low_ref[...], everything)
    stiff_rows(place_ref[0], stiff, slice(None), keep_ref, send_ref)


def late(keep_in, send_in, two_low_ref, two_high_ref, field_ref, high_ref, low_ref, target_ref, place_ref, keep_ref, send_ref):
    cols = field_ref.shape[0]
    core = place_ref[0]
    two = jnp.concatenate([two_low_ref[...], two_high_ref[...]], 0)
    stiff = dot_nt(high_ref[...], two) + dot_nt(low_ref[...], two)
    high, low = halves(field_ref[...])
    heavy = dot_nt(high, two) + dot_nt(low, two)
    half = target_ref.shape[0] // 2
    lanes = slice(2 * cols, 3 * cols)
    for side, ref in ((core, keep_ref), (1 - core, send_ref)):
        spread(ref, lanes, dot_nt(target_ref[rows_of(side, half), :], two), heavy)
    stiff_rows(core, stiff, lanes, keep_ref, send_ref)


def turned(x, steps, cols):
    groups = x.shape[1] // cols

    def by(k):
        return jnp.concatenate([x[:, (groups - k) * cols :], x[:, : (groups - k) * cols]], 1)

    result = x
    for k in range(1, groups):
        result = jnp.where(steps == k, by(k), result)
    return result


def split(x):
    high = x.astype(BF16)
    return high, (x - high.astype(F32)).astype(BF16)


def dot_split(a, b, dims):
    (ah, al), (bh, bl) = split(a), split(b)
    dot = functools.partial(lax.dot_general, dimension_numbers=(dims, ((), ())), preferred_element_type=F32)
    return dot(ah, bh) + (dot(ah, bl) + dot(al, bh))


def inverse_factor(work_ref, panel, few):
    n = work_ref.shape[0]
    tiles, strips = n // WIDTH, panel // 8
    row = lax.broadcasted_iota(jnp.int32, (8, WIDTH), 0)
    lane = lax.broadcasted_iota(jnp.int32, (8, WIDTH), 1)
    for start in range(0, n, panel):
        lines = [[work_ref[start + 8 * r : start + 8 * r + 8, lanes_of(t)] for r in range(strips)] for t in range(tiles)]
        pivots = [jnp.ones((8, WIDTH), F32)] * strips
        for first in range(0, panel, few):
            columns, factors = [], []
            for place in range(start + first, start + first + few):
                tile, inside = divmod(place, WIDTH)
                spread_out = {
                    r: jnp.broadcast_to(lines[tile][r][:, inside : inside + 1], (8, WIDTH)) for r in range(first // 8, strips)
                }
                columns.append(spread_out)
            for k in range(0, few, 2):
                at, i = divmod(first + k, 8)
                left, right = columns[k], columns[k + 1]
                pivot, below = left[at][i : i + 1], left[at][i + 1 : i + 2]
                beside = right[at][i : i + 1]
                minor = pivot * right[at][i + 1 : i + 2] - below * beside
                over = 1.0 / pivot
                slope, scale = below * over, pivot * (1.0 / minor)
                one = {r: left[r] * over for r in range(at, strips)}
                one[at] = jnp.where(row > i, one[at], 0.0)
                two = {r: (right[r] - one[r] * beside) * scale for r in range(at, strips)}
                two[at] = jnp.where(row > i + 1, two[at], 0.0)
                pivots[at] = jnp.where(row == i, pivot, jnp.where(row == i + 1, minor * over, pivots[at]))
                for l in range(k + 2, few):
                    u = columns[l][at][i : i + 1]
                    v = columns[l][at][i + 1 : i + 2] - slope * u
                    for r in range(at, strips):
                        columns[l][r] = columns[l][r] - one[r] * u - two[r] * v
                factors.append((at, i, one, two, slope))
            for k, (at, i, one, two, slope) in enumerate(factors):
                tile, inside = divmod(start + first + 2 * k, WIDTH)
                for t in range(tiles):
                    u, v = lines[t][at][i : i + 1], lines[t][at][i + 1 : i + 2]
                    if t == tile:
                        u = u + jnp.where(lane[:1] == inside, 1.0, 0.0)
                    v = v - slope * u
                    if t == tile:
                        v = v + jnp.where(lane[:1] == inside + 1, 1.0, 0.0)
                    for r in range(at, strips):
                        lines[t][r] = lines[t][r] - one[r] * u - two[r] * v
        factor_rows = [[] for _ in range(tiles)]
        update_rows = [[] for _ in range(tiles)]
        for r in range(strips):
            scale = 1.0 / jnp.sqrt(pivots[r])
            here = row + start + 8 * r
            for t in range(tiles):
                place = lane + t * WIDTH
                full = jnp.where(place == here, scale, lines[t][r] * scale)
                inverse = jnp.where(place <= here, full, 0.0)
                work_ref[start + 8 * r : start + 8 * r + 8, lanes_of(t)] = inverse
                factor_rows[t].append(full)
                update_rows[t].append(jnp.where((place >= start) & (place < start + panel), inverse, full))
        rest = n - start - panel
        if rest:
            factor, rows = (
                jnp.concatenate([jnp.concatenate(strip, 0) for strip in side], 1) for side in (factor_rows, update_rows)
            )
            update = dot_split(factor, rows, ((0,), (0,)))
            for t in range(tiles):
                old = work_ref[start + panel :, lanes_of(t)]
                place = lax.broadcasted_iota(jnp.int32, old.shape, 1) + t * WIDTH
                old = jnp.where((place >= start) & (place < start + panel), 0.0, old)
                work_ref[start + panel :, lanes_of(t)] = old - update[start + panel :, lanes_of(t)]


def along_z(parts_ref, out_ref):
    total = jnp.sum(parts_ref[...], axis=0)
    planes, rows = out_ref.shape[0], out_ref.shape[1] // 2
    g = (total.shape[0] - planes * rows) // (1 - planes)
    t = rows - g
    gram = total[planes * t :]
    for z in range(planes):
        mine = total[z * t : (z + 1) * t]
        out_ref[z, : 2 * t, :] = jnp.concatenate([mine[:, :WIDTH], mine[:, WIDTH:]], 0)
        out_ref[z, 2 * t : 2 * t + g, :] = gram[:, :WIDTH]
        out_ref[z, 2 * t + g :, :] = gram[:, WIDTH:]


def along_chips(parts_ref, target_ref, gram_ref):
    total = jnp.sum(parts_ref[...], axis=0)
    g = gram_ref.shape[1]
    t = target_ref.shape[1]
    for plane in range(target_ref.shape[0]):
        target_ref[plane] = total[:t]
    for chip in range(gram_ref.shape[0]):
        gram_ref[chip, :, :WIDTH] = total[t : t + g]
        gram_ref[chip, :, WIDTH:] = total[t + g :]


def solve(mine_ref, theirs_ref, place_ref, inverse_ref, ritz_ref, mass_ref, stiff_ref, work_ref):
    core = place_ref[0]
    total = work_ref.shape[0]
    chips, g = mine_ref.shape[:2]
    cols = total // 4
    along_x = cols // g
    for side, into in ((0, stiff_ref), (1, mass_ref)):
        chosen = core == side
        for q in range(total // cols):
            for x in range(along_x):
                chip = x * (total // cols) + q
                rows = jnp.where(chosen, mine_ref[chip], theirs_ref[chip])
                rows = jnp.concatenate([rows[:, total - q * cols :], rows[:, : total - q * cols]], 1) if q else rows
                into[q * cols + x * g : q * cols + (x + 1) * g, :] = rows
    gram = mass_ref[...]
    on = lax.broadcasted_iota(jnp.int32, gram.shape, 0) == lax.broadcasted_iota(jnp.int32, gram.shape, 1)
    diagonal = jnp.where(on, gram, 0.0)
    across = 1.0 / jnp.sqrt(jnp.sum(diagonal, axis=0, keepdims=True))
    down = 1.0 / jnp.sqrt(jnp.sum(diagonal, axis=1, keepdims=True))
    work_ref[...] = gram * across * down
    inverse_factor(work_ref, 64, 16)
    inverse = work_ref[...] * across
    inverse_ref[...] = inverse
    ritz_ref[...] = dot_split(dot_split(inverse, stiff_ref[...], ((1,), (1,))), inverse, ((1,), (1,)))


def participate(targets_in, inverse_ref, place_ref, keep_ref, send_ref, targets_ref):
    core, col, me = place_ref[0], place_ref[1], place_ref[2]
    groups = 4
    cols = inverse_ref.shape[0] // groups
    deep, wide = 8, targets_in.shape[0] // 8
    t = targets_in.shape[1] // 2
    for x in range(wide):
        for tile in range(2):
            rows = [targets_in[z * wide + x, tile * t : (tile + 1) * t] for z in range(deep)]
            targets_ref[x * deep * t : (x + 1) * deep * t, lanes_of(tile)] = jnp.concatenate(rows, 0)
    rows = inverse_ref[pl.ds(pl.multiple_of(me // 2 * 8, 8), 8), :]
    part = dot_split(turned(rows, lax.rem(groups - col, groups), cols), targets_ref[...], ((1,), (1,)))
    keep_ref[...] = jnp.where(core == 0, part[:4], part[4:])
    send_ref[...] = jnp.where(core == 0, part[4:], part[:4])


def combine(field_ref, own_ref, three_ref, two_low_ref, two_high_ref, one_ref, coef_ref, inverse_ref, place_ref, modes_ref):
    col = place_ref[1]
    cols = field_ref.shape[0]
    groups = inverse_ref.shape[0] // cols
    width_y = field_ref.shape[1] // WIDTH
    norm = jnp.float32(np.sqrt(np.float32(64 * width_y * WIDTH)))
    back = lax.rem(groups - col, groups)
    weights = turned(inverse_ref[rows_of(col, cols), :], back, cols)
    block = weights[:, :cols].astype(BF16)
    high, low = split(weights)
    held = (own_ref, three_ref, two_low_ref, two_high_ref, one_ref)
    for y in range(width_y):
        at = lanes_of(y)
        everything = jnp.concatenate([ref[:, at] for ref in held], 0)
        mass = jnp.concatenate([coef_ref[8 * MS : 8 * MS + 8, at]] * (cols // 8), axis=0)
        light = jnp.concatenate([coef_ref[8 * MI : 8 * MI + 8, at]] * (cols // 8), axis=0)
        rest = (field_ref[:, at] * mass - own_ref[:, at].astype(F32)).astype(BF16)
        result = (
            jnp.dot(high, everything, preferred_element_type=F32)
            + jnp.dot(low, everything, preferred_element_type=F32)
            + jnp.dot(block, rest, preferred_element_type=F32)
        )
        modes_ref[pl.ds(y, cols, stride=width_y), :] = result * light * norm


def local(start_block, node_mass, material_ids, moduli_table, influence):
    cols, _, width_y, width_z = start_block.shape
    lanes = width_y * width_z
    doms, groups = lax.axis_size("dom"), lax.axis_size("col")
    total_cols = cols * groups
    me, col = lax.axis_index("dom"), lax.axis_index("col")
    core = me % 2
    pair = [(i, i ^ 1) for i in range(doms)]
    across = [(i, i + 1 if i % 2 else i - 1) for i in range(1, doms - 1)]
    wide, deep = 4, 8
    place_of = np.arange(doms).reshape(deep, wide, 2)
    plane_groups = [place_of[:, :, c].reshape(-1).tolist() for c in range(2)]
    x_groups = [place_of[z, :, c].tolist() for z in range(deep) for c in range(2)]
    z_groups = [place_of[:, x, c].tolist() for x in range(wide) for c in range(2)]
    chip_of = place_of[..., None] * groups + np.arange(groups)
    chip_groups = [chip_of[z, :, c].reshape(-1).tolist() for z in range(deep) for c in range(2)]

    def exchange(payload):
        near = lax.ppermute(payload, "dom", pair)
        return near, lax.ppermute(payload, "dom", across)

    def col_ring(step):
        return [(i, (i + step) % groups) for i in range(groups)]

    place = jnp.stack([core, col, me]).astype(jnp.int32)
    targets = influence.reshape(influence.shape[0], lanes)

    base, pay, least = pl.pallas_call(
        prepare,
        out_shape=(
            shape(cols + 24, lanes),
            shape(cols + 16, lanes, BF16),
            jax.ShapeDtypeStruct((doms, 1, WIDTH), F32),
        ),
        in_specs=[pl.BlockSpec(memory_space=pltpu.HBM)] * 4,
        out_specs=(VMEM,) * 3,
        scratch_shapes=[
            pltpu.VMEM((cols * width_y, width_z), F32),
            pltpu.VMEM((width_y, width_z), F32),
            pltpu.VMEM((width_y, width_z), jnp.int32),
            pltpu.VMEM((1, moduli_table.shape[0]), F32),
            pltpu.SemaphoreType.DMA((4,)),
        ],
        compiler_params=pltpu.CompilerParams(vmem_limit_bytes=62398000),
    )(
        start_block.reshape(cols * width_y, width_z),
        node_mass.reshape(width_y, width_z),
        material_ids.reshape(width_y, width_z),
        moduli_table.reshape(1, -1),
    )
    near, far = exchange(pay)
    least = lax.all_to_all(least, "dom", 0, 0, tiled=True)
    forces, coef, field, top = pl.pallas_call(
        first_forces,
        out_shape=(shape(cols, lanes), shape(72, lanes), shape(cols, lanes), shape(8, WIDTH)),
        in_specs=[VMEM] * 3 + [SMEM],
        out_specs=(VMEM,) * 4,
        compiler_params=PARAMS,
    )(far, near, base, place)
    current, pay, scale, shift = pl.pallas_call(
        first_step,
        out_shape=(shape(cols, lanes), shape(cols, lanes, BF16), shape(8, lanes), shape(8, WIDTH)),
        in_specs=[VMEM] * 5,
        out_specs=(VMEM,) * 4,
        compiler_params=PARAMS,
    )(least, forces, field, coef, top)
    previous = field
    for step in range(DEGREE - 1):
        last = step == DEGREE - 2
        near, far = exchange(pay)
        outs = pl.pallas_call(
            functools.partial(later_step, last),
            out_shape=(shape(cols, lanes),) + (shape(cols, lanes, BF16),) * (2 if last else 1),
            in_specs=[VMEM] * 8,
            out_specs=(VMEM,) * (3 if last else 2),
            compiler_params=PARAMS,
        )(far, near, current, previous, coef, scale, shift, targets if last else shift)
        previous, current, pay = current, outs[0], outs[1]
    heavy = outs[2]
    near, far = exchange(pay)
    one, three = lax.ppermute(heavy, "col", col_ring(1)), lax.ppermute(heavy, "col", col_ring(3))
    two_low = lax.ppermute(one[: cols // 2], "col", col_ring(1))
    two_high = lax.ppermute(three[cols // 2 :], "col", col_ring(3))
    half = targets.shape[0] // 2
    t_rows, g_rows = half // wide, cols // wide
    chunk = jax.ShapeDtypeStruct((wide, t_rows + g_rows, total_cols), F32)
    keep, send = pl.pallas_call(
        early,
        out_shape=(chunk, chunk),
        in_specs=[VMEM] * 5 + [SMEM],
        out_specs=(VMEM,) * 2,
        scratch_shapes=[pltpu.VMEM((total_cols, lanes), BF16)],
        compiler_params=PARAMS,
    )(current, heavy, one, three, targets, place)
    split_field = (shape(cols, lanes, BF16),) * 2
    keep, send, high, low = pl.pallas_call(
        middle,
        out_shape=(chunk, chunk) + split_field,
        in_specs=[VMEM] * 9 + [SMEM],
        out_specs=(VMEM,) * 4,
        scratch_shapes=[pltpu.VMEM((total_cols, lanes), BF16)],
        input_output_aliases={0: 0, 1: 1},
        compiler_params=PARAMS,
    )(keep, send, far, near, current, coef, heavy, one, three, place)
    keep, send = pl.pallas_call(
        late,
        out_shape=(chunk, chunk),
        in_specs=[VMEM] * 8 + [SMEM],
        out_specs=(VMEM,) * 2,
        input_output_aliases={0: 0, 1: 1},
        compiler_params=PARAMS,
    )(keep, send, two_low, two_high, current, high, low, targets, place)

    summed = keep + lax.ppermute(send, "dom", pair)
    summed = lax.all_to_all(summed, "dom", 0, 0, tiled=True, axis_index_groups=x_groups)
    summed = pl.pallas_call(
        along_z,
        out_shape=jax.ShapeDtypeStruct((deep, 2 * (t_rows // deep + g_rows), WIDTH), F32),
        in_specs=[VMEM],
        out_specs=VMEM,
        compiler_params=PARAMS,
    )(summed)
    summed = lax.all_to_all(summed, "dom", 0, 0, tiled=True, axis_index_groups=z_groups)
    few = t_rows // deep
    target, gram = pl.pallas_call(
        along_chips,
        out_shape=(
            jax.ShapeDtypeStruct((deep * wide, 2 * few, WIDTH), F32),
            jax.ShapeDtypeStruct((wide * groups, g_rows, total_cols), F32),
        ),
        in_specs=[VMEM],
        out_specs=(VMEM,) * 2,
        compiler_params=PARAMS,
    )(summed)
    mine = lax.all_to_all(gram, ("dom", "col"), 0, 0, tiled=True, axis_index_groups=chip_groups)
    theirs = lax.ppermute(mine, "dom", pair)
    target = lax.all_to_all(target, "dom", 0, 0, tiled=True, axis_index_groups=plane_groups)
    inverse, ritz_matrix = pl.pallas_call(
        solve,
        out_shape=(shape(total_cols, total_cols),) * 2,
        in_specs=[VMEM] * 2 + [SMEM],
        out_specs=(VMEM,) * 2,
        scratch_shapes=[pltpu.VMEM((total_cols, total_cols), F32)] * 3,
        compiler_params=PARAMS,
    )(mine, theirs, place)
    part_rows = total_cols // doms
    kept, sent = pl.pallas_call(
        participate,
        out_shape=(shape(part_rows, half),) * 2,
        in_specs=[VMEM] * 2 + [SMEM],
        out_specs=(VMEM,) * 2,
        scratch_shapes=[pltpu.VMEM((half, total_cols), F32)],
        compiler_params=PARAMS,
    )(target, inverse, place)
    got = lax.ppermute(sent, "dom", pair)
    modes = pl.pallas_call(
        combine,
        out_shape=shape(cols * width_y, width_z),
        in_specs=[VMEM] * 8 + [SMEM],
        out_specs=VMEM,
        compiler_params=PARAMS,
    )(current, heavy, three, two_low, two_high, one, coef, inverse, place)
    first = core == 0
    participation = jnp.concatenate([jnp.where(first, kept, got), jnp.where(first, got, kept)], 1)
    return (modes.reshape(start_block.shape), ritz_matrix, participation)


def solution(mesh):
    placed = (
        P("col", "dom", None, None),
        P("dom", None, None),
        P("dom", None, None),
        P(),
        P("col", "dom", None, None),
    )
    return jax.shard_map(
        local,
        mesh=mesh,
        in_specs=placed,
        out_specs=(P("col", "dom", None, None), P(), P("dom", "col")),
        check_vma=False,
    )
```

```python
import functools

import jax
import jax.numpy as jnp
import numpy as np
from jax import lax
from jax.experimental import pallas as pl
from jax.experimental.pallas import tpu as pltpu
from jax.sharding import PartitionSpec as P

DEGREE = 4
LOW_RATIO = 0.02
F32, BF16 = jnp.float32, jnp.bfloat16
VMEM = pl.BlockSpec(memory_space=pltpu.VMEM)
SMEM = pl.BlockSpec(memory_space=pltpu.SMEM)
WIDTH = 128
PARAMS = pltpu.CompilerParams(vmem_limit_bytes=24 * 1024 * 1024)
H4, HZ, HZ4, E, EZ, G, GZ, MI, MS = range(9)


def shape(rows, lanes, dtype=F32):
    return jax.ShapeDtypeStruct((rows, lanes), dtype)


def lanes_of(y):
    return slice(y * WIDTH, (y + 1) * WIDTH)


def rows_of(group, size=16):
    return pl.ds(pl.multiple_of(group * size, size), size)


def twice(c):
    return jnp.concatenate([c, c], axis=0)


def stiffness_rows(width_y, u_at, v_at, w_at, coef):
    def with_roll(x):
        return x, pltpu.roll(x, WIDTH - 1, 1)

    u0, u1 = with_roll(u_at(0))
    v0, v1 = with_roll(v_at(0))
    w0, w1 = with_roll(w_at(0))
    kept = kept_z = None
    for y in range(width_y):
        c = functools.partial(coef, y)
        h4, hz, hz4 = c(H4), c(HZ), c(HZ4)
        ez, gz = c(EZ), c(GZ)
        p00 = ez * v0 + gz * w0
        p01 = ez * v1 + gz * w1
        if y + 1 < width_y:
            e, g = c(E), c(G)
            n0, n1 = with_roll(u_at(y + 1))
            x0, x1 = with_roll(v_at(y + 1))
            z0, z1 = with_roll(w_at(y + 1))
            p10 = ez * x0 + gz * z0
            p11 = ez * x1 + gz * z1
            q00 = e * v0 + g * w0
            q10 = e * x0 + g * z0
            side, other = p01 + p11, p00 + p10
            r00 = h4 * u0 - hz * n1 - q10 - side
            r10 = h4 * n0 - hz * u1 - q00 - side
            r01 = hz4 * u1 - hz * n0 - other - p11
            r11 = hz4 * n1 - hz * u0 - other - p01
        else:
            r00 = h4 * u0 - p01
            r01 = hz4 * u1 - p00
        here = r00 if kept is None else r00 + kept
        moved = r01 if kept_z is None else r01 + kept_z
        yield y, u0, here + pltpu.roll(moved, 1, 1)
        if y + 1 < width_y:
            kept, kept_z = r10, r11
            u0, u1, v0, v1, w0, w1 = n0, n1, x0, x1, z0, z1


def prepare(start_hbm, mass_hbm, ids_hbm, table_hbm, base_ref, pay_ref, least_ref, start_ref, mass_ref, ids_ref, table_ref, sems):
    pairs = ((mass_hbm, mass_ref), (ids_hbm, ids_ref), (table_hbm, table_ref), (start_hbm, start_ref))
    copies = [pltpu.make_async_copy(source, target, sems.at[i]) for i, (source, target) in enumerate(pairs)]
    for copy in copies:
        copy.start()
    cols = base_ref.shape[0] - 24
    width_y = ids_ref.shape[0]
    for copy in copies[:3]:
        copy.wait()
    mass, ids, table = mass_ref[...], ids_ref[...], table_ref[...]
    base_ref[cols + 16 :, :] = jnp.broadcast_to(jnp.max(table, axis=1, keepdims=True), (8, base_ref.shape[1]))
    least = jnp.min(jnp.min(mass, axis=0, keepdims=True), axis=1, keepdims=True)
    least_ref[...] = jnp.broadcast_to(least[None], least_ref.shape)
    moduli = jnp.zeros(ids.shape, F32)
    for k in range(table.shape[1]):
        moduli = jnp.where(ids == k, table[:, k : k + 1], moduli)
    moduli = moduli / 12.0
    high = moduli.astype(BF16).astype(F32)
    middle = (moduli - high).astype(BF16).astype(F32)
    low = moduli - high - middle
    pad = jnp.zeros((13, WIDTH), F32)
    for y in range(width_y):
        at = lanes_of(y)
        base_ref[cols : cols + 8, at] = jnp.broadcast_to(moduli[y : y + 1], (8, WIDTH))
        base_ref[cols + 8 : cols + 16, at] = jnp.broadcast_to(mass[y : y + 1], (8, WIDTH))
        parts = jnp.concatenate([high[y : y + 1], middle[y : y + 1], low[y : y + 1], pad], 0)
        pay_ref[cols:, at] = parts.astype(BF16)
    copies[3].wait()
    for y in range(width_y):
        plane = start_ref[pl.ds(y, cols, stride=width_y), :]
        base_ref[:cols, lanes_of(y)] = plane
        pay_ref[:cols, lanes_of(y)] = plane.astype(BF16)


def first_forces(far_ref, near_ref, base_ref, place_ref, forces_ref, coef_ref, field_ref, top_ref):
    cols = field_ref.shape[0]
    top_ref[...] = base_ref[cols + 16 :, :WIDTH]
    width_y = field_ref.shape[1] // WIDTH
    inner = lax.broadcasted_iota(jnp.int32, (8, WIDTH), 1) < WIDTH - 1
    first = place_ref[0] == 0
    for y in range(width_y):
        at = lanes_of(y)
        own, mass = base_ref[cols : cols + 8, at], base_ref[cols + 8 : cols + 16, at]
        parts = jnp.where(first, far_ref[cols:, at].astype(F32), near_ref[cols:, at].astype(F32))
        below = jnp.broadcast_to(parts[0:1] + parts[1:2] + parts[2:3], (8, WIDTH))
        near, far = jnp.where(first, own, below), jnp.where(first, below, own)
        both = near + far
        both_z = jnp.where(inner, both, 0.0)
        values = {
            H4: 4.0 * both,
            HZ: both_z,
            HZ4: 4.0 * both_z,
            E: near,
            EZ: jnp.where(inner, near, 0.0),
            G: far,
            GZ: jnp.where(inner, far, 0.0),
            MI: 1.0 / mass,
            MS: mass,
        }
        for place, value in values.items():
            coef_ref[8 * place : 8 * place + 8, at] = value

    def coef(y, place):
        return twice(coef_ref[8 * place : 8 * place + 8, lanes_of(y)])

    def group(i, carry):
        at = rows_of(i)
        rows = stiffness_rows(
            width_y,
            lambda y: base_ref[at, lanes_of(y)],
            lambda y: near_ref[at, lanes_of(y)].astype(F32),
            lambda y: far_ref[at, lanes_of(y)].astype(F32),
            coef,
        )
        for y, u, forces in rows:
            forces_ref[at, lanes_of(y)] = forces
            field_ref[at, lanes_of(y)] = u
        return carry

    lax.fori_loop(0, cols // 16, group, 0)


def first_step(least_ref, forces_ref, field_ref, coef_ref, top_ref, out_ref, pay_ref, scale_ref, shift_ref):
    cols = field_ref.shape[0]
    width_y = field_ref.shape[1] // WIDTH
    least = jnp.min(jnp.min(least_ref[...], axis=0), axis=1, keepdims=True)
    upper = 16.0 / 3.0 * top_ref[...] / least
    lower = LOW_RATIO * upper
    half = (upper - lower) / 2.0
    shift = (upper + lower) / 2.0 / half
    shift_ref[...] = shift
    for y in range(width_y):
        at = lanes_of(y)
        scale = 1.0 / (coef_ref[8 * MS : 8 * MS + 8, at] * half)
        scale_ref[:, at] = scale
        scale, shifts = (jnp.concatenate([x] * (cols // 8), 0) for x in (scale, shift))
        result = forces_ref[:, at] * scale - shifts * field_ref[:, at]
        out_ref[:, at] = result
        pay_ref[:, at] = result.astype(BF16)


def near_rows(width_y, u_at, v_at, coef):
    def with_roll(x):
        return x, pltpu.roll(x, WIDTH - 1, 1)

    u0, u1 = with_roll(u_at(0))
    v0, v1 = with_roll(v_at(0))
    kept = kept_z = None
    for y in range(width_y):
        c = functools.partial(coef, y)
        h4, hz4, ez = c(H4), c(HZ4), c(EZ)
        p00, p01 = ez * v0, ez * v1
        if y + 1 < width_y:
            hz, e = c(HZ), c(E)
            n0, n1 = with_roll(u_at(y + 1))
            x0, x1 = with_roll(v_at(y + 1))
            p10, p11 = ez * x0, ez * x1
            side, other = p01 + p11, p00 + p10
            r00 = h4 * u0 - hz * n1 - e * x0 - side
            r10 = h4 * n0 - hz * u1 - e * v0 - side
            r01 = hz4 * u1 - hz * n0 - other - p11
            r11 = hz4 * n1 - hz * u0 - other - p01
        else:
            r00 = h4 * u0 - p01
            r01 = hz4 * u1 - p00
        here = r00 if kept is None else r00 + kept
        moved = r01 if kept_z is None else r01 + kept_z
        yield y, u0, here + pltpu.roll(moved, 1, 1)
        if y + 1 < width_y:
            kept, kept_z = r10, r11
            u0, u1, v0, v1 = n0, n1, x0, x1


def far_rows(width_y, w_at, coef):
    def with_roll(x):
        return x, pltpu.roll(x, WIDTH - 1, 1)

    w0, w1 = with_roll(w_at(0))
    kept = kept_z = None
    for y in range(width_y):
        gz = coef(y, GZ)
        p00, p01 = gz * w0, gz * w1
        if y + 1 < width_y:
            g = coef(y, G)
            z0, z1 = with_roll(w_at(y + 1))
            p10, p11 = gz * z0, gz * z1
            side, other = p01 + p11, p00 + p10
            r00, r10 = g * z0 + side, g * w0 + side
            r01, r11 = other + p11, other + p01
        else:
            r00, r01 = p01, p00
        here = r00 if kept is None else r00 + kept
        moved = r01 if kept_z is None else r01 + kept_z
        yield y, here + pltpu.roll(moved, 1, 1)
        if y + 1 < width_y:
            kept, kept_z = r10, r11
            w0, w1 = z0, z1


def half_step(near_ref, field_ref, before_ref, coef_ref, scale_ref, shift_ref, target_ref, base_ref):
    cols = field_ref.shape[0]
    width_y = field_ref.shape[1] // WIDTH

    def coef(y, place):
        return twice(coef_ref[8 * place : 8 * place + 8, lanes_of(y)])

    def group(i, carry):
        at = rows_of(i)
        rows = near_rows(
            width_y, lambda y: field_ref[at, lanes_of(y)], lambda y: near_ref[at, lanes_of(y)].astype(F32), coef
        )
        shift2 = twice(shift_ref[...])
        for y, u, forces in rows:
            result = 2.0 * (forces * twice(scale_ref[:, lanes_of(y)]) - shift2 * u) - before_ref[at, lanes_of(y)]
            base_ref[at, lanes_of(y)] = result
        return carry

    lax.fori_loop(0, cols // 16, group, 0)


def full_step(last, far_ref, base_ref, coef_ref, scale_ref, out_ref, pay_ref, *heavy_ref):
    cols = base_ref.shape[0]
    width_y = base_ref.shape[1] // WIDTH

    def coef(y, place):
        return twice(coef_ref[8 * place : 8 * place + 8, lanes_of(y)])

    def group(i, carry):
        at = rows_of(i)
        for y, forces in far_rows(width_y, lambda y: far_ref[at, lanes_of(y)].astype(F32), coef):
            result = base_ref[at, lanes_of(y)] - 2.0 * (forces * twice(scale_ref[:, lanes_of(y)]))
            out_ref[at, lanes_of(y)] = result
            pay_ref[at, lanes_of(y)] = result.astype(BF16)
            if last:
                heavy_ref[0][at, lanes_of(y)] = (result * coef(y, MS)).astype(BF16)
        return carry

    lax.fori_loop(0, cols // 16, group, 0)


def dot_nt(a, b):
    return lax.dot_general(a, b, (((1,), (1,)), ((), ())), preferred_element_type=F32)


def spread(ref, lanes, targets, gram):
    parts = ref.shape[0]
    t, g = targets.shape[0] // parts, gram.shape[0] // parts
    for x in range(parts):
        ref[x, :t, lanes] = targets[x * t : (x + 1) * t]
        ref[x, t:, lanes] = gram[x * g : (x + 1) * g]


def halves(x):
    high = x.astype(BF16)
    return high, (x - high.astype(F32)).astype(BF16)


def early(field_ref, own_ref, one_ref, three_ref, target_ref, place_ref, keep_ref, send_ref, all_ref):
    cols = field_ref.shape[0]
    core = place_ref[0]
    all_ref[:cols] = own_ref[...]
    all_ref[cols : 2 * cols] = three_ref[...]
    all_ref[2 * cols : 3 * cols] = jnp.zeros((cols, all_ref.shape[1]), BF16)
    all_ref[3 * cols :] = one_ref[...]
    everything = all_ref[...]
    high, low = halves(field_ref[...])
    gram = dot_nt(high, everything) + dot_nt(low, everything)
    half = target_ref.shape[0] // 2
    for side, ref in ((core, keep_ref), (1 - core, send_ref)):
        spread(ref, slice(None), dot_nt(target_ref[rows_of(side, half), :], everything), gram)


def stiff_rows(core, stiff, lanes, keep_ref, send_ref):
    parts = keep_ref.shape[0]
    g = stiff.shape[0] // parts
    t = keep_ref.shape[1] - g

    def put(ref):
        for x in range(parts):
            ref[x, t:, lanes] = stiff[x * g : (x + 1) * g]

    pl.when(core == 0)(lambda: put(keep_ref))
    pl.when(core != 0)(lambda: put(send_ref))


def middle(keep_in, send_in, far_ref, near_ref, field_ref, coef_ref, own_ref, one_ref, three_ref, place_ref, keep_ref, send_ref, high_ref, low_ref, all_ref):
    cols = field_ref.shape[0]
    width_y = field_ref.shape[1] // WIDTH

    def coef(y, place):
        return twice(coef_ref[8 * place : 8 * place + 8, lanes_of(y)])

    def group(i, carry):
        at = rows_of(i)
        rows = stiffness_rows(
            width_y,
            lambda y: field_ref[at, lanes_of(y)],
            lambda y: near_ref[at, lanes_of(y)].astype(F32),
            lambda y: far_ref[at, lanes_of(y)].astype(F32),
            coef,
        )
        for y, u, forces in rows:
            high_ref[at, lanes_of(y)], low_ref[at, lanes_of(y)] = halves(forces * coef(y, MI))
        return carry

    lax.fori_loop(0, cols // 16, group, 0)
    all_ref[:cols] = own_ref[...]
    all_ref[cols : 2 * cols] = three_ref[...]
    all_ref[2 * cols : 3 * cols] = jnp.zeros((cols, all_ref.shape[1]), BF16)
    all_ref[3 * cols :] = one_ref[...]
    everything = all_ref[...]
    stiff = dot_nt(high_ref[...], everything) + dot_nt(low_ref[...], everything)
    stiff_rows(place_ref[0], stiff, slice(None), keep_ref, send_ref)


def late(keep_in, send_in, two_low_ref, two_high_ref, field_ref, high_ref, low_ref, target_ref, place_ref, keep_ref, send_ref):
    cols = field_ref.shape[0]
    core = place_ref[0]
    two = jnp.concatenate([two_low_ref[...], two_high_ref[...]], 0)
    stiff = dot_nt(high_ref[...], two) + dot_nt(low_ref[...], two)
    high, low = halves(field_ref[...])
    heavy = dot_nt(high, two) + dot_nt(low, two)
    half = target_ref.shape[0] // 2
    lanes = slice(2 * cols, 3 * cols)
    for side, ref in ((core, keep_ref), (1 - core, send_ref)):
        spread(ref, lanes, dot_nt(target_ref[rows_of(side, half), :], two), heavy)
    stiff_rows(core, stiff, lanes, keep_ref, send_ref)


def turned(x, steps, cols):
    groups = x.shape[1] // cols

    def by(k):
        return jnp.concatenate([x[:, (groups - k) * cols :], x[:, : (groups - k) * cols]], 1)

    result = x
    for k in range(1, groups):
        result = jnp.where(steps == k, by(k), result)
    return result


def split(x):
    high = x.astype(BF16)
    return high, (x - high.astype(F32)).astype(BF16)


def dot_split(a, b, dims):
    (ah, al), (bh, bl) = split(a), split(b)
    dot = functools.partial(lax.dot_general, dimension_numbers=(dims, ((), ())), preferred_element_type=F32)
    return dot(ah, bh) + (dot(ah, bl) + dot(al, bh))


def inverse_factor(work_ref, panel, few):
    n = work_ref.shape[0]
    tiles, strips = n // WIDTH, panel // 8
    row = lax.broadcasted_iota(jnp.int32, (8, WIDTH), 0)
    lane = lax.broadcasted_iota(jnp.int32, (8, WIDTH), 1)
    for start in range(0, n, panel):
        lines = [[work_ref[start + 8 * r : start + 8 * r + 8, lanes_of(t)] for r in range(strips)] for t in range(tiles)]
        pivots = [jnp.ones((8, WIDTH), F32)] * strips
        for first in range(0, panel, few):
            columns, factors = [], []
            for place in range(start + first, start + first + few):
                tile, inside = divmod(place, WIDTH)
                spread_out = {
                    r: jnp.broadcast_to(lines[tile][r][:, inside : inside + 1], (8, WIDTH)) for r in range(first // 8, strips)
                }
                columns.append(spread_out)
            for k in range(0, few, 2):
                at, i = divmod(first + k, 8)
                left, right = columns[k], columns[k + 1]
                pivot, below = left[at][i : i + 1], left[at][i + 1 : i + 2]
                beside = right[at][i : i + 1]
                minor = pivot * right[at][i + 1 : i + 2] - below * beside
                over = 1.0 / pivot
                slope, scale = below * over, pivot * (1.0 / minor)
                one = {r: left[r] * over for r in range(at, strips)}
                one[at] = jnp.where(row > i, one[at], 0.0)
                two = {r: (right[r] - one[r] * beside) * scale for r in range(at, strips)}
                two[at] = jnp.where(row > i + 1, two[at], 0.0)
                pivots[at] = jnp.where(row == i, pivot, jnp.where(row == i + 1, minor * over, pivots[at]))
                for l in range(k + 2, few):
                    u = columns[l][at][i : i + 1]
                    v = columns[l][at][i + 1 : i + 2] - slope * u
                    for r in range(at, strips):
                        columns[l][r] = columns[l][r] - one[r] * u - two[r] * v
                factors.append((at, i, one, two, slope))
            for k, (at, i, one, two, slope) in enumerate(factors):
                tile, inside = divmod(start + first + 2 * k, WIDTH)
                for t in range(tiles):
                    u, v = lines[t][at][i : i + 1], lines[t][at][i + 1 : i + 2]
                    if t == tile:
                        u = u + jnp.where(lane[:1] == inside, 1.0, 0.0)
                    v = v - slope * u
                    if t == tile:
                        v = v + jnp.where(lane[:1] == inside + 1, 1.0, 0.0)
                    for r in range(at, strips):
                        lines[t][r] = lines[t][r] - one[r] * u - two[r] * v
        factor_rows = [[] for _ in range(tiles)]
        update_rows = [[] for _ in range(tiles)]
        for r in range(strips):
            scale = 1.0 / jnp.sqrt(pivots[r])
            here = row + start + 8 * r
            for t in range(tiles):
                place = lane + t * WIDTH
                full = jnp.where(place == here, scale, lines[t][r] * scale)
                inverse = jnp.where(place <= here, full, 0.0)
                work_ref[start + 8 * r : start + 8 * r + 8, lanes_of(t)] = inverse
                factor_rows[t].append(full)
                update_rows[t].append(jnp.where((place >= start) & (place < start + panel), inverse, full))
        rest = n - start - panel
        if rest:
            factor, rows = (
                jnp.concatenate([jnp.concatenate(strip, 0) for strip in side], 1) for side in (factor_rows, update_rows)
            )
            update = dot_split(factor, rows, ((0,), (0,)))
            for t in range(tiles):
                old = work_ref[start + panel :, lanes_of(t)]
                place = lax.broadcasted_iota(jnp.int32, old.shape, 1) + t * WIDTH
                old = jnp.where((place >= start) & (place < start + panel), 0.0, old)
                work_ref[start + panel :, lanes_of(t)] = old - update[start + panel :, lanes_of(t)]


def along_z(parts_ref, out_ref):
    total = jnp.sum(parts_ref[...], axis=0)
    planes, rows = out_ref.shape[0], out_ref.shape[1] // 2
    g = (total.shape[0] - planes * rows) // (1 - planes)
    t = rows - g
    gram = total[planes * t :]
    for z in range(planes):
        mine = total[z * t : (z + 1) * t]
        out_ref[z, : 2 * t, :] = jnp.concatenate([mine[:, :WIDTH], mine[:, WIDTH:]], 0)
        out_ref[z, 2 * t : 2 * t + g, :] = gram[:, :WIDTH]
        out_ref[z, 2 * t + g :, :] = gram[:, WIDTH:]


def along_chips(parts_ref, target_ref, gram_ref):
    total = jnp.sum(parts_ref[...], axis=0)
    g = gram_ref.shape[1]
    t = target_ref.shape[1]
    for plane in range(target_ref.shape[0]):
        target_ref[plane] = total[:t]
    for chip in range(gram_ref.shape[0]):
        gram_ref[chip, :, :WIDTH] = total[t : t + g]
        gram_ref[chip, :, WIDTH:] = total[t + g :]


def solve(mine_ref, theirs_ref, place_ref, inverse_ref, ritz_ref, mass_ref, stiff_ref, work_ref):
    core = place_ref[0]
    total = work_ref.shape[0]
    chips, g = mine_ref.shape[:2]
    cols = total // 4
    along_x = cols // g
    for side, into in ((0, stiff_ref), (1, mass_ref)):
        chosen = core == side
        for q in range(total // cols):
            for x in range(along_x):
                chip = x * (total // cols) + q
                rows = jnp.where(chosen, mine_ref[chip], theirs_ref[chip])
                rows = jnp.concatenate([rows[:, total - q * cols :], rows[:, : total - q * cols]], 1) if q else rows
                into[q * cols + x * g : q * cols + (x + 1) * g, :] = rows
    gram = mass_ref[...]
    on = lax.broadcasted_iota(jnp.int32, gram.shape, 0) == lax.broadcasted_iota(jnp.int32, gram.shape, 1)
    diagonal = jnp.where(on, gram, 0.0)
    across = 1.0 / jnp.sqrt(jnp.sum(diagonal, axis=0, keepdims=True))
    down = 1.0 / jnp.sqrt(jnp.sum(diagonal, axis=1, keepdims=True))
    work_ref[...] = gram * across * down
    inverse_factor(work_ref, 64, 16)
    inverse = work_ref[...] * across
    inverse_ref[...] = inverse
    ritz_ref[...] = dot_split(dot_split(inverse, stiff_ref[...], ((1,), (1,))), inverse, ((1,), (1,)))


def participate(targets_in, inverse_ref, place_ref, keep_ref, send_ref, targets_ref):
    core, col, me = place_ref[0], place_ref[1], place_ref[2]
    groups = 4
    cols = inverse_ref.shape[0] // groups
    deep, wide = 8, targets_in.shape[0] // 8
    t = targets_in.shape[1] // 2
    for x in range(wide):
        for tile in range(2):
            rows = [targets_in[z * wide + x, tile * t : (tile + 1) * t] for z in range(deep)]
            targets_ref[x * deep * t : (x + 1) * deep * t, lanes_of(tile)] = jnp.concatenate(rows, 0)
    rows = inverse_ref[pl.ds(pl.multiple_of(me // 2 * 8, 8), 8), :]
    part = dot_split(turned(rows, lax.rem(groups - col, groups), cols), targets_ref[...], ((1,), (1,)))
    keep_ref[...] = jnp.where(core == 0, part[:4], part[4:])
    send_ref[...] = jnp.where(core == 0, part[4:], part[:4])


def combine(field_ref, own_ref, three_ref, two_low_ref, two_high_ref, one_ref, coef_ref, inverse_ref, place_ref, modes_ref):
    col = place_ref[1]
    cols = field_ref.shape[0]
    groups = inverse_ref.shape[0] // cols
    width_y = field_ref.shape[1] // WIDTH
    norm = jnp.float32(np.sqrt(np.float32(64 * width_y * WIDTH)))
    back = lax.rem(groups - col, groups)
    weights = turned(inverse_ref[rows_of(col, cols), :], back, cols)
    block = weights[:, :cols].astype(BF16)
    high, low = split(weights)
    held = (own_ref, three_ref, two_low_ref, two_high_ref, one_ref)
    for y in range(width_y):
        at = lanes_of(y)
        everything = jnp.concatenate([ref[:, at] for ref in held], 0)
        mass = jnp.concatenate([coef_ref[8 * MS : 8 * MS + 8, at]] * (cols // 8), axis=0)
        light = jnp.concatenate([coef_ref[8 * MI : 8 * MI + 8, at]] * (cols // 8), axis=0)
        rest = (field_ref[:, at] * mass - own_ref[:, at].astype(F32)).astype(BF16)
        result = (
            jnp.dot(high, everything, preferred_element_type=F32)
            + jnp.dot(low, everything, preferred_element_type=F32)
            + jnp.dot(block, rest, preferred_element_type=F32)
        )
        modes_ref[pl.ds(y, cols, stride=width_y), :] = result * light * norm


def local(start_block, node_mass, material_ids, moduli_table, influence):
    cols, _, width_y, width_z = start_block.shape
    lanes = width_y * width_z
    doms, groups = lax.axis_size("dom"), lax.axis_size("col")
    total_cols = cols * groups
    me, col = lax.axis_index("dom"), lax.axis_index("col")
    core = me % 2
    pair = [(i, i ^ 1) for i in range(doms)]
    across = [(i, i + 1 if i % 2 else i - 1) for i in range(1, doms - 1)]
    wide, deep = 4, 8
    place_of = np.arange(doms).reshape(deep, wide, 2)
    plane_groups = [place_of[:, :, c].reshape(-1).tolist() for c in range(2)]
    x_groups = [place_of[z, :, c].tolist() for z in range(deep) for c in range(2)]
    z_groups = [place_of[:, x, c].tolist() for x in range(wide) for c in range(2)]
    chip_of = place_of[..., None] * groups + np.arange(groups)
    chip_groups = [chip_of[z, :, c].reshape(-1).tolist() for z in range(deep) for c in range(2)]

    def exchange(payload):
        near = lax.ppermute(payload, "dom", pair)
        return near, lax.ppermute(payload, "dom", across)

    def col_ring(step):
        return [(i, (i + step) % groups) for i in range(groups)]

    place = jnp.stack([core, col, me]).astype(jnp.int32)
    targets = influence.reshape(influence.shape[0], lanes)

    base, pay, least = pl.pallas_call(
        prepare,
        out_shape=(
            shape(cols + 24, lanes),
            shape(cols + 16, lanes, BF16),
            jax.ShapeDtypeStruct((doms, 1, WIDTH), F32),
        ),
        in_specs=[pl.BlockSpec(memory_space=pltpu.HBM)] * 4,
        out_specs=(VMEM,) * 3,
        scratch_shapes=[
            pltpu.VMEM((cols * width_y, width_z), F32),
            pltpu.VMEM((width_y, width_z), F32),
            pltpu.VMEM((width_y, width_z), jnp.int32),
            pltpu.VMEM((1, moduli_table.shape[0]), F32),
            pltpu.SemaphoreType.DMA((4,)),
        ],
        compiler_params=pltpu.CompilerParams(vmem_limit_bytes=62398000),
    )(
        start_block.reshape(cols * width_y, width_z),
        node_mass.reshape(width_y, width_z),
        material_ids.reshape(width_y, width_z),
        moduli_table.reshape(1, -1),
    )
    near, far = exchange(pay)
    least = lax.all_to_all(least, "dom", 0, 0, tiled=True)
    forces, coef, field, top = pl.pallas_call(
        first_forces,
        out_shape=(shape(cols, lanes), shape(72, lanes), shape(cols, lanes), shape(8, WIDTH)),
        in_specs=[VMEM] * 3 + [SMEM],
        out_specs=(VMEM,) * 4,
        compiler_params=PARAMS,
    )(far, near, base, place)
    current, pay, scale, shift = pl.pallas_call(
        first_step,
        out_shape=(shape(cols, lanes), shape(cols, lanes, BF16), shape(8, lanes), shape(8, WIDTH)),
        in_specs=[VMEM] * 5,
        out_specs=(VMEM,) * 4,
        compiler_params=PARAMS,
    )(least, forces, field, coef, top)
    previous = field
    for step in range(DEGREE - 1):
        last = step == DEGREE - 2
        near, far = exchange(pay)
        partly = pl.pallas_call(
            half_step,
            out_shape=shape(cols, lanes),
            in_specs=[VMEM] * 7,
            out_specs=VMEM,
            compiler_params=PARAMS,
        )(near, current, previous, coef, scale, shift, targets if last else shift)
        outs = pl.pallas_call(
            functools.partial(full_step, last),
            out_shape=(shape(cols, lanes),) + (shape(cols, lanes, BF16),) * (2 if last else 1),
            in_specs=[VMEM] * 4,
            out_specs=(VMEM,) * (3 if last else 2),
            compiler_params=PARAMS,
        )(far, partly, coef, scale)
        previous, current, pay = current, outs[0], outs[1]
    heavy = outs[2]
    near, far = exchange(pay)
    one, three = lax.ppermute(heavy, "col", col_ring(1)), lax.ppermute(heavy, "col", col_ring(3))
    two_low = lax.ppermute(one[: cols // 2], "col", col_ring(1))
    two_high = lax.ppermute(three[cols // 2 :], "col", col_ring(3))
    half = targets.shape[0] // 2
    t_rows, g_rows = half // wide, cols // wide
    chunk = jax.ShapeDtypeStruct((wide, t_rows + g_rows, total_cols), F32)
    keep, send = pl.pallas_call(
        early,
        out_shape=(chunk, chunk),
        in_specs=[VMEM] * 5 + [SMEM],
        out_specs=(VMEM,) * 2,
        scratch_shapes=[pltpu.VMEM((total_cols, lanes), BF16)],
        compiler_params=PARAMS,
    )(current, heavy, one, three, targets, place)
    split_field = (shape(cols, lanes, BF16),) * 2
    keep, send, high, low = pl.pallas_call(
        middle,
        out_shape=(chunk, chunk) + split_field,
        in_specs=[VMEM] * 9 + [SMEM],
        out_specs=(VMEM,) * 4,
        scratch_shapes=[pltpu.VMEM((total_cols, lanes), BF16)],
        input_output_aliases={0: 0, 1: 1},
        compiler_params=PARAMS,
    )(keep, send, far, near, current, coef, heavy, one, three, place)
    keep, send = pl.pallas_call(
        late,
        out_shape=(chunk, chunk),
        in_specs=[VMEM] * 8 + [SMEM],
        out_specs=(VMEM,) * 2,
        input_output_aliases={0: 0, 1: 1},
        compiler_params=PARAMS,
    )(keep, send, two_low, two_high, current, high, low, targets, place)

    summed = keep + lax.ppermute(send, "dom", pair)
    summed = lax.all_to_all(summed, "dom", 0, 0, tiled=True, axis_index_groups=x_groups)
    summed = pl.pallas_call(
        along_z,
        out_shape=jax.ShapeDtypeStruct((deep, 2 * (t_rows // deep + g_rows), WIDTH), F32),
        in_specs=[VMEM],
        out_specs=VMEM,
        compiler_params=PARAMS,
    )(summed)
    summed = lax.all_to_all(summed, "dom", 0, 0, tiled=True, axis_index_groups=z_groups)
    few = t_rows // deep
    target, gram = pl.pallas_call(
        along_chips,
        out_shape=(
            jax.ShapeDtypeStruct((deep * wide, 2 * few, WIDTH), F32),
            jax.ShapeDtypeStruct((wide * groups, g_rows, total_cols), F32),
        ),
        in_specs=[VMEM],
        out_specs=(VMEM,) * 2,
        compiler_params=PARAMS,
    )(summed)
    mine = lax.all_to_all(gram, ("dom", "col"), 0, 0, tiled=True, axis_index_groups=chip_groups)
    theirs = lax.ppermute(mine, "dom", pair)
    target = lax.all_to_all(target, "dom", 0, 0, tiled=True, axis_index_groups=plane_groups)
    inverse, ritz_matrix = pl.pallas_call(
        solve,
        out_shape=(shape(total_cols, total_cols),) * 2,
        in_specs=[VMEM] * 2 + [SMEM],
        out_specs=(VMEM,) * 2,
        scratch_shapes=[pltpu.VMEM((total_cols, total_cols), F32)] * 3,
        compiler_params=PARAMS,
    )(mine, theirs, place)
    part_rows = total_cols // doms
    kept, sent = pl.pallas_call(
        participate,
        out_shape=(shape(part_rows, half),) * 2,
        in_specs=[VMEM] * 2 + [SMEM],
        out_specs=(VMEM,) * 2,
        scratch_shapes=[pltpu.VMEM((half, total_cols), F32)],
        compiler_params=PARAMS,
    )(target, inverse, place)
    got = lax.ppermute(sent, "dom", pair)
    modes = pl.pallas_call(
        combine,
        out_shape=shape(cols * width_y, width_z),
        in_specs=[VMEM] * 8 + [SMEM],
        out_specs=VMEM,
        compiler_params=PARAMS,
    )(current, heavy, three, two_low, two_high, one, coef, inverse, place)
    first = core == 0
    participation = jnp.concatenate([jnp.where(first, kept, got), jnp.where(first, got, kept)], 1)
    return (modes.reshape(start_block.shape), ritz_matrix, participation)


def solution(mesh):
    placed = (
        P("col", "dom", None, None),
        P("dom", None, None),
        P("dom", None, None),
        P(),
        P("col", "dom", None, None),
    )
    return jax.shard_map(
        local,
        mesh=mesh,
        in_specs=placed,
        out_specs=(P("col", "dom", None, None), P(), P("dom", "col")),
        check_vma=False,
    )
```

```python
import functools

import jax
import jax.numpy as jnp
import numpy as np
from jax import lax
from jax.experimental import pallas as pl
from jax.experimental.pallas import tpu as pltpu
from jax.sharding import PartitionSpec as P

DEGREE = 4
LOW_RATIO = 0.02
F32, BF16 = jnp.float32, jnp.bfloat16
VMEM = pl.BlockSpec(memory_space=pltpu.VMEM)
SMEM = pl.BlockSpec(memory_space=pltpu.SMEM)
WIDTH = 128
PARAMS = pltpu.CompilerParams(vmem_limit_bytes=24 * 1024 * 1024)
H4, HZ, HZ4, E, EZ, G, GZ, MI, MS = range(9)


def shape(rows, lanes, dtype=F32):
    return jax.ShapeDtypeStruct((rows, lanes), dtype)


def lanes_of(y):
    return slice(y * WIDTH, (y + 1) * WIDTH)


def rows_of(group, size=16):
    return pl.ds(pl.multiple_of(group * size, size), size)


def twice(c):
    return jnp.concatenate([c, c], axis=0)


def stiffness_rows(width_y, u_at, v_at, w_at, coef):
    def with_roll(x):
        return x, pltpu.roll(x, WIDTH - 1, 1)

    u0, u1 = with_roll(u_at(0))
    v0, v1 = with_roll(v_at(0))
    w0, w1 = with_roll(w_at(0))
    kept = kept_z = None
    for y in range(width_y):
        c = functools.partial(coef, y)
        h4, hz, hz4 = c(H4), c(HZ), c(HZ4)
        ez, gz = c(EZ), c(GZ)
        p00 = ez * v0 + gz * w0
        p01 = ez * v1 + gz * w1
        if y + 1 < width_y:
            e, g = c(E), c(G)
            n0, n1 = with_roll(u_at(y + 1))
            x0, x1 = with_roll(v_at(y + 1))
            z0, z1 = with_roll(w_at(y + 1))
            p10 = ez * x0 + gz * z0
            p11 = ez * x1 + gz * z1
            q00 = e * v0 + g * w0
            q10 = e * x0 + g * z0
            side, other = p01 + p11, p00 + p10
            r00 = h4 * u0 - hz * n1 - q10 - side
            r10 = h4 * n0 - hz * u1 - q00 - side
            r01 = hz4 * u1 - hz * n0 - other - p11
            r11 = hz4 * n1 - hz * u0 - other - p01
        else:
            r00 = h4 * u0 - p01
            r01 = hz4 * u1 - p00
        here = r00 if kept is None else r00 + kept
        moved = r01 if kept_z is None else r01 + kept_z
        yield y, u0, here + pltpu.roll(moved, 1, 1)
        if y + 1 < width_y:
            kept, kept_z = r10, r11
            u0, u1, v0, v1, w0, w1 = n0, n1, x0, x1, z0, z1


def prepare(start_hbm, mass_hbm, ids_hbm, table_hbm, base_ref, pay_ref, least_ref, start_ref, mass_ref, ids_ref, table_ref, sems):
    pairs = ((mass_hbm, mass_ref), (ids_hbm, ids_ref), (table_hbm, table_ref), (start_hbm, start_ref))
    copies = [pltpu.make_async_copy(source, target, sems.at[i]) for i, (source, target) in enumerate(pairs)]
    for copy in copies:
        copy.start()
    cols = base_ref.shape[0] - 24
    width_y = ids_ref.shape[0]
    for copy in copies[:3]:
        copy.wait()
    mass, ids, table = mass_ref[...], ids_ref[...], table_ref[...]
    base_ref[cols + 16 :, :] = jnp.broadcast_to(jnp.max(table, axis=1, keepdims=True), (8, base_ref.shape[1]))
    least = jnp.min(jnp.min(mass, axis=0, keepdims=True), axis=1, keepdims=True)
    least_ref[...] = jnp.broadcast_to(least[None], least_ref.shape)
    moduli = jnp.zeros(ids.shape, F32)
    for k in range(table.shape[1]):
        moduli = jnp.where(ids == k, table[:, k : k + 1], moduli)
    moduli = moduli / 12.0
    high = moduli.astype(BF16).astype(F32)
    middle = (moduli - high).astype(BF16).astype(F32)
    low = moduli - high - middle
    pad = jnp.zeros((13, WIDTH), F32)
    for y in range(width_y):
        at = lanes_of(y)
        base_ref[cols : cols + 8, at] = jnp.broadcast_to(moduli[y : y + 1], (8, WIDTH))
        base_ref[cols + 8 : cols + 16, at] = jnp.broadcast_to(mass[y : y + 1], (8, WIDTH))
        parts = jnp.concatenate([high[y : y + 1], middle[y : y + 1], low[y : y + 1], pad], 0)
        pay_ref[cols:, at] = parts.astype(BF16)
    copies[3].wait()
    for y in range(width_y):
        plane = start_ref[pl.ds(y, cols, stride=width_y), :]
        base_ref[:cols, lanes_of(y)] = plane
        pay_ref[:cols, lanes_of(y)] = plane.astype(BF16)


def first_forces(far_ref, near_ref, base_ref, place_ref, forces_ref, coef_ref, field_ref, top_ref):
    cols = field_ref.shape[0]
    top_ref[...] = base_ref[cols + 16 :, :WIDTH]
    width_y = field_ref.shape[1] // WIDTH
    inner = lax.broadcasted_iota(jnp.int32, (8, WIDTH), 1) < WIDTH - 1
    first = place_ref[0] == 0
    for y in range(width_y):
        at = lanes_of(y)
        own, mass = base_ref[cols : cols + 8, at], base_ref[cols + 8 : cols + 16, at]
        parts = jnp.where(first, far_ref[cols:, at].astype(F32), near_ref[cols:, at].astype(F32))
        below = jnp.broadcast_to(parts[0:1] + parts[1:2] + parts[2:3], (8, WIDTH))
        near, far = jnp.where(first, own, below), jnp.where(first, below, own)
        both = near + far
        both_z = jnp.where(inner, both, 0.0)
        values = {
            H4: 4.0 * both,
            HZ: both_z,
            HZ4: 4.0 * both_z,
            E: near,
            EZ: jnp.where(inner, near, 0.0),
            G: far,
            GZ: jnp.where(inner, far, 0.0),
            MI: 1.0 / mass,
            MS: mass,
        }
        for place, value in values.items():
            coef_ref[8 * place : 8 * place + 8, at] = value

    def coef(y, place):
        return twice(coef_ref[8 * place : 8 * place + 8, lanes_of(y)])

    def group(i, carry):
        at = rows_of(i)
        rows = stiffness_rows(
            width_y,
            lambda y: base_ref[at, lanes_of(y)],
            lambda y: near_ref[at, lanes_of(y)].astype(F32),
            lambda y: far_ref[at, lanes_of(y)].astype(F32),
            coef,
        )
        for y, u, forces in rows:
            forces_ref[at, lanes_of(y)] = forces
            field_ref[at, lanes_of(y)] = u
        return carry

    lax.fori_loop(0, cols // 16, group, 0)


def first_step(least_ref, forces_ref, field_ref, coef_ref, top_ref, out_ref, pay_ref, scale_ref, shift_ref):
    cols = field_ref.shape[0]
    width_y = field_ref.shape[1] // WIDTH
    least = jnp.min(jnp.min(least_ref[...], axis=0), axis=1, keepdims=True)
    upper = 16.0 / 3.0 * top_ref[...] / least
    lower = LOW_RATIO * upper
    half = (upper - lower) / 2.0
    shift = (upper + lower) / 2.0 / half
    shift_ref[...] = shift
    for y in range(width_y):
        at = lanes_of(y)
        scale = 1.0 / (coef_ref[8 * MS : 8 * MS + 8, at] * half)
        scale_ref[:, at] = scale
        scale, shifts = (jnp.concatenate([x] * (cols // 8), 0) for x in (scale, shift))
        result = forces_ref[:, at] * scale - shifts * field_ref[:, at]
        out_ref[:, at] = result
        pay_ref[:, at] = result.astype(BF16)


def near_rows(width_y, u_at, v_at, coef):
    def with_roll(x):
        return x, pltpu.roll(x, WIDTH - 1, 1)

    u0, u1 = with_roll(u_at(0))
    v0, v1 = with_roll(v_at(0))
    kept = kept_z = None
    for y in range(width_y):
        c = functools.partial(coef, y)
        h4, hz4, ez = c(H4), c(HZ4), c(EZ)
        p00, p01 = ez * v0, ez * v1
        if y + 1 < width_y:
            hz, e = c(HZ), c(E)
            n0, n1 = with_roll(u_at(y + 1))
            x0, x1 = with_roll(v_at(y + 1))
            p10, p11 = ez * x0, ez * x1
            side, other = p01 + p11, p00 + p10
            r00 = h4 * u0 - hz * n1 - e * x0 - side
            r10 = h4 * n0 - hz * u1 - e * v0 - side
            r01 = hz4 * u1 - hz * n0 - other - p11
            r11 = hz4 * n1 - hz * u0 - other - p01
        else:
            r00 = h4 * u0 - p01
            r01 = hz4 * u1 - p00
        here = r00 if kept is None else r00 + kept
        moved = r01 if kept_z is None else r01 + kept_z
        yield y, u0, here + pltpu.roll(moved, 1, 1)
        if y + 1 < width_y:
            kept, kept_z = r10, r11
            u0, u1, v0, v1 = n0, n1, x0, x1


def far_rows(width_y, w_at, coef):
    def with_roll(x):
        return x, pltpu.roll(x, WIDTH - 1, 1)

    w0, w1 = with_roll(w_at(0))
    kept = kept_z = None
    for y in range(width_y):
        gz = coef(y, GZ)
        p00, p01 = gz * w0, gz * w1
        if y + 1 < width_y:
            g = coef(y, G)
            z0, z1 = with_roll(w_at(y + 1))
            p10, p11 = gz * z0, gz * z1
            side, other = p01 + p11, p00 + p10
            r00, r10 = g * z0 + side, g * w0 + side
            r01, r11 = other + p11, other + p01
        else:
            r00, r01 = p01, p00
        here = r00 if kept is None else r00 + kept
        moved = r01 if kept_z is None else r01 + kept_z
        yield y, here + pltpu.roll(moved, 1, 1)
        if y + 1 < width_y:
            kept, kept_z = r10, r11
            w0, w1 = z0, z1


def half_step(near_ref, field_ref, before_ref, coef_ref, scale_ref, shift_ref, target_ref, base_ref):
    cols = field_ref.shape[0]
    width_y = field_ref.shape[1] // WIDTH

    def coef(y, place):
        return twice(coef_ref[8 * place : 8 * place + 8, lanes_of(y)])

    def group(i, carry):
        at = rows_of(i)
        rows = near_rows(
            width_y, lambda y: field_ref[at, lanes_of(y)], lambda y: near_ref[at, lanes_of(y)].astype(F32), coef
        )
        shift2 = twice(shift_ref[...])
        for y, u, forces in rows:
            result = 2.0 * (forces * twice(scale_ref[:, lanes_of(y)]) - shift2 * u) - before_ref[at, lanes_of(y)]
            base_ref[at, lanes_of(y)] = result
        return carry

    lax.fori_loop(0, cols // 16, group, 0)


def full_step(last, far_ref, base_ref, coef_ref, scale_ref, out_ref, pay_ref, *heavy_ref):
    cols = base_ref.shape[0]
    width_y = base_ref.shape[1] // WIDTH

    def coef(y, place):
        return twice(coef_ref[8 * place : 8 * place + 8, lanes_of(y)])

    def group(i, carry):
        at = rows_of(i)
        for y, forces in far_rows(width_y, lambda y: far_ref[at, lanes_of(y)].astype(F32), coef):
            result = base_ref[at, lanes_of(y)] - 2.0 * (forces * twice(scale_ref[:, lanes_of(y)]))
            out_ref[at, lanes_of(y)] = result
            pay_ref[at, lanes_of(y)] = result.astype(BF16)
            if last:
                heavy_ref[0][at, lanes_of(y)] = (result * coef(y, MS)).astype(BF16)
        return carry

    lax.fori_loop(0, cols // 16, group, 0)


def dot_nt(a, b):
    return lax.dot_general(a, b, (((1,), (1,)), ((), ())), preferred_element_type=F32)


def spread(ref, lanes, targets, gram):
    parts = ref.shape[0]
    t, g = targets.shape[0] // parts, gram.shape[0] // parts
    for x in range(parts):
        ref[x, :t, lanes] = targets[x * t : (x + 1) * t]
        ref[x, t:, lanes] = gram[x * g : (x + 1) * g]


def halves(x):
    high = x.astype(BF16)
    return high, (x - high.astype(F32)).astype(BF16)


def early(field_ref, own_ref, one_ref, three_ref, target_ref, place_ref, keep_ref, send_ref, all_ref):
    cols = field_ref.shape[0]
    core = place_ref[0]
    all_ref[:cols] = own_ref[...]
    all_ref[cols : 2 * cols] = three_ref[...]
    all_ref[2 * cols : 3 * cols] = jnp.zeros((cols, all_ref.shape[1]), BF16)
    all_ref[3 * cols :] = one_ref[...]
    everything = all_ref[...]
    high, low = halves(field_ref[...])
    gram = dot_nt(high, everything) + dot_nt(low, everything)
    half = target_ref.shape[0] // 2
    for side, ref in ((core, keep_ref), (1 - core, send_ref)):
        spread(ref, slice(None), dot_nt(target_ref[rows_of(side, half), :], everything), gram)


def stiff_rows(core, stiff, lanes, keep_ref, send_ref):
    parts = keep_ref.shape[0]
    g = stiff.shape[0] // parts
    t = keep_ref.shape[1] - g

    def put(ref):
        for x in range(parts):
            ref[x, t:, lanes] = stiff[x * g : (x + 1) * g]

    pl.when(core == 0)(lambda: put(keep_ref))
    pl.when(core != 0)(lambda: put(send_ref))


def half_stiffness(near_ref, field_ref, coef_ref, base_ref):
    cols = field_ref.shape[0]
    width_y = field_ref.shape[1] // WIDTH

    def coef(y, place):
        return twice(coef_ref[8 * place : 8 * place + 8, lanes_of(y)])

    def group(i, carry):
        at = rows_of(i)
        rows = near_rows(
            width_y, lambda y: field_ref[at, lanes_of(y)], lambda y: near_ref[at, lanes_of(y)].astype(F32), coef
        )
        for y, u, forces in rows:
            base_ref[at, lanes_of(y)] = forces
        return carry

    lax.fori_loop(0, cols // 16, group, 0)


def middle(keep_in, send_in, far_ref, base_ref, coef_ref, all_ref, place_ref, keep_ref, send_ref, high_ref, low_ref):
    cols = base_ref.shape[0]
    width_y = base_ref.shape[1] // WIDTH

    def coef(y, place):
        return twice(coef_ref[8 * place : 8 * place + 8, lanes_of(y)])

    def group(i, carry):
        at = rows_of(i)
        for y, forces in far_rows(width_y, lambda y: far_ref[at, lanes_of(y)].astype(F32), coef):
            scaled = (base_ref[at, lanes_of(y)] - forces) * coef(y, MI)
            high_ref[at, lanes_of(y)], low_ref[at, lanes_of(y)] = halves(scaled)
        return carry

    lax.fori_loop(0, cols // 16, group, 0)
    everything = all_ref[...]
    stiff = dot_nt(high_ref[...], everything) + dot_nt(low_ref[...], everything)
    stiff_rows(place_ref[0], stiff, slice(None), keep_ref, send_ref)


def late(keep_in, send_in, two_low_ref, two_high_ref, field_ref, high_ref, low_ref, target_ref, place_ref, keep_ref, send_ref):
    cols = field_ref.shape[0]
    core = place_ref[0]
    two = jnp.concatenate([two_low_ref[...], two_high_ref[...]], 0)
    stiff = dot_nt(high_ref[...], two) + dot_nt(low_ref[...], two)
    high, low = halves(field_ref[...])
    heavy = dot_nt(high, two) + dot_nt(low, two)
    half = target_ref.shape[0] // 2
    lanes = slice(2 * cols, 3 * cols)
    for side, ref in ((core, keep_ref), (1 - core, send_ref)):
        spread(ref, lanes, dot_nt(target_ref[rows_of(side, half), :], two), heavy)
    stiff_rows(core, stiff, lanes, keep_ref, send_ref)


def turned(x, steps, cols):
    groups = x.shape[1] // cols

    def by(k):
        return jnp.concatenate([x[:, (groups - k) * cols :], x[:, : (groups - k) * cols]], 1)

    result = x
    for k in range(1, groups):
        result = jnp.where(steps == k, by(k), result)
    return result


def split(x):
    high = x.astype(BF16)
    return high, (x - high.astype(F32)).astype(BF16)


def dot_split(a, b, dims):
    (ah, al), (bh, bl) = split(a), split(b)
    dot = functools.partial(lax.dot_general, dimension_numbers=(dims, ((), ())), preferred_element_type=F32)
    return dot(ah, bh) + (dot(ah, bl) + dot(al, bh))


def inverse_factor(work_ref, panel, few):
    n = work_ref.shape[0]
    tiles, strips = n // WIDTH, panel // 8
    row = lax.broadcasted_iota(jnp.int32, (8, WIDTH), 0)
    lane = lax.broadcasted_iota(jnp.int32, (8, WIDTH), 1)
    for start in range(0, n, panel):
        lines = [[work_ref[start + 8 * r : start + 8 * r + 8, lanes_of(t)] for r in range(strips)] for t in range(tiles)]
        pivots = [jnp.ones((8, WIDTH), F32)] * strips
        for first in range(0, panel, few):
            columns, factors = [], []
            for place in range(start + first, start + first + few):
                tile, inside = divmod(place, WIDTH)
                spread_out = {
                    r: jnp.broadcast_to(lines[tile][r][:, inside : inside + 1], (8, WIDTH)) for r in range(first // 8, strips)
                }
                columns.append(spread_out)
            for k in range(0, few, 2):
                at, i = divmod(first + k, 8)
                left, right = columns[k], columns[k + 1]
                pivot, below = left[at][i : i + 1], left[at][i + 1 : i + 2]
                beside = right[at][i : i + 1]
                minor = pivot * right[at][i + 1 : i + 2] - below * beside
                over = 1.0 / pivot
                slope, scale = below * over, pivot * (1.0 / minor)
                one = {r: left[r] * over for r in range(at, strips)}
                one[at] = jnp.where(row > i, one[at], 0.0)
                two = {r: (right[r] - one[r] * beside) * scale for r in range(at, strips)}
                two[at] = jnp.where(row > i + 1, two[at], 0.0)
                pivots[at] = jnp.where(row == i, pivot, jnp.where(row == i + 1, minor * over, pivots[at]))
                for l in range(k + 2, few):
                    u = columns[l][at][i : i + 1]
                    v = columns[l][at][i + 1 : i + 2] - slope * u
                    for r in range(at, strips):
                        columns[l][r] = columns[l][r] - one[r] * u - two[r] * v
                factors.append((at, i, one, two, slope))
            for k, (at, i, one, two, slope) in enumerate(factors):
                tile, inside = divmod(start + first + 2 * k, WIDTH)
                for t in range(tiles):
                    u, v = lines[t][at][i : i + 1], lines[t][at][i + 1 : i + 2]
                    if t == tile:
                        u = u + jnp.where(lane[:1] == inside, 1.0, 0.0)
                    v = v - slope * u
                    if t == tile:
                        v = v + jnp.where(lane[:1] == inside + 1, 1.0, 0.0)
                    for r in range(at, strips):
                        lines[t][r] = lines[t][r] - one[r] * u - two[r] * v
        factor_rows = [[] for _ in range(tiles)]
        update_rows = [[] for _ in range(tiles)]
        for r in range(strips):
            scale = 1.0 / jnp.sqrt(pivots[r])
            here = row + start + 8 * r
            for t in range(tiles):
                place = lane + t * WIDTH
                full = jnp.where(place == here, scale, lines[t][r] * scale)
                inverse = jnp.where(place <= here, full, 0.0)
                work_ref[start + 8 * r : start + 8 * r + 8, lanes_of(t)] = inverse
                factor_rows[t].append(full)
                update_rows[t].append(jnp.where((place >= start) & (place < start + panel), inverse, full))
        rest = n - start - panel
        if rest:
            factor, rows = (
                jnp.concatenate([jnp.concatenate(strip, 0) for strip in side], 1) for side in (factor_rows, update_rows)
            )
            update = dot_split(factor, rows, ((0,), (0,)))
            for t in range(tiles):
                old = work_ref[start + panel :, lanes_of(t)]
                place = lax.broadcasted_iota(jnp.int32, old.shape, 1) + t * WIDTH
                old = jnp.where((place >= start) & (place < start + panel), 0.0, old)
                work_ref[start + panel :, lanes_of(t)] = old - update[start + panel :, lanes_of(t)]


def along_z(parts_ref, out_ref):
    total = jnp.sum(parts_ref[...], axis=0)
    planes, rows = out_ref.shape[0], out_ref.shape[1] // 2
    g = (total.shape[0] - planes * rows) // (1 - planes)
    t = rows - g
    gram = total[planes * t :]
    for z in range(planes):
        mine = total[z * t : (z + 1) * t]
        out_ref[z, : 2 * t, :] = jnp.concatenate([mine[:, :WIDTH], mine[:, WIDTH:]], 0)
        out_ref[z, 2 * t : 2 * t + g, :] = gram[:, :WIDTH]
        out_ref[z, 2 * t + g :, :] = gram[:, WIDTH:]


def along_chips(parts_ref, target_ref, gram_ref):
    total = jnp.sum(parts_ref[...], axis=0)
    g = gram_ref.shape[1]
    t = target_ref.shape[1]
    for plane in range(target_ref.shape[0]):
        target_ref[plane] = total[:t]
    for chip in range(gram_ref.shape[0]):
        gram_ref[chip, :, :WIDTH] = total[t : t + g]
        gram_ref[chip, :, WIDTH:] = total[t + g :]


def solve(mine_ref, theirs_ref, place_ref, inverse_ref, ritz_ref, mass_ref, stiff_ref, work_ref):
    core = place_ref[0]
    total = work_ref.shape[0]
    chips, g = mine_ref.shape[:2]
    cols = total // 4
    groups, wide = total // cols, cols // g

    def put(parts_ref, into):
        for q in range(groups):
            for x in range(wide):
                rows = parts_ref[x * groups + q]
                rows = jnp.concatenate([rows[:, total - q * cols :], rows[:, : total - q * cols]], 1) if q else rows
                into[q * cols + x * g : q * cols + (x + 1) * g, :] = rows

    def put_both(first, second):
        put(first, stiff_ref)
        put(second, mass_ref)

    pl.when(core == 0)(lambda: put_both(mine_ref, theirs_ref))
    pl.when(core != 0)(lambda: put_both(theirs_ref, mine_ref))
    gram = mass_ref[...]
    on = lax.broadcasted_iota(jnp.int32, gram.shape, 0) == lax.broadcasted_iota(jnp.int32, gram.shape, 1)
    diagonal = jnp.where(on, gram, 0.0)
    across = 1.0 / jnp.sqrt(jnp.sum(diagonal, axis=0, keepdims=True))
    down = 1.0 / jnp.sqrt(jnp.sum(diagonal, axis=1, keepdims=True))
    work_ref[...] = gram * across * down
    inverse_factor(work_ref, 64, 16)
    inverse = work_ref[...] * across
    inverse_ref[...] = inverse
    ritz_ref[...] = dot_split(dot_split(inverse, stiff_ref[...], ((1,), (1,))), inverse, ((1,), (1,)))


def participate(targets_in, inverse_ref, place_ref, keep_ref, send_ref, targets_ref):
    core, col, me = place_ref[0], place_ref[1], place_ref[2]
    groups = 4
    cols = inverse_ref.shape[0] // groups
    deep, wide = 8, targets_in.shape[0] // 8
    t = targets_in.shape[1] // 2
    for x in range(wide):
        for tile in range(2):
            rows = [targets_in[z * wide + x, tile * t : (tile + 1) * t] for z in range(deep)]
            targets_ref[x * deep * t : (x + 1) * deep * t, lanes_of(tile)] = jnp.concatenate(rows, 0)
    rows = inverse_ref[pl.ds(pl.multiple_of(me // 2 * 8, 8), 8), :]
    part = dot_split(turned(rows, lax.rem(groups - col, groups), cols), targets_ref[...], ((1,), (1,)))
    keep_ref[...] = jnp.where(core == 0, part[:4], part[4:])
    send_ref[...] = jnp.where(core == 0, part[4:], part[:4])


def combine(field_ref, own_ref, three_ref, two_low_ref, two_high_ref, one_ref, coef_ref, inverse_ref, place_ref, modes_ref):
    col = place_ref[1]
    cols = field_ref.shape[0]
    groups = inverse_ref.shape[0] // cols
    width_y = field_ref.shape[1] // WIDTH
    norm = jnp.float32(np.sqrt(np.float32(64 * width_y * WIDTH)))
    back = lax.rem(groups - col, groups)
    weights = turned(inverse_ref[rows_of(col, cols), :], back, cols)
    block = weights[:, :cols].astype(BF16)
    high, low = split(weights)
    held = (own_ref, three_ref, two_low_ref, two_high_ref, one_ref)
    for y in range(width_y):
        at = lanes_of(y)
        everything = jnp.concatenate([ref[:, at] for ref in held], 0)
        mass = jnp.concatenate([coef_ref[8 * MS : 8 * MS + 8, at]] * (cols // 8), axis=0)
        light = jnp.concatenate([coef_ref[8 * MI : 8 * MI + 8, at]] * (cols // 8), axis=0)
        rest = (field_ref[:, at] * mass - own_ref[:, at].astype(F32)).astype(BF16)
        result = (
            jnp.dot(high, everything, preferred_element_type=F32)
            + jnp.dot(low, everything, preferred_element_type=F32)
            + jnp.dot(block, rest, preferred_element_type=F32)
        )
        modes_ref[pl.ds(y, cols, stride=width_y), :] = result * light * norm


def local(start_block, node_mass, material_ids, moduli_table, influence):
    cols, _, width_y, width_z = start_block.shape
    lanes = width_y * width_z
    doms, groups = lax.axis_size("dom"), lax.axis_size("col")
    total_cols = cols * groups
    me, col = lax.axis_index("dom"), lax.axis_index("col")
    core = me % 2
    pair = [(i, i ^ 1) for i in range(doms)]
    across = [(i, i + 1 if i % 2 else i - 1) for i in range(1, doms - 1)]
    wide, deep = 4, 8
    place_of = np.arange(doms).reshape(deep, wide, 2)
    plane_groups = [place_of[:, :, c].reshape(-1).tolist() for c in range(2)]
    x_groups = [place_of[z, :, c].tolist() for z in range(deep) for c in range(2)]
    z_groups = [place_of[:, x, c].tolist() for x in range(wide) for c in range(2)]
    chip_of = place_of[..., None] * groups + np.arange(groups)
    chip_groups = [chip_of[z, :, c].reshape(-1).tolist() for z in range(deep) for c in range(2)]

    def exchange(payload):
        near = lax.ppermute(payload, "dom", pair)
        return near, lax.ppermute(payload, "dom", across)

    def col_ring(step):
        return [(i, (i + step) % groups) for i in range(groups)]

    place = jnp.stack([core, col, me]).astype(jnp.int32)
    targets = influence.reshape(influence.shape[0], lanes)

    base, pay, least = pl.pallas_call(
        prepare,
        out_shape=(
            shape(cols + 24, lanes),
            shape(cols + 16, lanes, BF16),
            jax.ShapeDtypeStruct((doms, 1, WIDTH), F32),
        ),
        in_specs=[pl.BlockSpec(memory_space=pltpu.HBM)] * 4,
        out_specs=(VMEM,) * 3,
        scratch_shapes=[
            pltpu.VMEM((cols * width_y, width_z), F32),
            pltpu.VMEM((width_y, width_z), F32),
            pltpu.VMEM((width_y, width_z), jnp.int32),
            pltpu.VMEM((1, moduli_table.shape[0]), F32),
            pltpu.SemaphoreType.DMA((4,)),
        ],
        compiler_params=pltpu.CompilerParams(vmem_limit_bytes=62398000),
    )(
        start_block.reshape(cols * width_y, width_z),
        node_mass.reshape(width_y, width_z),
        material_ids.reshape(width_y, width_z),
        moduli_table.reshape(1, -1),
    )
    near, far = exchange(pay)
    least = lax.all_to_all(least, "dom", 0, 0, tiled=True)
    forces, coef, field, top = pl.pallas_call(
        first_forces,
        out_shape=(shape(cols, lanes), shape(72, lanes), shape(cols, lanes), shape(8, WIDTH)),
        in_specs=[VMEM] * 3 + [SMEM],
        out_specs=(VMEM,) * 4,
        compiler_params=PARAMS,
    )(far, near, base, place)
    current, pay, scale, shift = pl.pallas_call(
        first_step,
        out_shape=(shape(cols, lanes), shape(cols, lanes, BF16), shape(8, lanes), shape(8, WIDTH)),
        in_specs=[VMEM] * 5,
        out_specs=(VMEM,) * 4,
        compiler_params=PARAMS,
    )(least, forces, field, coef, top)
    previous = field
    for step in range(DEGREE - 1):
        last = step == DEGREE - 2
        near, far = exchange(pay)
        partly = pl.pallas_call(
            half_step,
            out_shape=shape(cols, lanes),
            in_specs=[VMEM] * 7,
            out_specs=VMEM,
            compiler_params=PARAMS,
        )(near, current, previous, coef, scale, shift, targets if last else shift)
        outs = pl.pallas_call(
            functools.partial(full_step, last),
            out_shape=(shape(cols, lanes),) + (shape(cols, lanes, BF16),) * (2 if last else 1),
            in_specs=[VMEM] * 4,
            out_specs=(VMEM,) * (3 if last else 2),
            compiler_params=PARAMS,
        )(far, partly, coef, scale)
        previous, current, pay = current, outs[0], outs[1]
    heavy = outs[2]
    near, far = exchange(pay)
    one, three = lax.ppermute(heavy, "col", col_ring(1)), lax.ppermute(heavy, "col", col_ring(3))
    two_low = lax.ppermute(one[: cols // 2], "col", col_ring(1))
    two_high = lax.ppermute(three[cols // 2 :], "col", col_ring(3))
    half = targets.shape[0] // 2
    t_rows, g_rows = half // wide, cols // wide
    chunk = jax.ShapeDtypeStruct((wide, t_rows + g_rows, total_cols), F32)
    keep, send, most = pl.pallas_call(
        early,
        out_shape=(chunk, chunk, shape(total_cols, lanes, BF16)),
        in_specs=[VMEM] * 5 + [SMEM],
        out_specs=(VMEM,) * 3,
        compiler_params=PARAMS,
    )(current, heavy, one, three, targets, place)
    partly = pl.pallas_call(
        half_stiffness,
        out_shape=shape(cols, lanes),
        in_specs=[VMEM] * 3,
        out_specs=VMEM,
        compiler_params=PARAMS,
    )(near, current, coef)
    split_field = (shape(cols, lanes, BF16),) * 2
    keep, send, high, low = pl.pallas_call(
        middle,
        out_shape=(chunk, chunk) + split_field,
        in_specs=[VMEM] * 6 + [SMEM],
        out_specs=(VMEM,) * 4,
        input_output_aliases={0: 0, 1: 1},
        compiler_params=PARAMS,
    )(keep, send, far, partly, coef, most, place)
    keep, send = pl.pallas_call(
        late,
        out_shape=(chunk, chunk),
        in_specs=[VMEM] * 8 + [SMEM],
        out_specs=(VMEM,) * 2,
        input_output_aliases={0: 0, 1: 1},
        compiler_params=PARAMS,
    )(keep, send, two_low, two_high, current, high, low, targets, place)

    summed = keep + lax.ppermute(send, "dom", pair)
    summed = lax.all_to_all(summed, "dom", 0, 0, tiled=True, axis_index_groups=x_groups)
    summed = pl.pallas_call(
        along_z,
        out_shape=jax.ShapeDtypeStruct((deep, 2 * (t_rows // deep + g_rows), WIDTH), F32),
        in_specs=[VMEM],
        out_specs=VMEM,
        compiler_params=PARAMS,
    )(summed)
    summed = lax.all_to_all(summed, "dom", 0, 0, tiled=True, axis_index_groups=z_groups)
    few = t_rows // deep
    target, gram = pl.pallas_call(
        along_chips,
        out_shape=(
            jax.ShapeDtypeStruct((deep * wide, 2 * few, WIDTH), F32),
            jax.ShapeDtypeStruct((wide * groups, g_rows, total_cols), F32),
        ),
        in_specs=[VMEM],
        out_specs=(VMEM,) * 2,
        compiler_params=PARAMS,
    )(summed)
    mine = lax.all_to_all(gram, ("dom", "col"), 0, 0, tiled=True, axis_index_groups=chip_groups)
    theirs = lax.ppermute(mine, "dom", pair)
    target = lax.all_to_all(target, "dom", 0, 0, tiled=True, axis_index_groups=plane_groups)
    inverse, ritz_matrix = pl.pallas_call(
        solve,
        out_shape=(shape(total_cols, total_cols),) * 2,
        in_specs=[VMEM] * 2 + [SMEM],
        out_specs=(VMEM,) * 2,
        scratch_shapes=[pltpu.VMEM((total_cols, total_cols), F32)] * 3,
        compiler_params=PARAMS,
    )(mine, theirs, place)
    part_rows = total_cols // doms
    kept, sent = pl.pallas_call(
        participate,
        out_shape=(shape(part_rows, half),) * 2,
        in_specs=[VMEM] * 2 + [SMEM],
        out_specs=(VMEM,) * 2,
        scratch_shapes=[pltpu.VMEM((half, total_cols), F32)],
        compiler_params=PARAMS,
    )(target, inverse, place)
    got = lax.ppermute(sent, "dom", pair)
    modes = pl.pallas_call(
        combine,
        out_shape=shape(cols * width_y, width_z),
        in_specs=[VMEM] * 8 + [SMEM],
        out_specs=VMEM,
        compiler_params=PARAMS,
    )(current, heavy, three, two_low, two_high, one, coef, inverse, place)
    first = core == 0
    participation = jnp.concatenate([jnp.where(first, kept, got), jnp.where(first, got, kept)], 1)
    return (modes.reshape(start_block.shape), ritz_matrix, participation)


def solution(mesh):
    placed = (
        P("col", "dom", None, None),
        P("dom", None, None),
        P("dom", None, None),
        P(),
        P("col", "dom", None, None),
    )
    return jax.shard_map(
        local,
        mesh=mesh,
        in_specs=placed,
        out_specs=(P("col", "dom", None, None), P(), P("dom", "col")),
        check_vma=False,
    )
```

```python
import functools

import jax
import jax.numpy as jnp
import numpy as np
from jax import lax
from jax.experimental import pallas as pl
from jax.experimental.pallas import tpu as pltpu
from jax.sharding import PartitionSpec as P

DEGREE = 4
LOW_RATIO = 0.02
F32, BF16 = jnp.float32, jnp.bfloat16
VMEM = pl.BlockSpec(memory_space=pltpu.VMEM)
SMEM = pl.BlockSpec(memory_space=pltpu.SMEM)
WIDTH = 128
PARAMS = pltpu.CompilerParams(vmem_limit_bytes=24 * 1024 * 1024)
H4, HZ, HZ4, E, EZ, G, GZ, MI, MS = range(9)


def shape(rows, lanes, dtype=F32):
    return jax.ShapeDtypeStruct((rows, lanes), dtype)


def lanes_of(y):
    return slice(y * WIDTH, (y + 1) * WIDTH)


def rows_of(group, size=16):
    return pl.ds(pl.multiple_of(group * size, size), size)


def twice(c):
    return jnp.concatenate([c, c], axis=0)


def stiffness_rows(width_y, u_at, v_at, w_at, coef):
    def with_roll(x):
        return x, pltpu.roll(x, WIDTH - 1, 1)

    u0, u1 = with_roll(u_at(0))
    v0, v1 = with_roll(v_at(0))
    w0, w1 = with_roll(w_at(0))
    kept = kept_z = None
    for y in range(width_y):
        c = functools.partial(coef, y)
        h4, hz, hz4 = c(H4), c(HZ), c(HZ4)
        ez, gz = c(EZ), c(GZ)
        p00 = ez * v0 + gz * w0
        p01 = ez * v1 + gz * w1
        if y + 1 < width_y:
            e, g = c(E), c(G)
            n0, n1 = with_roll(u_at(y + 1))
            x0, x1 = with_roll(v_at(y + 1))
            z0, z1 = with_roll(w_at(y + 1))
            p10 = ez * x0 + gz * z0
            p11 = ez * x1 + gz * z1
            q00 = e * v0 + g * w0
            q10 = e * x0 + g * z0
            side, other = p01 + p11, p00 + p10
            r00 = h4 * u0 - hz * n1 - q10 - side
            r10 = h4 * n0 - hz * u1 - q00 - side
            r01 = hz4 * u1 - hz * n0 - other - p11
            r11 = hz4 * n1 - hz * u0 - other - p01
        else:
            r00 = h4 * u0 - p01
            r01 = hz4 * u1 - p00
        here = r00 if kept is None else r00 + kept
        moved = r01 if kept_z is None else r01 + kept_z
        yield y, u0, here + pltpu.roll(moved, 1, 1)
        if y + 1 < width_y:
            kept, kept_z = r10, r11
            u0, u1, v0, v1, w0, w1 = n0, n1, x0, x1, z0, z1


def prepare(start_hbm, mass_hbm, ids_hbm, table_hbm, base_ref, pay_ref, least_ref, start_ref, mass_ref, ids_ref, table_ref, sems):
    pairs = ((mass_hbm, mass_ref), (ids_hbm, ids_ref), (table_hbm, table_ref), (start_hbm, start_ref))
    copies = [pltpu.make_async_copy(source, target, sems.at[i]) for i, (source, target) in enumerate(pairs)]
    for copy in copies:
        copy.start()
    cols = base_ref.shape[0] - 24
    width_y = ids_ref.shape[0]
    for copy in copies[:3]:
        copy.wait()
    mass, ids, table = mass_ref[...], ids_ref[...], table_ref[...]
    base_ref[cols + 16 :, :] = jnp.broadcast_to(jnp.max(table, axis=1, keepdims=True), (8, base_ref.shape[1]))
    least = jnp.min(jnp.min(mass, axis=0, keepdims=True), axis=1, keepdims=True)
    least_ref[...] = jnp.broadcast_to(least[None], least_ref.shape)
    moduli = jnp.zeros(ids.shape, F32)
    for k in range(table.shape[1]):
        moduli = jnp.where(ids == k, table[:, k : k + 1], moduli)
    moduli = moduli / 12.0
    high = moduli.astype(BF16).astype(F32)
    middle = (moduli - high).astype(BF16).astype(F32)
    low = moduli - high - middle
    pad = jnp.zeros((13, WIDTH), F32)
    for y in range(width_y):
        at = lanes_of(y)
        base_ref[cols : cols + 8, at] = jnp.broadcast_to(moduli[y : y + 1], (8, WIDTH))
        base_ref[cols + 8 : cols + 16, at] = jnp.broadcast_to(mass[y : y + 1], (8, WIDTH))
        parts = jnp.concatenate([high[y : y + 1], middle[y : y + 1], low[y : y + 1], pad], 0)
        pay_ref[cols:, at] = parts.astype(BF16)
    copies[3].wait()
    for y in range(width_y):
        plane = start_ref[pl.ds(y, cols, stride=width_y), :]
        base_ref[:cols, lanes_of(y)] = plane
        pay_ref[:cols, lanes_of(y)] = plane.astype(BF16)


def first_forces(far_ref, near_ref, base_ref, place_ref, forces_ref, coef_ref, field_ref, top_ref):
    cols = field_ref.shape[0]
    top_ref[...] = base_ref[cols + 16 :, :WIDTH]
    width_y = field_ref.shape[1] // WIDTH
    inner = lax.broadcasted_iota(jnp.int32, (8, WIDTH), 1) < WIDTH - 1
    first = place_ref[0] == 0
    for y in range(width_y):
        at = lanes_of(y)
        own, mass = base_ref[cols : cols + 8, at], base_ref[cols + 8 : cols + 16, at]
        parts = jnp.where(first, far_ref[cols:, at].astype(F32), near_ref[cols:, at].astype(F32))
        below = jnp.broadcast_to(parts[0:1] + parts[1:2] + parts[2:3], (8, WIDTH))
        near, far = jnp.where(first, own, below), jnp.where(first, below, own)
        both = near + far
        both_z = jnp.where(inner, both, 0.0)
        values = {
            H4: 4.0 * both,
            HZ: both_z,
            HZ4: 4.0 * both_z,
            E: near,
            EZ: jnp.where(inner, near, 0.0),
            G: far,
            GZ: jnp.where(inner, far, 0.0),
            MI: 1.0 / mass,
            MS: mass,
        }
        for place, value in values.items():
            coef_ref[8 * place : 8 * place + 8, at] = value

    def coef(y, place):
        return twice(coef_ref[8 * place : 8 * place + 8, lanes_of(y)])

    def group(i, carry):
        at = rows_of(i)
        rows = stiffness_rows(
            width_y,
            lambda y: base_ref[at, lanes_of(y)],
            lambda y: near_ref[at, lanes_of(y)].astype(F32),
            lambda y: far_ref[at, lanes_of(y)].astype(F32),
            coef,
        )
        for y, u, forces in rows:
            forces_ref[at, lanes_of(y)] = forces
            field_ref[at, lanes_of(y)] = u
        return carry

    lax.fori_loop(0, cols // 16, group, 0)


def first_step(least_ref, forces_ref, field_ref, coef_ref, top_ref, out_ref, pay_ref, scale_ref, shift_ref):
    cols = field_ref.shape[0]
    width_y = field_ref.shape[1] // WIDTH
    least = jnp.min(jnp.min(least_ref[...], axis=0), axis=1, keepdims=True)
    upper = 16.0 / 3.0 * top_ref[...] / least
    lower = LOW_RATIO * upper
    half = (upper - lower) / 2.0
    shift = (upper + lower) / 2.0 / half
    shift_ref[...] = shift
    for y in range(width_y):
        at = lanes_of(y)
        scale = 1.0 / (coef_ref[8 * MS : 8 * MS + 8, at] * half)
        scale_ref[:, at] = scale
        scale, shifts = (jnp.concatenate([x] * (cols // 8), 0) for x in (scale, shift))
        result = forces_ref[:, at] * scale - shifts * field_ref[:, at]
        out_ref[:, at] = result
        pay_ref[:, at] = result.astype(BF16)


def near_rows(width_y, u_at, v_at, coef):
    def with_roll(x):
        return x, pltpu.roll(x, WIDTH - 1, 1)

    u0, u1 = with_roll(u_at(0))
    v0, v1 = with_roll(v_at(0))
    kept = kept_z = None
    for y in range(width_y):
        c = functools.partial(coef, y)
        h4, hz4, ez = c(H4), c(HZ4), c(EZ)
        p00, p01 = ez * v0, ez * v1
        if y + 1 < width_y:
            hz, e = c(HZ), c(E)
            n0, n1 = with_roll(u_at(y + 1))
            x0, x1 = with_roll(v_at(y + 1))
            p10, p11 = ez * x0, ez * x1
            side, other = p01 + p11, p00 + p10
            r00 = h4 * u0 - hz * n1 - e * x0 - side
            r10 = h4 * n0 - hz * u1 - e * v0 - side
            r01 = hz4 * u1 - hz * n0 - other - p11
            r11 = hz4 * n1 - hz * u0 - other - p01
        else:
            r00 = h4 * u0 - p01
            r01 = hz4 * u1 - p00
        here = r00 if kept is None else r00 + kept
        moved = r01 if kept_z is None else r01 + kept_z
        yield y, u0, here + pltpu.roll(moved, 1, 1)
        if y + 1 < width_y:
            kept, kept_z = r10, r11
            u0, u1, v0, v1 = n0, n1, x0, x1


def far_rows(width_y, w_at, coef):
    def with_roll(x):
        return x, pltpu.roll(x, WIDTH - 1, 1)

    w0, w1 = with_roll(w_at(0))
    kept = kept_z = None
    for y in range(width_y):
        gz = coef(y, GZ)
        p00, p01 = gz * w0, gz * w1
        if y + 1 < width_y:
            g = coef(y, G)
            z0, z1 = with_roll(w_at(y + 1))
            p10, p11 = gz * z0, gz * z1
            side, other = p01 + p11, p00 + p10
            r00, r10 = g * z0 + side, g * w0 + side
            r01, r11 = other + p11, other + p01
        else:
            r00, r01 = p01, p00
        here = r00 if kept is None else r00 + kept
        moved = r01 if kept_z is None else r01 + kept_z
        yield y, here + pltpu.roll(moved, 1, 1)
        if y + 1 < width_y:
            kept, kept_z = r10, r11
            w0, w1 = z0, z1


def half_step(near_ref, field_ref, before_ref, coef_ref, scale_ref, shift_ref, target_ref, base_ref):
    cols = field_ref.shape[0]
    width_y = field_ref.shape[1] // WIDTH

    def coef(y, place):
        return twice(coef_ref[8 * place : 8 * place + 8, lanes_of(y)])

    def group(i, carry):
        at = rows_of(i)
        rows = near_rows(
            width_y, lambda y: field_ref[at, lanes_of(y)], lambda y: near_ref[at, lanes_of(y)].astype(F32), coef
        )
        shift2 = twice(shift_ref[...])
        for y, u, forces in rows:
            result = 2.0 * (forces * twice(scale_ref[:, lanes_of(y)]) - shift2 * u) - before_ref[at, lanes_of(y)]
            base_ref[at, lanes_of(y)] = result
        return carry

    lax.fori_loop(0, cols // 16, group, 0)


def full_step(last, far_ref, base_ref, coef_ref, scale_ref, out_ref, pay_ref, *heavy_ref):
    cols = base_ref.shape[0]
    width_y = base_ref.shape[1] // WIDTH

    def coef(y, place):
        return twice(coef_ref[8 * place : 8 * place + 8, lanes_of(y)])

    def group(i, carry):
        at = rows_of(i)
        for y, forces in far_rows(width_y, lambda y: far_ref[at, lanes_of(y)].astype(F32), coef):
            result = base_ref[at, lanes_of(y)] - 2.0 * (forces * twice(scale_ref[:, lanes_of(y)]))
            out_ref[at, lanes_of(y)] = result
            pay_ref[at, lanes_of(y)] = result.astype(BF16)
            if last:
                heavy_ref[0][at, lanes_of(y)] = (result * coef(y, MS)).astype(BF16)
        return carry

    lax.fori_loop(0, cols // 16, group, 0)


def dot_nt(a, b):
    return lax.dot_general(a, b, (((1,), (1,)), ((), ())), preferred_element_type=F32)


def spread(ref, lanes, targets, gram):
    parts = ref.shape[0]
    t, g = targets.shape[0] // parts, gram.shape[0] // parts
    for x in range(parts):
        ref[x, :t, lanes] = targets[x * t : (x + 1) * t]
        ref[x, t:, lanes] = gram[x * g : (x + 1) * g]


def halves(x):
    high = x.astype(BF16)
    return high, (x - high.astype(F32)).astype(BF16)


def dot_both(high, low, b):
    rows = high.shape[0]
    result = dot_nt(jnp.concatenate([high, low], 0), b)
    return result[:rows] + result[rows:]


def by_core(core, keep_ref, send_ref, put):
    pl.when(core == 0)(lambda: put(keep_ref, send_ref))
    pl.when(core != 0)(lambda: put(send_ref, keep_ref))


def early(field_ref, own_ref, one_ref, three_ref, target_ref, place_ref, keep_ref, send_ref, all_ref):
    cols = field_ref.shape[0]
    core = place_ref[0]
    all_ref[:cols] = own_ref[...]
    all_ref[cols : 2 * cols] = three_ref[...]
    all_ref[2 * cols : 3 * cols] = jnp.zeros((cols, all_ref.shape[1]), BF16)
    all_ref[3 * cols :] = one_ref[...]
    everything = all_ref[...]
    high, low = halves(field_ref[...])
    gram = dot_both(high, low, everything)
    half = target_ref.shape[0] // 2
    targets = dot_nt(target_ref[...], everything)

    def put(first, second):
        spread(first, slice(None), targets[:half], gram)
        spread(second, slice(None), targets[half:], gram)

    by_core(core, keep_ref, send_ref, put)


def stiff_rows(core, stiff, lanes, keep_ref, send_ref):
    parts = keep_ref.shape[0]
    g = stiff.shape[0] // parts
    t = keep_ref.shape[1] - g

    def put(ref):
        for x in range(parts):
            ref[x, t:, lanes] = stiff[x * g : (x + 1) * g]

    pl.when(core == 0)(lambda: put(keep_ref))
    pl.when(core != 0)(lambda: put(send_ref))


def half_stiffness(near_ref, field_ref, coef_ref, base_ref):
    cols = field_ref.shape[0]
    width_y = field_ref.shape[1] // WIDTH

    def coef(y, place):
        return twice(coef_ref[8 * place : 8 * place + 8, lanes_of(y)])

    def group(i, carry):
        at = rows_of(i)
        rows = near_rows(
            width_y, lambda y: field_ref[at, lanes_of(y)], lambda y: near_ref[at, lanes_of(y)].astype(F32), coef
        )
        for y, u, forces in rows:
            base_ref[at, lanes_of(y)] = forces
        return carry

    lax.fori_loop(0, cols // 16, group, 0)


def middle(keep_in, send_in, far_ref, base_ref, coef_ref, all_ref, place_ref, keep_ref, send_ref, high_ref, low_ref):
    cols = base_ref.shape[0]
    width_y = base_ref.shape[1] // WIDTH

    def coef(y, place):
        return twice(coef_ref[8 * place : 8 * place + 8, lanes_of(y)])

    def group(i, carry):
        at = rows_of(i)
        for y, forces in far_rows(width_y, lambda y: far_ref[at, lanes_of(y)].astype(F32), coef):
            scaled = (base_ref[at, lanes_of(y)] - forces) * coef(y, MI)
            high_ref[at, lanes_of(y)], low_ref[at, lanes_of(y)] = halves(scaled)
        return carry

    lax.fori_loop(0, cols // 16, group, 0)
    everything = all_ref[...]
    stiff = dot_both(high_ref[...], low_ref[...], everything)
    stiff_rows(place_ref[0], stiff, slice(None), keep_ref, send_ref)


def late(keep_in, send_in, two_low_ref, two_high_ref, field_ref, high_ref, low_ref, target_ref, place_ref, keep_ref, send_ref):
    cols = field_ref.shape[0]
    core = place_ref[0]
    two = jnp.concatenate([two_low_ref[...], two_high_ref[...]], 0)
    high, low = halves(field_ref[...])
    grams = dot_nt(jnp.concatenate([high_ref[...], low_ref[...], high, low], 0), two)
    stiff = grams[:cols] + grams[cols : 2 * cols]
    heavy = grams[2 * cols : 3 * cols] + grams[3 * cols :]
    half = target_ref.shape[0] // 2
    lanes = slice(2 * cols, 3 * cols)
    targets = dot_nt(target_ref[...], two)

    def put(first, second):
        spread(first, lanes, targets[:half], stiff)
        spread(second, lanes, targets[half:], heavy)

    by_core(core, keep_ref, send_ref, put)


def turned(x, steps, cols):
    groups = x.shape[1] // cols

    def by(k):
        return jnp.concatenate([x[:, (groups - k) * cols :], x[:, : (groups - k) * cols]], 1)

    result = x
    for k in range(1, groups):
        result = jnp.where(steps == k, by(k), result)
    return result


def split(x):
    high = x.astype(BF16)
    return high, (x - high.astype(F32)).astype(BF16)


def dot_split(a, b, dims):
    (ah, al), (bh, bl) = split(a), split(b)
    dot = functools.partial(lax.dot_general, dimension_numbers=(dims, ((), ())), preferred_element_type=F32)
    return dot(ah, bh) + (dot(ah, bl) + dot(al, bh))


def inverse_factor(work_ref, panel, few):
    n = work_ref.shape[0]
    tiles, strips = n // WIDTH, panel // 8
    row = lax.broadcasted_iota(jnp.int32, (8, WIDTH), 0)
    lane = lax.broadcasted_iota(jnp.int32, (8, WIDTH), 1)
    for start in range(0, n, panel):
        lines = [[work_ref[start + 8 * r : start + 8 * r + 8, lanes_of(t)] for r in range(strips)] for t in range(tiles)]
        pivots = [jnp.ones((8, WIDTH), F32)] * strips
        for first in range(0, panel, few):
            columns, factors = [], []
            for place in range(start + first, start + first + few):
                tile, inside = divmod(place, WIDTH)
                spread_out = {
                    r: jnp.broadcast_to(lines[tile][r][:, inside : inside + 1], (8, WIDTH)) for r in range(first // 8, strips)
                }
                columns.append(spread_out)
            for k in range(0, few, 2):
                at, i = divmod(first + k, 8)
                left, right = columns[k], columns[k + 1]
                pivot, below = left[at][i : i + 1], left[at][i + 1 : i + 2]
                beside = right[at][i : i + 1]
                minor = pivot * right[at][i + 1 : i + 2] - below * beside
                over = 1.0 / pivot
                slope, scale = below * over, pivot * (1.0 / minor)
                one = {r: left[r] * over for r in range(at, strips)}
                one[at] = jnp.where(row > i, one[at], 0.0)
                two = {r: (right[r] - one[r] * beside) * scale for r in range(at, strips)}
                two[at] = jnp.where(row > i + 1, two[at], 0.0)
                pivots[at] = jnp.where(row == i, pivot, jnp.where(row == i + 1, minor * over, pivots[at]))
                for l in range(k + 2, few):
                    u = columns[l][at][i : i + 1]
                    v = columns[l][at][i + 1 : i + 2] - slope * u
                    for r in range(at, strips):
                        columns[l][r] = columns[l][r] - one[r] * u - two[r] * v
                factors.append((at, i, one, two, slope))
            for k, (at, i, one, two, slope) in enumerate(factors):
                tile, inside = divmod(start + first + 2 * k, WIDTH)
                for t in range(tiles):
                    u, v = lines[t][at][i : i + 1], lines[t][at][i + 1 : i + 2]
                    if t == tile:
                        u = u + jnp.where(lane[:1] == inside, 1.0, 0.0)
                    v = v - slope * u
                    if t == tile:
                        v = v + jnp.where(lane[:1] == inside + 1, 1.0, 0.0)
                    for r in range(at, strips):
                        lines[t][r] = lines[t][r] - one[r] * u - two[r] * v
        factor_rows = [[] for _ in range(tiles)]
        update_rows = [[] for _ in range(tiles)]
        for r in range(strips):
            scale = 1.0 / jnp.sqrt(pivots[r])
            here = row + start + 8 * r
            for t in range(tiles):
                place = lane + t * WIDTH
                full = jnp.where(place == here, scale, lines[t][r] * scale)
                inverse = jnp.where(place <= here, full, 0.0)
                work_ref[start + 8 * r : start + 8 * r + 8, lanes_of(t)] = inverse
                factor_rows[t].append(full)
                update_rows[t].append(jnp.where((place >= start) & (place < start + panel), inverse, full))
        rest = n - start - panel
        if rest:
            factor, rows = (
                jnp.concatenate([jnp.concatenate(strip, 0) for strip in side], 1) for side in (factor_rows, update_rows)
            )
            update = dot_split(factor, rows, ((0,), (0,)))
            for t in range(tiles):
                old = work_ref[start + panel :, lanes_of(t)]
                place = lax.broadcasted_iota(jnp.int32, old.shape, 1) + t * WIDTH
                old = jnp.where((place >= start) & (place < start + panel), 0.0, old)
                work_ref[start + panel :, lanes_of(t)] = old - update[start + panel :, lanes_of(t)]


def along_z(parts_ref, out_ref):
    total = jnp.sum(parts_ref[...], axis=0)
    planes, rows = out_ref.shape[0], out_ref.shape[1] // 2
    g = (total.shape[0] - planes * rows) // (1 - planes)
    t = rows - g
    gram = total[planes * t :]
    for z in range(planes):
        mine = total[z * t : (z + 1) * t]
        out_ref[z, : 2 * t, :] = jnp.concatenate([mine[:, :WIDTH], mine[:, WIDTH:]], 0)
        out_ref[z, 2 * t : 2 * t + g, :] = gram[:, :WIDTH]
        out_ref[z, 2 * t + g :, :] = gram[:, WIDTH:]


def along_chips(parts_ref, target_ref, gram_ref):
    total = jnp.sum(parts_ref[...], axis=0)
    g = gram_ref.shape[1]
    t = target_ref.shape[1]
    for plane in range(target_ref.shape[0]):
        target_ref[plane] = total[:t]
    for chip in range(gram_ref.shape[0]):
        gram_ref[chip, :, :WIDTH] = total[t : t + g]
        gram_ref[chip, :, WIDTH:] = total[t + g :]


def solve(mine_ref, theirs_ref, place_ref, inverse_ref, ritz_ref, mass_ref, stiff_ref, work_ref):
    core = place_ref[0]
    total = work_ref.shape[0]
    chips, g = mine_ref.shape[:2]
    cols = total // 4
    groups, wide = total // cols, cols // g

    def put(parts_ref, into):
        for q in range(groups):
            for x in range(wide):
                rows = parts_ref[x * groups + q]
                rows = jnp.concatenate([rows[:, total - q * cols :], rows[:, : total - q * cols]], 1) if q else rows
                into[q * cols + x * g : q * cols + (x + 1) * g, :] = rows

    def put_both(first, second):
        put(first, stiff_ref)
        put(second, mass_ref)

    pl.when(core == 0)(lambda: put_both(mine_ref, theirs_ref))
    pl.when(core != 0)(lambda: put_both(theirs_ref, mine_ref))
    gram = mass_ref[...]
    on = lax.broadcasted_iota(jnp.int32, gram.shape, 0) == lax.broadcasted_iota(jnp.int32, gram.shape, 1)
    diagonal = jnp.where(on, gram, 0.0)
    across = 1.0 / jnp.sqrt(jnp.sum(diagonal, axis=0, keepdims=True))
    down = 1.0 / jnp.sqrt(jnp.sum(diagonal, axis=1, keepdims=True))
    work_ref[...] = gram * across * down
    inverse_factor(work_ref, 64, 16)
    inverse = work_ref[...] * across
    inverse_ref[...] = inverse
    ritz_ref[...] = dot_split(dot_split(inverse, stiff_ref[...], ((1,), (1,))), inverse, ((1,), (1,)))


def participate(targets_in, inverse_ref, place_ref, keep_ref, send_ref, targets_ref):
    core, col, me = place_ref[0], place_ref[1], place_ref[2]
    groups = 4
    cols = inverse_ref.shape[0] // groups
    deep, wide = 8, targets_in.shape[0] // 8
    t = targets_in.shape[1] // 2
    for x in range(wide):
        for tile in range(2):
            rows = [targets_in[z * wide + x, tile * t : (tile + 1) * t] for z in range(deep)]
            targets_ref[x * deep * t : (x + 1) * deep * t, lanes_of(tile)] = jnp.concatenate(rows, 0)
    rows = inverse_ref[pl.ds(pl.multiple_of(me // 2 * 8, 8), 8), :]
    part = dot_split(turned(rows, lax.rem(groups - col, groups), cols), targets_ref[...], ((1,), (1,)))
    keep_ref[...] = jnp.where(core == 0, part[:4], part[4:])
    send_ref[...] = jnp.where(core == 0, part[4:], part[:4])


def combine(field_ref, own_ref, three_ref, two_low_ref, two_high_ref, one_ref, coef_ref, inverse_ref, place_ref, modes_ref):
    col = place_ref[1]
    cols = field_ref.shape[0]
    groups = inverse_ref.shape[0] // cols
    width_y = field_ref.shape[1] // WIDTH
    norm = jnp.float32(np.sqrt(np.float32(64 * width_y * WIDTH)))
    back = lax.rem(groups - col, groups)
    weights = turned(inverse_ref[rows_of(col, cols), :], back, cols)
    block = weights[:, :cols].astype(BF16)
    both = jnp.concatenate(split(weights), 0)
    held = (own_ref, three_ref, two_low_ref, two_high_ref, one_ref)
    for y in range(width_y):
        at = lanes_of(y)
        everything = jnp.concatenate([ref[:, at] for ref in held], 0)
        mass = jnp.concatenate([coef_ref[8 * MS : 8 * MS + 8, at]] * (cols // 8), axis=0)
        light = jnp.concatenate([coef_ref[8 * MI : 8 * MI + 8, at]] * (cols // 8), axis=0)
        rest = (field_ref[:, at] * mass - own_ref[:, at].astype(F32)).astype(BF16)
        parts = jnp.dot(both, everything, preferred_element_type=F32)
        result = parts[:cols] + parts[cols:] + jnp.dot(block, rest, preferred_element_type=F32)
        modes_ref[pl.ds(y, cols, stride=width_y), :] = result * light * norm


def local(start_block, node_mass, material_ids, moduli_table, influence):
    cols, _, width_y, width_z = start_block.shape
    lanes = width_y * width_z
    doms, groups = lax.axis_size("dom"), lax.axis_size("col")
    total_cols = cols * groups
    me, col = lax.axis_index("dom"), lax.axis_index("col")
    core = me % 2
    pair = [(i, i ^ 1) for i in range(doms)]
    across = [(i, i + 1 if i % 2 else i - 1) for i in range(1, doms - 1)]
    wide, deep = 4, 8
    place_of = np.arange(doms).reshape(deep, wide, 2)
    plane_groups = [place_of[:, :, c].reshape(-1).tolist() for c in range(2)]
    x_groups = [place_of[z, :, c].tolist() for z in range(deep) for c in range(2)]
    z_groups = [place_of[:, x, c].tolist() for x in range(wide) for c in range(2)]
    chip_of = place_of[..., None] * groups + np.arange(groups)
    chip_groups = [chip_of[z, :, c].reshape(-1).tolist() for z in range(deep) for c in range(2)]

    def exchange(payload):
        near = lax.ppermute(payload, "dom", pair)
        return near, lax.ppermute(payload, "dom", across)

    def col_ring(step):
        return [(i, (i + step) % groups) for i in range(groups)]

    place = jnp.stack([core, col, me]).astype(jnp.int32)
    targets = influence.reshape(influence.shape[0], lanes)

    base, pay, least = pl.pallas_call(
        prepare,
        out_shape=(
            shape(cols + 24, lanes),
            shape(cols + 16, lanes, BF16),
            jax.ShapeDtypeStruct((doms, 1, WIDTH), F32),
        ),
        in_specs=[pl.BlockSpec(memory_space=pltpu.HBM)] * 4,
        out_specs=(VMEM,) * 3,
        scratch_shapes=[
            pltpu.VMEM((cols * width_y, width_z), F32),
            pltpu.VMEM((width_y, width_z), F32),
            pltpu.VMEM((width_y, width_z), jnp.int32),
            pltpu.VMEM((1, moduli_table.shape[0]), F32),
            pltpu.SemaphoreType.DMA((4,)),
        ],
        compiler_params=pltpu.CompilerParams(vmem_limit_bytes=62398000),
    )(
        start_block.reshape(cols * width_y, width_z),
        node_mass.reshape(width_y, width_z),
        material_ids.reshape(width_y, width_z),
        moduli_table.reshape(1, -1),
    )
    near, far = exchange(pay)
    least = lax.all_to_all(least, "dom", 0, 0, tiled=True)
    forces, coef, field, top = pl.pallas_call(
        first_forces,
        out_shape=(shape(cols, lanes), shape(72, lanes), shape(cols, lanes), shape(8, WIDTH)),
        in_specs=[VMEM] * 3 + [SMEM],
        out_specs=(VMEM,) * 4,
        compiler_params=PARAMS,
    )(far, near, base, place)
    current, pay, scale, shift = pl.pallas_call(
        first_step,
        out_shape=(shape(cols, lanes), shape(cols, lanes, BF16), shape(8, lanes), shape(8, WIDTH)),
        in_specs=[VMEM] * 5,
        out_specs=(VMEM,) * 4,
        compiler_params=PARAMS,
    )(least, forces, field, coef, top)
    previous = field
    for step in range(DEGREE - 1):
        last = step == DEGREE - 2
        near, far = exchange(pay)
        partly = pl.pallas_call(
            half_step,
            out_shape=shape(cols, lanes),
            in_specs=[VMEM] * 7,
            out_specs=VMEM,
            compiler_params=PARAMS,
        )(near, current, previous, coef, scale, shift, targets if last else shift)
        outs = pl.pallas_call(
            functools.partial(full_step, last),
            out_shape=(shape(cols, lanes),) + (shape(cols, lanes, BF16),) * (2 if last else 1),
            in_specs=[VMEM] * 4,
            out_specs=(VMEM,) * (3 if last else 2),
            compiler_params=PARAMS,
        )(far, partly, coef, scale)
        previous, current, pay = current, outs[0], outs[1]
    heavy = outs[2]
    near, far = exchange(pay)
    one, three = lax.ppermute(heavy, "col", col_ring(1)), lax.ppermute(heavy, "col", col_ring(3))
    two_low = lax.ppermute(one[: cols // 2], "col", col_ring(1))
    two_high = lax.ppermute(three[cols // 2 :], "col", col_ring(3))
    half = targets.shape[0] // 2
    t_rows, g_rows = half // wide, cols // wide
    chunk = jax.ShapeDtypeStruct((wide, t_rows + g_rows, total_cols), F32)
    keep, send, most = pl.pallas_call(
        early,
        out_shape=(chunk, chunk, shape(total_cols, lanes, BF16)),
        in_specs=[VMEM] * 5 + [SMEM],
        out_specs=(VMEM,) * 3,
        compiler_params=PARAMS,
    )(current, heavy, one, three, targets, place)
    partly = pl.pallas_call(
        half_stiffness,
        out_shape=shape(cols, lanes),
        in_specs=[VMEM] * 3,
        out_specs=VMEM,
        compiler_params=PARAMS,
    )(near, current, coef)
    split_field = (shape(cols, lanes, BF16),) * 2
    keep, send, high, low = pl.pallas_call(
        middle,
        out_shape=(chunk, chunk) + split_field,
        in_specs=[VMEM] * 6 + [SMEM],
        out_specs=(VMEM,) * 4,
        input_output_aliases={0: 0, 1: 1},
        compiler_params=PARAMS,
    )(keep, send, far, partly, coef, most, place)
    keep, send = pl.pallas_call(
        late,
        out_shape=(chunk, chunk),
        in_specs=[VMEM] * 8 + [SMEM],
        out_specs=(VMEM,) * 2,
        input_output_aliases={0: 0, 1: 1},
        compiler_params=PARAMS,
    )(keep, send, two_low, two_high, current, high, low, targets, place)

    summed = keep + lax.ppermute(send, "dom", pair)
    summed = lax.all_to_all(summed, "dom", 0, 0, tiled=True, axis_index_groups=x_groups)
    summed = pl.pallas_call(
        along_z,
        out_shape=jax.ShapeDtypeStruct((deep, 2 * (t_rows // deep + g_rows), WIDTH), F32),
        in_specs=[VMEM],
        out_specs=VMEM,
        compiler_params=PARAMS,
    )(summed)
    summed = lax.all_to_all(summed, "dom", 0, 0, tiled=True, axis_index_groups=z_groups)
    few = t_rows // deep
    target, gram = pl.pallas_call(
        along_chips,
        out_shape=(
            jax.ShapeDtypeStruct((deep * wide, 2 * few, WIDTH), F32),
            jax.ShapeDtypeStruct((wide * groups, g_rows, total_cols), F32),
        ),
        in_specs=[VMEM],
        out_specs=(VMEM,) * 2,
        compiler_params=PARAMS,
    )(summed)
    mine = lax.all_to_all(gram, ("dom", "col"), 0, 0, tiled=True, axis_index_groups=chip_groups)
    theirs = lax.ppermute(mine, "dom", pair)
    target = lax.all_to_all(target, "dom", 0, 0, tiled=True, axis_index_groups=plane_groups)
    inverse, ritz_matrix = pl.pallas_call(
        solve,
        out_shape=(shape(total_cols, total_cols),) * 2,
        in_specs=[VMEM] * 2 + [SMEM],
        out_specs=(VMEM,) * 2,
        scratch_shapes=[pltpu.VMEM((total_cols, total_cols), F32)] * 3,
        compiler_params=PARAMS,
    )(mine, theirs, place)
    part_rows = total_cols // doms
    kept, sent = pl.pallas_call(
        participate,
        out_shape=(shape(part_rows, half),) * 2,
        in_specs=[VMEM] * 2 + [SMEM],
        out_specs=(VMEM,) * 2,
        scratch_shapes=[pltpu.VMEM((half, total_cols), F32)],
        compiler_params=PARAMS,
    )(target, inverse, place)
    got = lax.ppermute(sent, "dom", pair)
    modes = pl.pallas_call(
        combine,
        out_shape=shape(cols * width_y, width_z),
        in_specs=[VMEM] * 8 + [SMEM],
        out_specs=VMEM,
        compiler_params=PARAMS,
    )(current, heavy, three, two_low, two_high, one, coef, inverse, place)
    first = core == 0
    participation = jnp.concatenate([jnp.where(first, kept, got), jnp.where(first, got, kept)], 1)
    return (modes.reshape(start_block.shape), ritz_matrix, participation)


def solution(mesh):
    placed = (
        P("col", "dom", None, None),
        P("dom", None, None),
        P("dom", None, None),
        P(),
        P("col", "dom", None, None),
    )
    return jax.shard_map(
        local,
        mesh=mesh,
        in_specs=placed,
        out_specs=(P("col", "dom", None, None), P(), P("dom", "col")),
        check_vma=False,
    )
```
